32 devices in a mesh: dp: 4 (over z), ctx: 8 (over y, x, core).
Axes of the slice: x: 2, y: 2, z: 4, core: 2. Of those that a mesh axis runs over, the one named last changes fastest.
Arguments:
- tokens: bfloat16 [16, 2048, 1024], P('dp', 'ctx'), may hold values from -6 to 6
- segments: int32 [16, 2048], P('dp', 'ctx'), may hold values from -1 to 31, as said below
- cotangent: bfloat16 [16, 2048, 1024], P('dp', 'ctx'), may hold values from -6 to 6
- w_query: float32 [1024, 1024], P(('dp', 'ctx')), may hold values from -0.1875 to 0.1875
- w_key: float32 [1024, 1024], P(('dp', 'ctx')), may hold values from -0.1875 to 0.1875
- w_value: float32 [1024, 1024], P(('dp', 'ctx')), may hold values from -0.1875 to 0.1875
- w_out: float32 [1024, 1024], P(('dp', 'ctx')), may hold values from -0.75 to 0.75
- w_up: float32 [1024, 4096], P(('dp', 'ctx')), may hold values from -0.1875 to 0.1875
- w_down: float32 [4096, 1024], P(('dp', 'ctx')), may hold values from -0.09375 to 0.09375
- b_query: float32 [1024], P(('dp', 'ctx')), may hold values from -3 to 3
- b_value: float32 [1024], P(('dp', 'ctx')), may hold values from -3 to 3
- b_out: float32 [1024], P(('dp', 'ctx')), may hold values from -3 to 3
- b_up: float32 [4096], P(('dp', 'ctx')), may hold values from -3 to 3
- b_down: float32 [1024], P(('dp', 'ctx')), may hold values from -3 to 3
- gain_attn: float32 [1024], P(('dp', 'ctx')), may hold values from 0.5 to 1.5
- shift_attn: float32 [1024], P(('dp', 'ctx')), may hold values from -3 to 3
- gain_mlp: float32 [1024], P(('dp', 'ctx')), may hold values from 0.5 to 1.5
- shift_mlp: float32 [1024], P(('dp', 'ctx')), may hold values from -3 to 3
Outputs:
- output: bfloat16 [16, 2048, 1024], P('dp', 'ctx')
- grad_tokens: bfloat16 [16, 2048, 1024], P('dp', 'ctx')
- grad_w_query: float32 [1024, 1024], P(('dp', 'ctx'))
- grad_w_key: float32 [1024, 1024], P(('dp', 'ctx'))
- grad_w_value: float32 [1024, 1024], P(('dp', 'ctx'))
- grad_w_out: float32 [1024, 1024], P(('dp', 'ctx'))
- grad_w_up: float32 [1024, 4096], P(('dp', 'ctx'))
- grad_w_down: float32 [4096, 1024], P(('dp', 'ctx'))
- grad_b_query: float32 [1024], P(('dp', 'ctx'))
- grad_b_value: float32 [1024], P(('dp', 'ctx'))
- grad_b_out: float32 [1024], P(('dp', 'ctx'))
- grad_b_up: float32 [4096], P(('dp', 'ctx'))
- grad_b_down: float32 [1024], P(('dp', 'ctx'))
- grad_gain_attn: float32 [1024], P(('dp', 'ctx'))
- grad_shift_attn: float32 [1024], P(('dp', 'ctx'))
- grad_gain_mlp: float32 [1024], P(('dp', 'ctx'))
- grad_shift_mlp: float32 [1024], P(('dp', 'ctx'))
The draws below stay inside these ranges and needn't reach their ends.
Inputs may be any that keep to these rules, and one draw needn't show every extreme that they name: `segments`: within a sequence, document numbers start at 0 and never fall; pad slots, numbered -1, form a tail of at most 512 slots. Among the 4 sequences of each index of dp, one is a single document without pad slots. Number 31 and pad slots both occur in every draw.
All inputs are finite; a program needn't handle non-finite values.
Results may differ from the reference program's by a relative error of at most 0.019.
Values may be sent and summed in bfloat16 or wider, within the bound.
No kernel may reach another device: no remote copies, remote signals or barrier semaphores. Data moves between devices by JAX's collectives and lax.ppermute only.
A program may use at most 256 MiB of HBM per device.

```python
import jax
import jax.numpy as jnp
from jax import lax

D = 1024
H = 16
HD = 64
FF = 4096
SEQ_LEN = 2048
NSEQ = 4
SEQS = 16


def draw_segments(key, part):
    key = jax.random.fold_in(key, 7)
    key_count, key_cuts, key_pads, key_whole = jax.random.split(key, 4)
    chosen = jax.random.randint(key_whole, (SEQS // NSEQ,), 0, NSEQ)
    seq_index = jnp.arange(SEQS)
    group_index = seq_index // NSEQ
    place_index = seq_index % NSEQ
    after_chosen = place_index == (jnp.repeat(chosen, NSEQ) + 1) % NSEQ
    most_docs = after_chosen & (group_index == 0)
    most_pads = after_chosen & (group_index == SEQS // NSEQ - 1)
    cut_count = jnp.left_shift(1, jax.random.randint(key_count, (SEQS,), 0, 6)) - 1
    cut_count = jnp.where(most_docs, 31, cut_count)
    cut_places = jax.random.randint(key_cuts, (SEQS, 32), 1, SEQ_LEN)
    cut_places = jnp.where(jnp.arange(32)[None, :] < cut_count[:, None], cut_places, SEQ_LEN)
    places = jnp.arange(SEQ_LEN)
    seg_ids = jnp.sum((cut_places[:, None, :] <= places[None, :, None]).astype(jnp.int32), axis=-1)
    pad_rows = jax.random.randint(key_pads, (SEQS,), 0, SEQ_LEN // 4 + 1)
    pad_rows = jnp.where(most_docs, 0, pad_rows)
    pad_rows = jnp.where(most_pads, SEQ_LEN // 4, pad_rows)
    seg_ids = jnp.where(places[None, :] >= SEQ_LEN - pad_rows[:, None], -1, seg_ids)
    single_doc = place_index == jnp.repeat(chosen, NSEQ)
    return jnp.where(single_doc[:, None], 0, seg_ids).astype(jnp.int32)


def with_spikes(entries, stream_key, source, target, blocks, factor):
    def block_of(dim):
        return (jnp.arange(entries.shape[dim]) // (entries.shape[dim] // blocks)).reshape((-1,) + (1,) * (entries.ndim - 1 - dim))

    first = jax.random.permutation(stream_key, blocks)[block_of(target)]
    second = (block_of(target) + blocks // 2) % blocks
    return jnp.where((block_of(source) == first) | (block_of(source) == second), factor * entries, entries)


def shard_levels(own_key, extent, cuts, low, top_value):
    def one(axis_at, blocks):
        draws = jax.random.uniform(jax.random.fold_in(jax.random.fold_in(own_key, 6), axis_at), (blocks,), jnp.float32, low / len(cuts), top_value / len(cuts))
        return jnp.repeat(jnp.exp(draws), extent[axis_at] // blocks).reshape((-1,) + (1,) * (len(extent) - axis_at - 1))

    level = one(*cuts[0])
    for cut in cuts[1:]:
        level = level * one(*cut)
    return level


def normal_values(key, extent, width, most, shards=(), held_as=jnp.bfloat16):
    loudness = shard_levels(key, extent, shards, -0.22, 0.18) if shards else 1.0
    values = jax.random.normal(key, extent, jnp.float32) * width * loudness
    return jnp.minimum(jnp.maximum(values, -most), most).astype(held_as)


def noise_with(key, shape, scale, most, cuts, heavy, held_as=jnp.bfloat16):
    array = scale * jax.random.normal(key, shape, jnp.float32)
    if cuts:
        array = array * shard_levels(key, shape, cuts, -0.22, 0.18)
    return jnp.clip(with_spikes(array, jax.random.fold_in(key, 3), *heavy), -most, most).astype(held_as)


def setup_inputs(seed: int = 0) -> dict:
    arg_keys = jax.random.split(jax.random.key(seed), 19)
    return {
        "tokens": normal_values(arg_keys[0], (SEQS, SEQ_LEN, D), 1.0, 6.0, ((0, 4), (1, 8))),
        "segments": draw_segments(jax.random.fold_in(arg_keys[18], 71), 0),
        "cotangent": noise_with(arg_keys[2], (SEQS, SEQ_LEN, D), 1.0, 6.0, ((0, 4), (1, 8)), (0, 2, 4, 2.0)),
        "w_query": normal_values(arg_keys[3], (D, D), D ** -0.5, 0.1875, ((0, 32),), jnp.float32),
        "w_key": normal_values(arg_keys[4], (D, D), D ** -0.5, 0.1875, ((0, 32),), jnp.float32),
        "w_value": normal_values(arg_keys[5], (D, D), D ** -0.5, 0.1875, ((0, 32),), jnp.float32),
        "w_out": normal_values(arg_keys[6], (D, D), (D // 16) ** -0.5, 0.75, ((0, 32),), jnp.float32),
        "w_up": normal_values(arg_keys[7], (D, FF), D ** -0.5, 0.1875, ((0, 32),), jnp.float32),
        "w_down": normal_values(arg_keys[8], (FF, D), FF ** -0.5, 0.09375, ((0, 32),), jnp.float32),
        "b_query": normal_values(arg_keys[9], (D,), 0.5, 3.0, ((0, 32),), jnp.float32),
        "b_value": normal_values(arg_keys[10], (D,), 0.5, 3.0, ((0, 32),), jnp.float32),
        "b_out": normal_values(arg_keys[11], (D,), 0.5, 3.0, ((0, 32),), jnp.float32),
        "b_up": normal_values(arg_keys[12], (FF,), 0.5, 3.0, ((0, 32),), jnp.float32),
        "b_down": normal_values(arg_keys[13], (D,), 0.5, 3.0, ((0, 32),), jnp.float32),
        "gain_attn": jnp.clip(1.0 + 0.1 * jax.random.normal(arg_keys[14], (D,), jnp.float32), 0.5, 1.5),
        "shift_attn": normal_values(arg_keys[15], (D,), 0.5, 3.0, ((0, 32),), jnp.float32),
        "gain_mlp": jnp.clip(1.0 + 0.1 * jax.random.normal(arg_keys[16], (D,), jnp.float32), 0.5, 1.5),
        "shift_mlp": normal_values(arg_keys[17], (D,), 0.5, 3.0, ((0, 32),), jnp.float32),
    }


HIGHEST = lax.Precision.HIGHEST
MASKED = -1e+30
EPSILON = 1e-05
QSCALE = 0.125

@jax.custom_vjp
def low(v):
    return lax.optimization_barrier(v.astype(jnp.bfloat16)).astype(jnp.float32)

@jax.custom_vjp
def low_back(v):
    return v

def low_keep(v):
    return (low(v), None)

def low_pass(kept, grad):
    return (grad,)

def back_keep(v):
    return (v, None)

def back_low(kept, grad):
    return (low(grad),)
low.defvjp(low_keep, low_pass)
low_back.defvjp(back_keep, back_low)

def both_round(value):
    return low(low_back(value))

def layer_norm(hidden, gain, shift):
    centred = hidden - lax.optimization_barrier(jnp.mean(hidden, axis=-1, keepdims=True))
    variance = lax.optimization_barrier(jnp.mean(centred * centred, axis=-1, keepdims=True))
    return centred * lax.rsqrt(variance + EPSILON) * gain + shift

def project(inputs, weight):
    return jnp.dot(inputs, weight, precision=HIGHEST)

def sequence_layer(params, inputs, seg_ids):
    w_query, w_key, w_value, w_out, w_up, w_down, b_query, b_value, b_out, b_up, b_down, gain_attn, shift_attn, gain_mlp, shift_mlp = [low(master) for master in params]
    length = inputs.shape[0]
    queries = both_round((project(inputs, w_query) + b_query) * QSCALE).reshape(length, H, HD)
    key_rows = both_round(project(inputs, w_key)).reshape(length, H, HD)
    values = both_round(project(inputs, w_value) + b_value).reshape(length, H, HD)
    scores = jnp.einsum('qhd,khd->hqk', queries, key_rows, precision=HIGHEST)
    allowed = seg_ids[:, None] == seg_ids[None, :]
    scores = low_back(jnp.where(allowed[None], scores, MASKED))
    soft_probs = low(jax.nn.softmax(scores, axis=-1))
    mixed_heads = both_round(jnp.einsum('hqk,khd->qhd', soft_probs, values, precision=HIGHEST).reshape(length, H * HD))
    branch_one = low_back(project(mixed_heads, w_out) + b_out)
    normed = layer_norm(inputs + branch_one, gain_attn, shift_attn)
    pre_act = low_back(project(low(normed), w_up) + b_up)
    activated = low(jax.nn.gelu(pre_act, approximate=False))
    branch_two = low_back(project(activated, w_down) + b_down)
    return layer_norm(normed + branch_two, gain_mlp, shift_mlp)

def reference(tokens, segments, cotangent, w_query, w_key, w_value, w_out, w_up, w_down, b_query, b_value, b_out, b_up, b_down, gain_attn, shift_attn, gain_mlp, shift_mlp):
    params = (w_query, w_key, w_value, w_out, w_up, w_down, b_query, b_value, b_out, b_up, b_down, gain_attn, shift_attn, gain_mlp, shift_mlp)
    inputs = tokens.astype(jnp.float32)
    grad_out = cotangent.astype(jnp.float32)

    def whole(params_in, inputs_in):

        def scan_step(carried, seq_item):
            return (carried, jax.checkpoint(sequence_layer)(params_in, seq_item[0], seq_item[1]))
        unused, outputs = lax.scan(scan_step, jnp.zeros((), jnp.float32), (inputs_in, segments))
        return outputs
    outputs, pullback = jax.vjp(whole, params, inputs)
    grad_params, grad_inputs = pullback(grad_out)
    return (outputs.astype(jnp.bfloat16), grad_inputs.astype(jnp.bfloat16), grad_params[0], grad_params[1], grad_params[2], grad_params[3], grad_params[4], grad_params[5], grad_params[6], grad_params[7], grad_params[8], grad_params[9], grad_params[10], grad_params[11], grad_params[12], grad_params[13], grad_params[14])
```

```python
import functools

import jax
import jax.numpy as jnp
from jax import lax
from jax.experimental import pallas as pl
from jax.experimental.pallas import tpu as pltpu
from jax.sharding import PartitionSpec as P

HD = 64
MASKED = -1e30
EPSILON = 1e-05
QSCALE = 0.125
BF = jnp.bfloat16
F32 = jnp.float32
NT = (((1,), (1,)), ((), ()))
NN = (((1,), (0,)), ((), ()))
TN = (((0,), (0,)), ((), ()))
VMEM_LIMIT = 56 << 20
BOTH = ("dp", "ctx")


def mm(a, b, dims=NN):
    return lax.dot_general(a, b, dims, preferred_element_type=F32)


def params():
    return pltpu.CompilerParams(vmem_limit_bytes=VMEM_LIMIT)


def head_parts(block):
    lane = lax.broadcasted_iota(jnp.int32, block.shape, 1)
    zero = jnp.zeros_like(block)
    return [jnp.where(lane < HD, block, zero), jnp.where(lane < HD, zero, block)]


def attend_kernel(chunk, q_ref, k_ref, v_ref, sq_ref, sk_ref, o_ref, p_ref, l_ref, vt_ref, kn_ref):
    i = pl.program_id(1)
    total = k_ref.shape[0]
    block = q_ref.shape[0]

    @pl.when(i == 0)
    def _():
        vt_ref[...] = v_ref[...].T
        keys = k_ref[...].astype(F32)
        norms = jnp.sum((keys * keys).T.reshape(2, HD, total), axis=1)
        kn_ref[...] = jnp.sqrt(jnp.max(norms, axis=1, keepdims=True))

    q = q_ref[...]
    parts = head_parts(q)
    q32 = q.astype(F32)
    qn = jnp.sqrt(jnp.sum((q32 * q32).T.reshape(2, HD, block), axis=1))
    bound = qn * kn_ref[...]
    seg_q = sq_ref[...]
    ones = jnp.ones((16, chunk), BF)

    def scores(h, lo):
        s = mm(k_ref[lo : lo + chunk, :], parts[h], NT)
        return jnp.where(sk_ref[lo : lo + chunk, :] == seg_q, s, MASKED)

    def finish(shift):
        acc = [jnp.zeros((HD + 16, block), F32)] * 2
        for lo in range(0, total, chunk):
            for h in range(2):
                p = jnp.exp(scores(h, lo) - shift[h : h + 1]).astype(BF)
                p_ref[h, lo : lo + chunk, :] = p
                left = jnp.concatenate([vt_ref[h * HD : h * HD + HD, lo : lo + chunk], ones], axis=0)
                acc[h] = acc[h] + mm(left, p)
        sums = [acc[h][HD : HD + 1] for h in range(2)]
        out = jnp.concatenate([acc[h][:HD] / sums[h] for h in range(2)], axis=0)
        o_ref[...] = out.T.astype(BF)
        sums = jnp.concatenate(sums, axis=0)
        l_ref[...] = 1.0 / sums
        return sums

    sums = finish(bound)
    good = jnp.min(sums) > 1e-20

    @pl.when(jnp.logical_not(good))
    def _():
        most = [jnp.full((1, block), MASKED, F32)] * 2
        for lo in range(0, total, chunk):
            for h in range(2):
                most[h] = jnp.maximum(most[h], jnp.max(scores(h, lo), axis=0, keepdims=True))
        finish(jnp.concatenate(most, axis=0))


def attend(qkv, seg_row, seg_col, block=256, chunk=512):
    total = qkv.shape[1]
    pairs = qkv.shape[2] // 128
    specs = lambda c: pl.BlockSpec((None, total, 128), lambda h, i: (c, 0, h))
    return pl.pallas_call(
        functools.partial(attend_kernel, chunk),
        grid=(pairs, total // block),
        in_specs=[
            pl.BlockSpec((None, block, 128), lambda h, i: (0, i, h)),
            specs(1),
            specs(2),
            pl.BlockSpec((1, block), lambda h, i: (0, i)),
            pl.BlockSpec((total, 1), lambda h, i: (0, 0)),
        ],
        out_specs=[
            pl.BlockSpec((block, 128), lambda h, i: (i, h)),
            pl.BlockSpec((None, 2, total, block), lambda h, i: (h, 0, 0, i)),
            pl.BlockSpec((None, 2, block), lambda h, i: (h, 0, i)),
        ],
        out_shape=[
            jax.ShapeDtypeStruct((total, pairs * 128), BF),
            jax.ShapeDtypeStruct((pairs, 2, total, total), BF),
            jax.ShapeDtypeStruct((pairs, 2, total), F32),
        ],
        scratch_shapes=[pltpu.VMEM((128, total), BF), pltpu.VMEM((2, 1), F32)],
        compiler_params=params(),
        cost_estimate=pl.CostEstimate(flops=45 * 10**9, bytes_accessed=80 << 20, transcendentals=0),
        name="attend",
    )(qkv, qkv, qkv, seg_row, seg_col)


def attend_back_kernel(
    chunk, q_ref, k_ref, v_ref, o_ref, do_ref, p_ref, l_ref, dq_ref, dk_ref, dv_ref, kt_ref, dk_acc, dv_acc
):
    i = pl.program_id(1)
    total = k_ref.shape[0]
    block = q_ref.shape[0]

    @pl.when(i == 0)
    def _():
        kt_ref[...] = k_ref[...].T
        dk_acc[...] = jnp.zeros_like(dk_acc)
        dv_acc[...] = jnp.zeros_like(dv_acc)

    do = do_ref[...]
    q_parts = head_parts(q_ref[...])
    do_parts = head_parts(do)
    product = do.astype(F32) * o_ref[...].astype(F32)
    delta = jnp.sum(product.T.reshape(2, HD, block), axis=1)
    inverse = l_ref[...]
    grad_q = [jnp.zeros((HD, block), F32)] * 2
    for lo in range(0, total, chunk):
        rows = slice(lo, lo + chunk)
        values = v_ref[rows, :]
        for h in range(2):
            p = p_ref[h, rows, :].astype(F32) * inverse[h : h + 1]
            grad_p = mm(values, do_parts[h], NT)
            grad_s = (p * (grad_p - delta[h : h + 1])).astype(BF)
            dv_acc[rows, :] += mm(p.astype(BF), do_parts[h])
            dk_acc[rows, :] += mm(grad_s, q_parts[h])
            grad_q[h] = grad_q[h] + mm(kt_ref[h * HD : h * HD + HD, rows], grad_s)
    dq_ref[...] = jnp.concatenate(grad_q, axis=0).T.astype(BF)

    @pl.when(i == pl.num_programs(1) - 1)
    def _():
        dk_ref[...] = dk_acc[...].astype(BF)
        dv_ref[...] = dv_acc[...].astype(BF)


def attend_back(qkv, out, grad_out, probs, inverse, block=256, chunk=512):
    total = qkv.shape[1]
    pairs = qkv.shape[2] // 128
    whole = lambda c: pl.BlockSpec((None, total, 128), lambda h, i: (c, 0, h))
    rows = pl.BlockSpec((block, 128), lambda h, i: (i, h))
    keys = pl.BlockSpec((total, 128), lambda h, i: (0, h))
    return pl.pallas_call(
        functools.partial(attend_back_kernel, chunk),
        grid=(pairs, total // block),
        in_specs=[
            pl.BlockSpec((None, block, 128), lambda h, i: (0, i, h)),
            whole(1),
            whole(2),
            rows,
            rows,
            pl.BlockSpec((None, 2, total, block), lambda h, i: (h, 0, 0, i)),
            pl.BlockSpec((None, 2, block), lambda h, i: (h, 0, i)),
        ],
        out_specs=[rows, keys, keys],
        out_shape=[jax.ShapeDtypeStruct((total, pairs * 128), BF)] * 3,
        scratch_shapes=[
            pltpu.VMEM((128, total), BF),
            pltpu.VMEM((total, 128), F32),
            pltpu.VMEM((total, 128), F32),
        ],
        compiler_params=params(),
        cost_estimate=pl.CostEstimate(flops=85 * 10**9, bytes_accessed=80 << 20, transcendentals=0),
        name="attend_back",
    )(qkv, qkv, qkv, out, grad_out, probs, inverse)


def gelu_parts(u):
    scaled = jnp.abs(u) * 0.7071067811865476
    den = 1.0 + 0.3275911 * scaled
    t = pl.reciprocal(den, approx=True)
    t = t * (2.0 - den * t)
    e = jnp.exp(u * u * -0.5)
    poly = t * (
        0.127414796
        + t * (-0.142248368 + t * (0.7107068705 + t * (-0.7265760135 + t * 0.5307027145)))
    )
    tail = poly * e
    phi = jnp.where(u >= 0, 1.0 - tail, tail)
    return u * phi, phi + u * (e * 0.3989422804014327)


def mean(value):
    return jnp.mean(value, axis=-1, keepdims=True)


def normed(hidden):
    centred = hidden - mean(hidden)
    inverse = lax.rsqrt(mean(centred * centred) + EPSILON)
    return centred * inverse, inverse


def norm_back(grad_in, scaled, inverse, gain):
    grad_scaled = grad_in * gain
    return inverse * (grad_scaled - mean(grad_scaled) - scaled * mean(grad_scaled * scaled))


def fold(value):
    return jnp.sum(value.reshape(value.shape[0] // 8, 8, value.shape[1]), axis=0)


def add_fold(ref, first, value):
    part = fold(value)

    @pl.when(first)
    def _():
        ref[...] = part

    @pl.when(jnp.logical_not(first))
    def _():
        ref[...] += part


def mid_up_kernel(step, x_ref, o_ref, wo_ref, wu_ref, vec_ref, bu_ref, xh_ref, r_ref, xb_ref, g_ref, gp_ref):
    hidden = x_ref[...].astype(F32) + mm(o_ref[...], wo_ref[...]) + vec_ref[0:1, :]
    scaled, inverse = normed(hidden)
    xh_ref[...] = scaled
    r_ref[...] = inverse
    xb = (scaled * vec_ref[1:2, :] + vec_ref[2:3, :]).astype(BF)
    xb_ref[...] = xb
    for lo in range(0, wu_ref.shape[1], step):
        cols = slice(lo, lo + step)
        g, gp = gelu_parts(mm(xb, wu_ref[:, cols]) + bu_ref[:, cols])
        g_ref[:, cols] = g.astype(BF)
        gp_ref[:, cols] = gp.astype(BF)


def mid_up(x, o, w_out, w_up, vecs, b_up, block=256, step=512):
    rows, d = x.shape
    ff = w_up.shape[1]
    row = lambda n: pl.BlockSpec((block, n), lambda i: (i, 0))
    full = lambda a: pl.BlockSpec(a.shape, lambda i: (0, 0), pipeline_mode=pl.Buffered(1))
    return pl.pallas_call(
        functools.partial(mid_up_kernel, step),
        grid=(rows // block,),
        in_specs=[row(d), row(d), full(w_out), full(w_up), full(vecs), full(b_up)],
        out_specs=[row(d), row(1), row(d), row(ff), row(ff)],
        out_shape=[
            jax.ShapeDtypeStruct((rows, d), F32),
            jax.ShapeDtypeStruct((rows, 1), F32),
            jax.ShapeDtypeStruct((rows, d), BF),
            jax.ShapeDtypeStruct((rows, ff), BF),
            jax.ShapeDtypeStruct((rows, ff), BF),
        ],
        compiler_params=params(),
        cost_estimate=pl.CostEstimate(flops=11 * 10**9, bytes_accessed=36 << 20, transcendentals=0),
        name="mid_up",
    )(x, o, w_out, w_up, vecs, b_up)


def mid_down_kernel(
    step, g_ref, gp_ref, xh_ref, dy_ref, wd_ref, vec_ref, out_ref, dh_ref, dm_ref, du_ref, s_ref, su_ref
):
    first = pl.program_id(0) == 0
    x1 = xh_ref[...] * vec_ref[1:2, :] + vec_ref[2:3, :]
    hidden = x1 + mm(g_ref[...], wd_ref[...]) + vec_ref[3:4, :]
    scaled, inverse = normed(hidden)
    gain = vec_ref[4:5, :]
    out_ref[...] = (scaled * gain + vec_ref[5:6, :]).astype(BF)
    dy = dy_ref[...].astype(F32)
    dh = norm_back(dy, scaled, inverse, gain)
    dm = dh.astype(BF)
    dh_ref[...] = dh
    dm_ref[...] = dm
    add_fold(s_ref.at[0:8, :], first, dy * scaled)
    add_fold(s_ref.at[8:16, :], first, dy)
    add_fold(s_ref.at[16:24, :], first, dm.astype(F32))
    for lo in range(0, wd_ref.shape[0], step):
        cols = slice(lo, lo + step)
        du = (mm(dm, wd_ref[cols, :], NT) * gp_ref[:, cols].astype(F32)).astype(BF)
        du_ref[:, cols] = du
        add_fold(su_ref.at[:, cols], first, du.astype(F32))


def mid_down(g, gp, xh, dy, w_down, vecs, block=256, step=512):
    rows, d = xh.shape
    ff = g.shape[1]
    row = lambda n: pl.BlockSpec((block, n), lambda i: (i, 0))
    full = lambda a: pl.BlockSpec(a.shape, lambda i: (0, 0), pipeline_mode=pl.Buffered(1))
    keep = lambda r, n: pl.BlockSpec((r, n), lambda i: (0, 0))
    return pl.pallas_call(
        functools.partial(mid_down_kernel, step),
        grid=(rows // block,),
        in_specs=[row(ff), row(ff), row(d), row(d), full(w_down), full(vecs)],
        out_specs=[row(d), row(d), row(d), row(ff), keep(24, d), keep(8, ff)],
        out_shape=[
            jax.ShapeDtypeStruct((rows, d), BF),
            jax.ShapeDtypeStruct((rows, d), F32),
            jax.ShapeDtypeStruct((rows, d), BF),
            jax.ShapeDtypeStruct((rows, ff), BF),
            jax.ShapeDtypeStruct((24, d), F32),
            jax.ShapeDtypeStruct((8, ff), F32),
        ],
        compiler_params=params(),
        cost_estimate=pl.CostEstimate(flops=17 * 10**9, bytes_accessed=44 << 20, transcendentals=0),
        name="mid_down",
    )(g, gp, xh, dy, w_down, vecs)


def mid_back_kernel(dh_ref, du_ref, xh_ref, r_ref, wu_ref, wo_ref, vec_ref, dh1_ref, da_ref, do_ref, s_ref):
    first = pl.program_id(0) == 0
    dx = dh_ref[...] + mm(du_ref[...], wu_ref[...], NT)
    scaled = xh_ref[...]
    dh1 = norm_back(dx, scaled, r_ref[...], vec_ref[1:2, :])
    dh1_ref[...] = dh1
    da = dh1.astype(BF)
    da_ref[...] = da
    do_ref[...] = mm(da, wo_ref[...], NT).astype(BF)
    add_fold(s_ref.at[0:8, :], first, dx * scaled)
    add_fold(s_ref.at[8:16, :], first, dx)
    add_fold(s_ref.at[16:24, :], first, da.astype(F32))


def mid_back(dh, du, xh, r, w_up, w_out, vecs, block=256):
    rows, d = dh.shape
    row = lambda n: pl.BlockSpec((block, n), lambda i: (i, 0))
    full = lambda a: pl.BlockSpec(a.shape, lambda i: (0, 0), pipeline_mode=pl.Buffered(1))
    return pl.pallas_call(
        mid_back_kernel,
        grid=(rows // block,),
        in_specs=[row(d), row(du.shape[1]), row(d), row(1), full(w_up), full(w_out), full(vecs)],
        out_specs=[row(d), row(d), row(d), pl.BlockSpec((24, d), lambda i: (0, 0))],
        out_shape=[
            jax.ShapeDtypeStruct((rows, d), F32),
            jax.ShapeDtypeStruct((rows, d), BF),
            jax.ShapeDtypeStruct((rows, d), BF),
            jax.ShapeDtypeStruct((24, d), F32),
        ],
        compiler_params=params(),
        cost_estimate=pl.CostEstimate(flops=11 * 10**9, bytes_accessed=36 << 20, transcendentals=0),
        name="mid_back",
    )(dh, du, xh, r, w_up, w_out, vecs)


def swap(value, mask):
    count = lax.axis_size("ctx")
    return lax.ppermute(value, "ctx", [(d, d ^ mask) for d in range(count)])


def pick(value, index, axis=0):
    return lax.dynamic_index_in_dim(value, index, axis, keepdims=False)


def to_chip(value, chip, chips):
    return [pick(value, chip)] + [swap(pick(value, chip ^ r), 2 * r) for r in range(1, chips)]


def from_chip(pieces, chip):
    chips = len(pieces)
    back = jnp.stack([pieces[0]] + [swap(pieces[r], 2 * r) for r in range(1, chips)])
    return jnp.take(back, jnp.arange(chips) ^ chip, axis=0)


def halve(value, axis, bit, chip, last):
    own = (chip >> bit) & 1
    sent = swap(pick(value, 1 - own, axis), 2 << bit)
    total = pick(value, own, axis).astype(F32) + sent.astype(F32)
    return total.astype(BF)


def reduce_rows(grad, chip, core):
    groups, chips, _, rows, cols = grad.shape
    bits = chips.bit_length() - 1
    me = lax.axis_index("dp")
    shaped = grad.reshape((groups,) + (2,) * bits + (2, rows, cols))
    parts = []
    for part, order in ((shaped[: groups // 2], range(bits)), (shaped[groups // 2 :], range(bits - 1, -1, -1))):
        left = list(range(bits - 1, -1, -1))
        for bit in order:
            part = halve(part, 1 + left.index(bit), bit, chip, False)
            left.remove(bit)
        parts.append(part)
    both = jnp.concatenate(parts, axis=0)
    total = pick(both, me).astype(F32)
    for step in range(1, groups):
        pairs = [(s, (s + step) % groups) for s in range(groups)]
        total = total + lax.ppermute(pick(both, (me + step) % groups), "dp", pairs).astype(F32)
    total = total.astype(BF)
    mine, other = pick(total, core), swap(pick(total, 1 - core), 1)
    ordered = jnp.where(core == 0, jnp.stack([mine, other]), jnp.stack([other, mine]))
    return jnp.moveaxis(ordered, 0, 1).reshape(rows, 2 * cols).astype(F32)


def half_cols(value, which):
    width = value.shape[-1] // 2
    return lax.dynamic_slice_in_dim(value, which * width, width, value.ndim - 1)


def gather(value):
    return lax.all_gather(value, BOTH, axis=0, tiled=True)


def local(
    tokens, segments, cotangent, w_query, w_key, w_value, w_out, w_up, w_down,
    b_query, b_value, b_out, b_up, b_down, gain_attn, shift_attn, gain_mlp, shift_mlp,
):
    seqs, span, d = tokens.shape
    count = lax.axis_size("ctx")
    groups = lax.axis_size("dp")
    chips = count // 2
    me = lax.axis_index("ctx")
    chip, core = me // 2, me % 2
    ff = w_up.shape[1]
    half = d // 2
    shards = groups * count

    vec_names = (b_query, b_value, b_out, gain_attn, shift_attn, b_down, gain_mlp, shift_mlp)
    vec_pack = jnp.concatenate([v.astype(BF) for v in vec_names] + [b_up.astype(BF)]).reshape(1, -1)
    vec_all = gather(vec_pack).astype(F32)
    width = d // shards
    vec = [vec_all[:, n * width : (n + 1) * width].reshape(1, d) for n in range(8)]
    bias_query, bias_value = vec[0], vec[1]
    bias_up = vec_all[:, 8 * width :].reshape(1, ff)
    vecs = jnp.concatenate(vec[2:] + [jnp.zeros((2, d), F32)], axis=0)

    full_query, full_key, full_value = [gather(w.astype(BF)) for w in (w_query, w_key, w_value)]
    full_out, full_up, full_down = [gather(w.astype(BF)) for w in (w_out, w_up, w_down)]

    mine = jnp.concatenate(to_chip(tokens, chip, chips), axis=0)
    seg_mine = jnp.concatenate(to_chip(segments, chip, chips), axis=0)
    dy = jnp.concatenate(to_chip(cotangent, chip, chips), axis=0)
    mate = swap(mine, 1)
    seg = jnp.concatenate([seg_mine, swap(seg_mine, 1)])
    own = mine.shape[0]
    x_all = jnp.concatenate([mine, mate], axis=0)

    w_cat = jnp.stack(
        [half_cols(full_query, core) * jnp.asarray(QSCALE, BF), half_cols(full_key, core), half_cols(full_value, core)]
    )
    bias_cat = jnp.stack(
        [half_cols(bias_query, core) * QSCALE, jnp.zeros((1, half), F32), half_cols(bias_value, core)]
    )
    qkv = (jnp.einsum("td,cdn->ctn", x_all, w_cat, preferred_element_type=F32) + bias_cat).astype(BF)
    attn, probs, inverse = attend(qkv, seg.reshape(1, -1), seg.reshape(-1, 1))

    other_heads = swap(attn[own:], 1)
    heads = [attn[:own], other_heads]
    o_full = jnp.where(core == 0, jnp.concatenate(heads, axis=1), jnp.concatenate(heads[::-1], axis=1))
    xh, r, xb, g, gp = mid_up(mine, o_full, full_out, full_up, vecs, bias_up)
    out, dh2, dm, du, sums_two, sums_up = mid_down(g, gp, xh, dy, full_down, vecs)
    dh1, da, do, sums_one = mid_back(dh2, du, xh, r, full_up, full_out, vecs)
    result_out = from_chip(list(out.reshape(chips, span, d)), chip)

    do_other = swap(half_cols(do, 1 - core), 1)
    do_all = jnp.concatenate([half_cols(do, core), do_other], axis=0)

    def weight_grad(left, right, rows):
        sent = swap(mm(left, half_cols(right, 1 - core), TN).astype(BF), 1)
        whole = (mm(left, half_cols(right, core), TN) + sent.astype(F32)).astype(BF)
        return reduce_rows(whole.reshape(groups, chips, 2, rows, -1), chip, core)

    grad_down = weight_grad(g, dm, ff // shards)
    grad_up = weight_grad(xb, du, d // shards)
    grad_out = weight_grad(o_full, da, d // shards)

    grads = attend_back(qkv, attn, do_all, probs, inverse)
    grad_proj = [mm(x_all, part, TN) for part in grads]
    grad_proj[0] = grad_proj[0] * QSCALE
    rows = d // shards
    grad_query, grad_key, grad_value = [
        reduce_rows(part.astype(BF).reshape(groups, chips, 2, rows, half), chip, core) for part in grad_proj
    ]
    token_part = sum(mm(part, w_cat[n], NT) for n, part in enumerate(grads))
    grad_mine = dh1 + token_part[:own] + swap(token_part[own:].astype(BF), 1).astype(F32)
    grad_tokens = from_chip(list(grad_mine.astype(BF).reshape(chips, span, d)), chip)

    bias_q = jnp.sum(grads[0].astype(F32), axis=0) * QSCALE
    bias_v = jnp.sum(grads[2].astype(F32), axis=0)
    zero = jnp.zeros((half,), F32)

    def place(part):
        return jnp.where(core == 0, jnp.concatenate([part, zero]), jnp.concatenate([zero, part]))

    fold_rows = lambda sums: jnp.sum(sums.reshape(-1, 8, sums.shape[1]), axis=1)
    two, one = fold_rows(sums_two), fold_rows(sums_one)
    small = [place(bias_q), place(bias_v), one[2], one[0], one[1], two[2], two[0], two[1]]
    small = jnp.concatenate([v.reshape(shards, -1) for v in small] + [fold_rows(sums_up).reshape(shards, -1)], axis=1)
    small = lax.psum_scatter(small, BOTH, scatter_dimension=0, tiled=True).reshape(-1)
    parts = [small[n * width : (n + 1) * width] for n in range(8)]
    g_bq, g_bv, g_bo, g_ga, g_sa, g_bd, g_gm, g_sm = parts
    g_bu = small[8 * width :]
    return (
        result_out, grad_tokens, grad_query, grad_key, grad_value, grad_out, grad_up, grad_down,
        g_bq, g_bv, g_bo, g_bu, g_bd, g_ga, g_sa, g_gm, g_sm,
    )


def solution(mesh):
    act, flat, mat, vec = P("dp", "ctx", None), P("dp", "ctx"), P(BOTH, None), P(BOTH)
    return jax.shard_map(
        local,
        mesh=mesh,
        in_specs=(act, flat, act) + (mat,) * 6 + (vec,) * 9,
        out_specs=(act, act) + (mat,) * 6 + (vec,) * 9,
        check_vma=False,
    )
```

```python
import functools

import jax
import jax.numpy as jnp
from jax import lax
from jax.experimental import pallas as pl
from jax.experimental.pallas import tpu as pltpu
from jax.sharding import PartitionSpec as P

HD = 64
MASKED = -1e30
EPSILON = 1e-05
QSCALE = 0.125
BF = jnp.bfloat16
F32 = jnp.float32
NT = (((1,), (1,)), ((), ()))
NN = (((1,), (0,)), ((), ()))
TN = (((0,), (0,)), ((), ()))
VMEM_LIMIT = 56 << 20
BOTH = ("dp", "ctx")
ANY = pl.BlockSpec(memory_space=pl.ANY)
SMEM = pl.BlockSpec(memory_space=pltpu.SMEM)
TILE = 16


def mm(a, b, dims=NN):
    return lax.dot_general(a, b, dims, preferred_element_type=F32)


def params():
    return pltpu.CompilerParams(vmem_limit_bytes=VMEM_LIMIT)


def shard_copies(refs, order_ref, cols, target, sems, base=0, turn=None):
    copies = []
    total = target.shape[0]
    for ref in refs:
        rows = ref.shape[1]
        for n in range(ref.shape[0]):
            index = len(copies)
            row = order_ref[index] * rows
            if turn is not None:
                row = lax.rem(row + turn, total)
            row = pl.multiple_of(row, TILE)
            copies.append(pltpu.make_async_copy(ref.at[n, :, cols], target.at[pl.ds(row, rows), :], sems.at[base + index]))
    return copies


def shards_of(pieces):
    return sum(piece.shape[0] for piece in pieces)


def place_kernel(count, width, order_ref, *refs):
    refs, (w_ref, vec_ref, sems) = refs[:count], refs[count:]
    shards = shards_of(refs)
    first = pl.multiple_of(order_ref[shards], 128)
    copies = shard_copies(refs, order_ref, pl.ds(first, width), w_ref, sems)
    copies += shard_copies(refs, order_ref, slice(2 * width, refs[0].shape[2]), vec_ref, sems, shards)
    for copy in copies:
        copy.start()
    for copy in copies:
        copy.wait()


def place(pieces, order, width):
    rows = shards_of(pieces) * pieces[0].shape[1]
    return pl.pallas_call(
        functools.partial(place_kernel, len(pieces), width),
        in_specs=[SMEM] + [ANY] * len(pieces),
        out_shape=[
            jax.ShapeDtypeStruct((rows, width), BF),
            jax.ShapeDtypeStruct((rows, pieces[0].shape[2] - 2 * width), BF),
        ],
        scratch_shapes=[pltpu.SemaphoreType.DMA((2 * shards_of(pieces),))],
        compiler_params=params(),
        name="place",
    )(order, *pieces)


def head_parts(block):
    lane = lax.broadcasted_iota(jnp.int32, block.shape, 1)
    zero = jnp.zeros_like(block)
    return [jnp.where(lane < HD, block, zero), jnp.where(lane < HD, zero, block)]


def attend_kernel(chunk, extra, q_ref, k_ref, v_ref, sq_ref, sk_ref, *rest):
    o_ref, p_ref, l_ref, vt_ref, kn_ref = rest[extra:]
    i = pl.program_id(1)
    total = k_ref.shape[0]
    block = q_ref.shape[0]

    @pl.when(i == 0)
    def _():
        vt_ref[...] = v_ref[...].T
        keys = k_ref[...].astype(F32)
        norms = jnp.sum((keys * keys).T.reshape(2, HD, total), axis=1)
        kn_ref[...] = jnp.sqrt(jnp.max(norms, axis=1, keepdims=True))

    q = q_ref[...]
    parts = head_parts(q)
    q32 = q.astype(F32)
    qn = jnp.sqrt(jnp.sum((q32 * q32).T.reshape(2, HD, block), axis=1))
    bound = qn * kn_ref[...]
    seg_q = sq_ref[...]
    ones = jnp.ones((16, chunk), BF)

    def scores(h, lo):
        s = mm(k_ref[lo : lo + chunk, :], parts[h], NT)
        return jnp.where(sk_ref[lo : lo + chunk, :] == seg_q, s, MASKED)

    def finish(shift):
        acc = [jnp.zeros((HD + 16, block), F32)] * 2
        for lo in range(0, total, chunk):
            for h in range(2):
                p = jnp.exp(scores(h, lo) - shift[h : h + 1]).astype(BF)
                p_ref[h, lo : lo + chunk, :] = p
                left = jnp.concatenate([vt_ref[h * HD : h * HD + HD, lo : lo + chunk], ones], axis=0)
                acc[h] = acc[h] + mm(left, p)
        sums = [acc[h][HD : HD + 1] for h in range(2)]
        out = jnp.concatenate([acc[h][:HD] / sums[h] for h in range(2)], axis=0)
        o_ref[...] = out.T.astype(BF)
        sums = jnp.concatenate(sums, axis=0)
        l_ref[...] = 1.0 / sums
        return sums

    sums = finish(bound)
    good = jnp.min(sums) > 1e-20

    @pl.when(jnp.logical_not(good))
    def _():
        most = [jnp.full((1, block), MASKED, F32)] * 2
        for lo in range(0, total, chunk):
            for h in range(2):
                most[h] = jnp.maximum(most[h], jnp.max(scores(h, lo), axis=0, keepdims=True))
        finish(jnp.concatenate(most, axis=0))


def attend(qkv, seg_row, seg_col, base, pairs, held=None, waits=(), block=256, chunk=512):
    total = qkv.shape[0]
    specs = lambda c: pl.BlockSpec((total, 128), lambda h, i: (0, 3 * (base + h) + c))
    kept = [] if held is None else [held]
    return pl.pallas_call(
        functools.partial(attend_kernel, chunk, len(waits) + len(kept)),
        grid=(pairs, total // block),
        in_specs=[
            pl.BlockSpec((block, 128), lambda h, i: (i, 3 * (base + h))),
            specs(1),
            specs(2),
            pl.BlockSpec((1, block), lambda h, i: (0, i)),
            pl.BlockSpec((total, 1), lambda h, i: (0, 0)),
        ] + [ANY] * (len(kept) + len(waits)),
        out_specs=[
            pl.BlockSpec((block, 128), lambda h, i: (i, base + h)),
            pl.BlockSpec((None, 2, total, block), lambda h, i: (h, 0, 0, i)),
            pl.BlockSpec((None, 2, block), lambda h, i: (h, 0, i)),
        ],
        out_shape=[
            jax.ShapeDtypeStruct((total, qkv.shape[1] // 3), BF),
            jax.ShapeDtypeStruct((pairs, 2, total, total), BF),
            jax.ShapeDtypeStruct((pairs, 2, total), F32),
        ],
        scratch_shapes=[pltpu.VMEM((128, total), BF), pltpu.VMEM((2, 1), F32)],
        compiler_params=params(),
        cost_estimate=pl.CostEstimate(flops=pairs * 12 * 10**9, bytes_accessed=pairs << 24, transcendentals=0),
        input_output_aliases={5: 0} if kept else {},
        name="attend",
    )(qkv, qkv, qkv, seg_row, seg_col, *kept, *waits)


def attend_back_kernel(chunk, extra, q_ref, k_ref, v_ref, o_ref, do_ref, do2_ref, p_ref, l_ref, *rest):
    out_ref, mark_ref, kt_ref, dk_acc, dv_acc = rest[extra:]
    mark_ref[...] = jnp.zeros_like(mark_ref)
    i = pl.program_id(1)
    total = k_ref.shape[0]
    block = q_ref.shape[0]

    @pl.when(i == 0)
    def _():
        kt_ref[...] = k_ref[...].T
        dk_acc[...] = jnp.zeros_like(dk_acc)
        dv_acc[...] = jnp.zeros_like(dv_acc)

    do = jnp.where(i < pl.num_programs(1) // 2, do_ref[...], do2_ref[...])
    q_parts = head_parts(q_ref[...])
    do_parts = head_parts(do)
    product = do.astype(F32) * o_ref[...].astype(F32)
    delta = jnp.sum(product.T.reshape(2, HD, block), axis=1)
    inverse = l_ref[...]
    grad_q = [jnp.zeros((HD, block), F32)] * 2
    for lo in range(0, total, chunk):
        rows = slice(lo, lo + chunk)
        values = v_ref[rows, :]
        for h in range(2):
            p = p_ref[h, rows, :].astype(F32) * inverse[h : h + 1]
            grad_p = mm(values, do_parts[h], NT)
            grad_s = (p * (grad_p - delta[h : h + 1])).astype(BF)
            dv_acc[rows, :] += mm(p.astype(BF), do_parts[h])
            dk_acc[rows, :] += mm(grad_s, q_parts[h])
            grad_q[h] = grad_q[h] + mm(kt_ref[h * HD : h * HD + HD, rows], grad_s)
    out_ref[pl.ds(pl.multiple_of(i * block, block), block), 0:128] = jnp.concatenate(grad_q, axis=0).T.astype(BF)

    @pl.when(i == pl.num_programs(1) - 1)
    def _():
        out_ref[:, 128:256] = dk_acc[...].astype(BF)
        out_ref[:, 256:384] = dv_acc[...].astype(BF)


def attend_back(qkv, out, grad_mine, grad_mate, probs, inverse, base, held=None, waits=(), block=256, chunk=512):
    total = qkv.shape[0]
    kept = [] if held is None else [held]
    pairs = probs.shape[0]
    last = total // block // 2 - 1
    whole = lambda c: pl.BlockSpec((total, 128), lambda h, i: (0, 3 * (base + h) + c))
    rows = pl.BlockSpec((block, 128), lambda h, i: (i, base + h))
    return pl.pallas_call(
        functools.partial(attend_back_kernel, chunk, len(waits) + len(kept)),
        grid=(pairs, total // block),
        in_specs=[
            pl.BlockSpec((block, 128), lambda h, i: (i, 3 * (base + h))),
            whole(1),
            whole(2),
            rows,
            pl.BlockSpec((block, 128), lambda h, i: (jnp.minimum(i, last), base + h)),
            pl.BlockSpec((block, 128), lambda h, i: (jnp.maximum(i - last - 1, 0), base + h)),
            pl.BlockSpec((None, 2, total, block), lambda h, i: (h, 0, 0, i)),
            pl.BlockSpec((None, 2, block), lambda h, i: (h, 0, i)),
        ] + [ANY] * (len(kept) + len(waits)),
        out_specs=[pl.BlockSpec((total, 384), lambda h, i: (0, base + h)), pl.BlockSpec((8, 128), lambda h, i: (0, 0))],
        out_shape=[jax.ShapeDtypeStruct(qkv.shape, BF), jax.ShapeDtypeStruct((8, 128), F32)],
        scratch_shapes=[
            pltpu.VMEM((128, total), BF),
            pltpu.VMEM((total, 128), F32),
            pltpu.VMEM((total, 128), F32),
        ],
        compiler_params=params(),
        cost_estimate=pl.CostEstimate(flops=pairs * 21 * 10**9, bytes_accessed=pairs << 24, transcendentals=0),
        input_output_aliases={8: 0} if kept else {},
        name="attend_back",
    )(qkv, qkv, qkv, out, grad_mine, grad_mate, probs, inverse, *kept, *waits)


def gelu_parts(u):
    scaled = jnp.abs(u) * 0.7071067811865476
    den = 1.0 + 0.3275911 * scaled
    t = pl.reciprocal(den, approx=True)
    t = t * (2.0 - den * t)
    e = jnp.exp(u * u * -0.5)
    poly = t * (
        0.127414796
        + t * (-0.142248368 + t * (0.7107068705 + t * (-0.7265760135 + t * 0.5307027145)))
    )
    tail = poly * e
    phi = jnp.where(u >= 0, 1.0 - tail, tail)
    return u * phi, phi + u * (e * 0.3989422804014327)


def mean(value):
    return jnp.mean(value, axis=-1, keepdims=True)


def normed(hidden):
    centred = hidden - mean(hidden)
    inverse = lax.rsqrt(mean(centred * centred) + EPSILON)
    return centred * inverse, inverse


def norm_back(grad_in, scaled, inverse, gain):
    grad_scaled = grad_in * gain
    return inverse * (grad_scaled - mean(grad_scaled) - scaled * mean(grad_scaled * scaled))


def fold(value):
    return jnp.sum(value.reshape(value.shape[0] // 8, 8, value.shape[1]), axis=0)


def add_fold(ref, first, value):
    part = fold(value)

    @pl.when(first)
    def _():
        ref[...] = part

    @pl.when(jnp.logical_not(first))
    def _():
        ref[...] += part


def token_rows(x, span, block, at=lambda i: i):
    return pl.BlockSpec((block // span, span, x.shape[2]), lambda i: (at(i), 0, 0))


def qkv_kernel(xm_ref, xt_ref, w_ref, b_ref, out_ref):
    i = pl.program_id(0)
    x = jnp.where(i < pl.num_programs(0) // 2, xm_ref[...], xt_ref[...])
    out_ref[...] = (mm(x.reshape(out_ref.shape[0], -1), w_ref[...]) + b_ref[...]).astype(BF)


def project(x_mine, x_mate, span, weight, bias, block=256):
    steps = x_mine.shape[0] * span // block
    full = lambda a: pl.BlockSpec(a.shape, lambda i: (0, 0), pipeline_mode=pl.Buffered(1))
    width = weight.shape[1]
    return pl.pallas_call(
        qkv_kernel,
        grid=(2 * steps,),
        in_specs=[
            token_rows(x_mine, span, block, lambda i: jnp.minimum(i, steps - 1)),
            token_rows(x_mate, span, block, lambda i: jnp.maximum(i - steps, 0)),
            full(weight),
            full(bias),
        ],
        out_specs=pl.BlockSpec((block, width), lambda i: (i, 0)),
        out_shape=jax.ShapeDtypeStruct((2 * steps * block, width), BF),
        compiler_params=params(),
        cost_estimate=pl.CostEstimate(flops=7 * 10**9, bytes_accessed=14 << 20, transcendentals=0),
        name="project",
    )(x_mine, x_mate, weight, bias)


def mid_up_kernel(step, count, mates, order_ref, x_ref, om_ref, vec_ref, bu_ref, *refs):
    mate_refs, refs = refs[:mates], refs[mates:]
    pieces, (xh_ref, r_ref, xb_ref, g_ref, gp_ref, wo_ref, wu_ref, sems) = refs[:count], refs[count:]
    first = pl.program_id(0) == 0
    d, ff = wu_ref.shape
    shards = shards_of(pieces)

    def out_copies():
        return shard_copies(pieces, order_ref, slice(0, d), wo_ref, sems, 0, order_ref[shards])

    def up_copies():
        return shard_copies(pieces, order_ref, slice(d, d + ff), wu_ref, sems, shards)

    @pl.when(first)
    def _():
        for copy in out_copies() + up_copies():
            copy.start()
        for copy in out_copies():
            copy.wait()

    half = om_ref.shape[1]
    mixed = mm(om_ref[...], wo_ref[0:half, :])
    for ref in mate_refs:
        mixed = mixed + mm(ref[...], wo_ref[half : half + ref.shape[1], :])
        half += ref.shape[1]
    hidden = x_ref[...].reshape(mixed.shape).astype(F32) + mixed + vec_ref[0:1, :]
    scaled, inverse = normed(hidden)
    xh_ref[...] = scaled
    r_ref[...] = inverse
    xb = (scaled * vec_ref[1:2, :] + vec_ref[2:3, :]).astype(BF)
    xb_ref[...] = xb

    @pl.when(first)
    def _():
        for copy in up_copies():
            copy.wait()

    for lo in range(0, ff, step):
        cols = slice(lo, lo + step)
        g, gp = gelu_parts(mm(xb, wu_ref[:, cols]) + bu_ref[:, cols])
        g_ref[:, cols] = g.astype(BF)
        gp_ref[:, cols] = gp.astype(BF)


def mid_up(x, span, attn, o_mate, pieces, order, vecs, b_up, block=256, step=512):
    rows, d = x.shape[0] * span, x.shape[2]
    ff = b_up.shape[1]
    row = lambda n: pl.BlockSpec((block, n), lambda i: (i, 0))
    full = lambda a: pl.BlockSpec(a.shape, lambda i: (0, 0), pipeline_mode=pl.Buffered(1))
    return pl.pallas_call(
        functools.partial(mid_up_kernel, step, len(pieces), len(o_mate)),
        grid=(rows // block,),
        in_specs=[SMEM, token_rows(x, span, block), row(d // 2), full(vecs), full(b_up)]
        + [row(a.shape[1]) for a in o_mate]
        + [ANY] * len(pieces),
        out_specs=[row(d), row(1), row(d), row(ff), row(ff)],
        out_shape=[
            jax.ShapeDtypeStruct((rows, d), F32),
            jax.ShapeDtypeStruct((rows, 1), F32),
            jax.ShapeDtypeStruct((rows, d), BF),
            jax.ShapeDtypeStruct((rows, ff), BF),
            jax.ShapeDtypeStruct((rows, ff), BF),
        ],
        scratch_shapes=[
            pltpu.VMEM((d, d), BF),
            pltpu.VMEM((d, ff), BF),
            pltpu.SemaphoreType.DMA((2 * shards_of(pieces),)),
        ],
        compiler_params=params(),
        cost_estimate=pl.CostEstimate(flops=20 * 10**9, bytes_accessed=36 << 20, transcendentals=0),
        name="mid_up",
    )(order, x, attn, vecs, b_up, *o_mate, *pieces)


def mid_down_kernel(step, count, order_ref, g_ref, gp_ref, xh_ref, dy_ref, vec_ref, *refs):
    pieces, (out_ref, dh_ref, dm_ref, du_ref, s_ref, su_ref, wd_ref, sems) = refs[:count], refs[count:]
    first = pl.program_id(0) == 0
    d = wd_ref.shape[1]

    @pl.when(first)
    def _():
        copies = shard_copies(pieces, order_ref, slice(0, d), wd_ref, sems)
        for copy in copies:
            copy.start()
        for copy in copies:
            copy.wait()

    x1 = xh_ref[...] * vec_ref[1:2, :] + vec_ref[2:3, :]
    hidden = x1 + mm(g_ref[...], wd_ref[...]) + vec_ref[3:4, :]
    scaled, inverse = normed(hidden)
    gain = vec_ref[4:5, :]
    out_ref[...] = (scaled * gain + vec_ref[5:6, :]).astype(BF)
    dy = dy_ref[...].astype(F32)
    dh = norm_back(dy, scaled, inverse, gain)
    dm = dh.astype(BF)
    dh_ref[...] = dh
    dm_ref[...] = dm
    add_fold(s_ref.at[0:8, :], first, dy * scaled)
    add_fold(s_ref.at[8:16, :], first, dy)
    add_fold(s_ref.at[16:24, :], first, dm.astype(F32))
    for lo in range(0, wd_ref.shape[0], step):
        cols = slice(lo, lo + step)
        du = (mm(dm, wd_ref[cols, :], NT) * gp_ref[:, cols].astype(F32)).astype(BF)
        du_ref[:, cols] = du
        add_fold(su_ref.at[:, cols], first, du.astype(F32))


def mid_down(g, gp, xh, dy, pieces, order, vecs, block=256, step=2048):
    rows, d = xh.shape
    ff = g.shape[1]
    row = lambda n: pl.BlockSpec((block, n), lambda i: (i, 0))
    full = lambda a: pl.BlockSpec(a.shape, lambda i: (0, 0), pipeline_mode=pl.Buffered(1))
    keep = lambda r, n: pl.BlockSpec((r, n), lambda i: (0, 0))
    return pl.pallas_call(
        functools.partial(mid_down_kernel, step, len(pieces)),
        grid=(rows // block,),
        in_specs=[SMEM, row(ff), row(ff), row(d), row(d), full(vecs)] + [ANY] * len(pieces),
        out_specs=[row(d), row(d), row(d), row(ff), keep(24, d), keep(8, ff)],
        out_shape=[
            jax.ShapeDtypeStruct((rows, d), BF),
            jax.ShapeDtypeStruct((rows, d), F32),
            jax.ShapeDtypeStruct((rows, d), BF),
            jax.ShapeDtypeStruct((rows, ff), BF),
            jax.ShapeDtypeStruct((24, d), F32),
            jax.ShapeDtypeStruct((8, ff), F32),
        ],
        scratch_shapes=[pltpu.VMEM((ff, d), BF), pltpu.SemaphoreType.DMA((shards_of(pieces),))],
        compiler_params=params(),
        cost_estimate=pl.CostEstimate(flops=25 * 10**9, bytes_accessed=44 << 20, transcendentals=0),
        name="mid_down",
    )(order, g, gp, xh, dy, vecs, *pieces)


def mid_back_kernel(count, order_ref, dh_ref, du_ref, xh_ref, r_ref, vec_ref, *refs):
    pieces, (dh1_ref, da_ref, dom_ref, dot_ref, s_ref, wu_ref, wo_ref, sems) = refs[:count], refs[count:]
    first = pl.program_id(0) == 0
    d, ff = wu_ref.shape
    half = dom_ref.shape[1]
    shards = shards_of(pieces)

    @pl.when(first)
    def _():
        copies = shard_copies(pieces, order_ref, slice(d, d + ff), wu_ref, sems, shards)
        copies += shard_copies(pieces, order_ref, slice(0, d), wo_ref, sems, 0, order_ref[shards])
        for copy in copies:
            copy.start()
        for copy in copies:
            copy.wait()

    dx = dh_ref[...] + mm(du_ref[...], wu_ref[...], NT)
    scaled = xh_ref[...]
    dh1 = norm_back(dx, scaled, r_ref[...], vec_ref[1:2, :])
    dh1_ref[...] = dh1
    da = dh1.astype(BF)
    da_ref[...] = da
    dom_ref[...] = mm(da, wo_ref[0:half, :], NT).astype(BF)
    dot_ref[...] = mm(da, wo_ref[half:, :], NT).astype(BF)
    add_fold(s_ref.at[0:8, :], first, dx * scaled)
    add_fold(s_ref.at[8:16, :], first, dx)
    add_fold(s_ref.at[16:24, :], first, da.astype(F32))


def mid_back(dh, du, xh, r, pieces, order, vecs, block=256):
    rows, d = dh.shape
    ff = du.shape[1]
    row = lambda n: pl.BlockSpec((block, n), lambda i: (i, 0))
    full = lambda a: pl.BlockSpec(a.shape, lambda i: (0, 0), pipeline_mode=pl.Buffered(1))
    return pl.pallas_call(
        functools.partial(mid_back_kernel, len(pieces)),
        grid=(rows // block,),
        in_specs=[SMEM, row(d), row(ff), row(d), row(1), full(vecs)] + [ANY] * len(pieces),
        out_specs=[row(d), row(d), row(d // 2), row(d // 2), pl.BlockSpec((24, d), lambda i: (0, 0))],
        out_shape=[
            jax.ShapeDtypeStruct((rows, d), F32),
            jax.ShapeDtypeStruct((rows, d), BF),
            jax.ShapeDtypeStruct((rows, d // 2), BF),
            jax.ShapeDtypeStruct((rows, d // 2), BF),
            jax.ShapeDtypeStruct((24, d), F32),
        ],
        scratch_shapes=[
            pltpu.VMEM((d, ff), BF),
            pltpu.VMEM((d, d), BF),
            pltpu.SemaphoreType.DMA((2 * shards_of(pieces),)),
        ],
        compiler_params=params(),
        cost_estimate=pl.CostEstimate(flops=15 * 10**9, bytes_accessed=36 << 20, transcendentals=0),
        name="mid_back",
    )(order, dh, du, xh, r, vecs, *pieces)


def token_kernel(split, waits, chip_ref, grad_ref, w_ref, *refs):
    outs = refs[len(refs) - split :]
    total = mm(grad_ref[...], w_ref[...], NT)
    for ref in refs[: len(refs) - split - waits]:
        total = total + ref[...].astype(F32)
    total = total.astype(BF)
    if split == 1:
        outs[0][...] = total
        return
    for n in range(split):

        @pl.when(pl.program_id(0) == n)
        def _():
            outs[n][...] = total


def token_grad(grads, weight, shift, adds, chip, chips, split, waits=()):
    d = weight.shape[0]
    rows = grads.shape[0] // 2
    block = rows // chips
    base = shift * chips
    at = lambda i, c: c[0] ^ i if split else i
    plain = lambda a: pl.BlockSpec((block, a.shape[1]), lambda i, c: (at(i, c), 0))
    if split:
        out_specs = [pl.BlockSpec((block, d), lambda i, c: (0, 0))] * chips
        out_shape = [jax.ShapeDtypeStruct((block, d), BF)] * chips
    else:
        out_specs = [pl.BlockSpec((block, d), lambda i, c: (i, 0))]
        out_shape = [jax.ShapeDtypeStruct((rows, d), BF)]
    return pl.pallas_call(
        functools.partial(token_kernel, len(out_shape), len(waits)),
        grid_spec=pltpu.PrefetchScalarGridSpec(
            num_scalar_prefetch=1,
            grid=(chips,),
            in_specs=[
                pl.BlockSpec((block, grads.shape[1]), lambda i, c: (base + at(i, c), 0)),
                pl.BlockSpec(weight.shape, lambda i, c: (0, 0), pipeline_mode=pl.Buffered(1)),
            ]
            + [plain(a) for a in adds]
            + [ANY] * len(waits),
            out_specs=out_specs,
        ),
        out_shape=out_shape,
        compiler_params=params(),
        cost_estimate=pl.CostEstimate(flops=10**8, bytes_accessed=1 << 16, transcendentals=0),
        name="token_grad",
    )(jnp.reshape(chip, (1,)).astype(jnp.int32), grads, weight, *adds, *waits)


def order_kernel(chip_ref, *refs):
    pieces, (out_ref, sems) = refs[:-2], refs[-2:]
    copies = [
        pltpu.make_async_copy(piece, out_ref.at[chip_ref[0] ^ n], sems.at[n]) for n, piece in enumerate(pieces)
    ]
    for copy in copies:
        copy.start()
    for copy in copies:
        copy.wait()


def in_order(pieces, chip):
    chips = len(pieces)
    return pl.pallas_call(
        order_kernel,
        in_specs=[SMEM] + [ANY] * chips,
        out_shape=jax.ShapeDtypeStruct((chips,) + pieces[0].shape, BF),
        scratch_shapes=[pltpu.SemaphoreType.DMA((chips,))],
        compiler_params=params(),
        name="in_order",
    )(jnp.reshape(chip, (1,)).astype(jnp.int32), *pieces)


def by_chip(value, out_ref, lo):
    chips, dps, rows, _ = out_ref.shape
    value = value.reshape(dps, chips, rows, value.shape[1])
    for n in range(dps):
        out_ref[:, n, :, lo : lo + value.shape[3]] = value[n].astype(BF)


def proj_kernel(xm_ref, xt_ref, grad_ref, *refs):
    out_ref = refs[-1]
    own = grad_ref.shape[0] // 2
    xm = xm_ref[...].reshape(own, -1)
    xt = xt_ref[...].reshape(own, -1)
    by_chip(mm(xm, grad_ref[0:own, :], TN) + mm(xt, grad_ref[own:, :], TN), out_ref, 0)
    if grad_ref.shape[1] < out_ref.shape[3]:
        out_ref[:, :, :, grad_ref.shape[1] :] = refs[0][...]


def dp_steps(groups, least):
    return max(1, min(groups, least // 128))


def shard_specs(steps, groups, chips, rows, cols):
    spec = pl.BlockSpec((chips, groups // steps, rows, cols), lambda i, *_: (0, i, 0, 0))
    return spec, jax.ShapeDtypeStruct((chips, groups, rows, cols), BF)


def proj_grad(x_mine, x_mate, span, grads, first, pairs, groups, chips, waits=(), extra=None):
    own, d = x_mine.shape[0] * span, x_mine.shape[2]
    width = 384 * pairs
    more = [] if extra is None else [extra]
    steps = dp_steps(groups, d)
    col = pl.BlockSpec((x_mine.shape[0], span, d // steps), lambda i: (0, 0, i))
    rows = d // groups // chips
    spec, shape = shard_specs(steps, groups, chips, rows, width + sum(a.shape[3] for a in more))
    return pl.pallas_call(
        proj_kernel,
        grid=(steps,),
        in_specs=[col, col]
        + [pl.BlockSpec((2 * own, width), lambda i: (0, first // pairs), pipeline_mode=pl.Buffered(1))]
        + [shard_specs(steps, groups, chips, rows, a.shape[3])[0] for a in more]
        + [ANY] * len(waits),
        out_specs=spec,
        out_shape=shape,
        compiler_params=params(),
        cost_estimate=pl.CostEstimate(flops=10**8, bytes_accessed=1 << 16, transcendentals=0),
        name="proj_grad",
    )(x_mine, x_mate, grads, *more, *waits)


def weight_kernel(adds, waits, turn_ref, *refs):
    out_ref, refs = refs[-1], refs[: len(refs) - 1 - waits]
    count = (len(refs) - adds) // 2
    more = refs[2 * count :]
    lo = 0
    for n in range(count):
        value = mm(refs[2 * n][...], refs[2 * n + 1][...], TN)
        width = value.shape[1]
        chips, dps, rows, _ = out_ref.shape
        value = value.reshape(dps, chips, rows, width)
        for k in range(dps):
            part = value[k]
            if more:
                part = part + more[0][:, k, :, lo : lo + width].astype(F32)
            out_ref[:, k, :, lo : lo + width] = part.astype(BF)
        lo += width
    if lo < out_ref.shape[3]:
        out_ref[:, :, :, lo:] = more[-1][...]


def weight_grad(sides, turns, groups, chips, adds=(), waits=()):
    in_specs, args = [], []
    steps = dp_steps(groups, min(left.shape[1] for left, _ in sides))
    rows_of = lambda a: a.shape[1] // steps
    for n, (left, right) in enumerate(sides):
        tokens = left.shape[0]
        in_specs.append(
            pl.BlockSpec((tokens, rows_of(left)), lambda i, t, n=n: (0, lax.rem(i + t[1 + n] * (steps // 2), steps)))
        )
        in_specs.append(
            pl.BlockSpec((tokens, right.shape[1] // 2), lambda i, t: (0, t[0]), pipeline_mode=pl.Buffered(1))
        )
        args += [left, right]
    rows = sides[0][0].shape[1] // groups // chips
    cols = sum(right.shape[1] // 2 for _, right in sides)
    if len(adds) > 1:
        cols += adds[1].shape[3]
    in_specs += [shard_specs(steps, groups, chips, rows, a.shape[3])[0] for a in adds] + [ANY] * len(waits)
    spec, shape = shard_specs(steps, groups, chips, rows, cols)
    flops = sum(a.shape[0] * a.shape[1] * b.shape[1] for a, b in sides)
    return pl.pallas_call(
        functools.partial(weight_kernel, len(adds), len(waits)),
        grid_spec=pltpu.PrefetchScalarGridSpec(
            num_scalar_prefetch=1, grid=(steps,), in_specs=in_specs, out_specs=spec
        ),
        out_shape=shape,
        compiler_params=params(),
        cost_estimate=pl.CostEstimate(flops=flops, bytes_accessed=20 << 20, transcendentals=0),
        name="weight_grad",
    )(turns, *args, *adds, *waits)


def swap(value, mask):
    count = lax.axis_size("ctx")
    return lax.ppermute(value, "ctx", [(d, d ^ mask) for d in range(count)])


def along(value, step):
    count = lax.axis_size("dp")
    return lax.ppermute(value, "dp", [(s, (s + step) % count) for s in range(count)])


def pick(value, index, axis=0):
    return lax.dynamic_index_in_dim(value, index, axis, keepdims=False)


def over_chips(value):
    count = lax.axis_size("ctx")
    groups = [list(range(core, count, 2)) for core in range(2)]
    return lax.all_to_all(value, "ctx", 0, 0, axis_index_groups=groups)


def repeat(value):
    return jnp.broadcast_to(value[None], (lax.axis_size("ctx") // 2,) + value.shape)


def tick(value):
    return (value[(0,) * value.ndim].astype(F32) > 1e30).astype(jnp.int32)


def tie_kernel(*refs):
    pass


def tie(value, *waits):
    return pl.pallas_call(
        tie_kernel,
        in_specs=[ANY] * (1 + len(waits)),
        out_specs=ANY,
        out_shape=jax.ShapeDtypeStruct(value.shape, value.dtype),
        input_output_aliases={0: 0},
        name="tie",
    )(value, *waits)


class Gather:
    def __init__(self, own, place):
        self.place = place
        self.groups = lax.axis_size("dp")
        self.chips = lax.axis_size("ctx") // 2
        self.own = own
        self.whole = own.shape[0] % TILE != 0

    def along_dp(self, value):
        if self.whole:
            return []
        self.turns = [value] + [along(value, s) for s in range(1, self.groups)]
        return self.turns[1:]

    def over_chips(self, later):
        if self.whole:
            return []
        self.held = over_chips(repeat(jnp.stack(self.turns) + later.astype(BF)))
        return [self.held]

    def plane(self):
        if self.whole:
            return []
        got = [swap(self.own, 2 * r) for r in range(1, self.chips)]
        self.held = jnp.stack([self.own] + got)
        return got

    def dp_arrays(self):
        self.held = self.turns
        return self.turns

    def between_cores(self, *waits):
        me, chip, core = self.place
        if self.whole:
            return [lax.all_gather(self.own, BOTH, axis=0, tiled=True)[None]], jnp.zeros((1,), jnp.int32)
        count = 2 * self.chips
        turn = (me - jnp.arange(self.groups)) % self.groups * count
        chip_of = jnp.arange(self.chips)
        if isinstance(self.held, list):
            pieces, order = [], []
            for n, value in enumerate(self.held):
                value = tie(value, *waits) if waits else value
                pieces += [value, swap(value, 1)]
                order += [turn[n] + 2 * (chip_of ^ chip) + core, turn[n] + 2 * (chip_of ^ chip) + 1 - core]
        else:
            flat = self.held.reshape((-1,) + self.own.shape)
            flat = tie(flat, *waits) if waits else flat
            pieces = [flat, swap(flat, 1)]
            numbers = (turn[None] + 2 * chip_of[:, None]).reshape(-1)
            order = [numbers + core, numbers + 1 - core]
        return pieces, jnp.concatenate(order).astype(jnp.int32)


class Reduce:
    def __init__(self, grad, place, direct=False):
        self.place = place
        self.groups = grad.shape[1]
        if direct:
            chip = place[1]
            sent = [pick(grad, chip ^ r) for r in range(1, grad.shape[0])]
            self.got = [pick(grad, chip)] + [swap(v, 2 * (r + 1)) for r, v in enumerate(sent)]
        else:
            self.got = over_chips(grad)

    def chip_sum(self, *waits):
        if isinstance(self.got, list):
            last = tie(self.got[-1], *self.got[1:-1], *waits)
            self.part = sum(v.astype(F32) for v in self.got[:-1] + [last]).astype(BF)
        else:
            self.part = jnp.sum(tie(self.got, *waits).astype(F32), axis=0).astype(BF)
        return [self.part]

    def along_dp(self):
        me = self.place[0]
        sent = [pick(self.part, (me + step) % self.groups) for step in range(1, self.groups)]
        self.turns = [pick(self.part, me)] + [along(v, n + 1) for n, v in enumerate(sent)]

    def dp_sum(self, *waits):
        last = tie(self.turns[-1], *self.turns[1:-1], *waits)
        total = sum(v.astype(F32) for v in self.turns[:-1] + [last]).astype(BF)
        self.total = total.reshape(2, -1, total.shape[1])
        return [self.total]

    def finish(self):
        core = self.place[2]
        mine = pick(self.total, core).astype(F32)
        other = swap(pick(self.total, 1 - core), 1).astype(F32)
        return [jnp.where(core == 0, mine, other), jnp.where(core == 0, other, mine)], mine + other


def half_cols(value, which):
    width = value.shape[-1] // 2
    return lax.dynamic_slice_in_dim(value, which * width, width, value.ndim - 1)


def spread(vectors, shards, rows):
    flat = jnp.concatenate([v.reshape(shards, -1) for v in vectors], axis=1)
    return jnp.pad(flat, ((0, 0), (0, rows * 128 - flat.shape[1]))).reshape(shards, rows, 128)


def fold_rows(sums):
    return jnp.sum(sums.reshape(-1, 8, sums.shape[1]), axis=1)


def local(
    tokens, segments, cotangent, w_query, w_key, w_value, w_out, w_up, w_down,
    b_query, b_value, b_out, b_up, b_down, gain_attn, shift_attn, gain_mlp, shift_mlp,
):
    seqs, span, d = tokens.shape
    count = lax.axis_size("ctx")
    groups = lax.axis_size("dp")
    chips = count // 2
    ctx = lax.axis_index("ctx")
    chip, core = ctx // 2, ctx % 2
    place_of = (lax.axis_index("dp"), chip, core)
    ff = w_up.shape[1]
    half = d // 2
    shards = groups * count
    rows = d // shards
    width = d // shards
    pairs = half // 128
    bf = lambda v: v.astype(BF)

    vec_names = (b_query, b_value, b_out, gain_attn, shift_attn, b_down, gain_mlp, shift_mlp)
    vec_size = 8 * width + ff // shards
    extra = -(-(vec_size + seqs * span) // (rows * 128)) * 128
    vec_pack = jnp.concatenate([bf(v) for v in vec_names] + [bf(b_up), bf(segments.reshape(-1))])
    vec_pack = jnp.pad(vec_pack, (0, rows * extra - vec_pack.shape[0])).reshape(rows, extra)
    by_pair = [bf(w).reshape(rows, 2 * pairs, 1, 128) for w in (w_query * QSCALE, w_key, w_value)]
    pack_proj = jnp.concatenate(
        [jnp.concatenate(by_pair, axis=2).reshape(rows, 3 * d), vec_pack], axis=1
    )

    got = over_chips(tokens)
    own = chips * span
    proj = Gather(pack_proj, place_of)
    turns_of = proj.along_dp(proj.own)
    got = tie(got, *turns_of)
    mate = swap(got, 1)
    later = tick(got)
    held = proj.over_chips(later)
    pieces, order = proj.between_cores()
    everywhere = lambda v: lax.all_gather(bf(v) + later.astype(BF), BOTH, axis=0, tiled=True).reshape(2, -1, v.shape[1])
    up_pieces = [everywhere(jnp.concatenate([w_out, w_up], axis=1))]
    down_pieces = [everywhere(w_down)]
    down_order = jnp.arange(2, dtype=jnp.int32)
    if proj.whole:
        w_cat = half_cols(pieces[0][0, :, : 3 * d], core)
        vec_block = pieces[0][0, :, 3 * d :]
    else:
        w_cat, vec_block = place(pieces, jnp.append(order, core * 3 * half), 3 * half)
    packed = vec_block.reshape(shards, rows * extra)
    vec_all = packed[:, :vec_size].astype(F32)
    seg_all = packed[:, vec_size : vec_size + seqs * span].reshape(groups, chips, 2, seqs, span)
    seg_own = pick(pick(seg_all, place_of[0]), chip, 2)
    seg = jnp.concatenate([pick(seg_own, core, 1), pick(seg_own, 1 - core, 1)]).reshape(-1).astype(jnp.int32)
    vec = [vec_all[:, n * width : (n + 1) * width].reshape(1, d) for n in range(8)]
    bias_up = vec_all[:, 8 * width : 8 * width + ff // shards].reshape(1, ff)
    vecs = jnp.concatenate(vec[2:] + [jnp.zeros((2, d), F32)], axis=0)
    bias_by_pair = [v.reshape(1, 2 * pairs, 1, 128) for v in (vec[0] * QSCALE, jnp.zeros((1, d), F32), vec[1])]
    bias_cat = half_cols(jnp.concatenate(bias_by_pair, axis=2).reshape(1, 3 * d), core)

    qkv = project(got, mate, span, w_cat, bias_cat)
    seg_row, seg_col = seg.reshape(1, -1), seg.reshape(-1, 1)

    waits = []
    attn, probs, inverse, o_mate = None, [], [], []
    for n in range(pairs):
        attn, p, l = attend(qkv, seg_row, seg_col, n, 1, attn, waits)
        probs.append(p)
        inverse.append(l)
        waits = []
        if n % 2 == 1:
            o_mate.append(swap(attn[own:, (n - 1) * 128 : (n + 1) * 128], 1))
    dy = over_chips(cotangent + tick(attn).astype(BF)).reshape(own, d)
    up_order = jnp.stack([jnp.zeros((), jnp.int32), jnp.ones((), jnp.int32), d - core * half]).astype(jnp.int32)
    xh, r, xb, g, gp = mid_up(got, span, attn, o_mate, up_pieces, up_order, vecs, bias_up)
    out, dh2, dm, du, sums_two, sums_up = mid_down(g, gp, xh, dy, down_pieces, down_order, vecs)
    result_out = over_chips(out.reshape(chips, span, d))

    zero = jnp.zeros((), jnp.int32)
    turns = lambda half_of, *more: jnp.stack([half_of, *more]).astype(jnp.int32)
    got_down = swap(weight_grad([(g, dm)], turns(1 - core, zero), groups, chips), 1)
    dh1, da, do_mine, do_send, sums_one = mid_back(dh2, du, xh, r, up_pieces, up_order, vecs)
    do_mate = swap(do_send, 1)
    kept_down = weight_grad([(g, dm)], turns(core, zero), groups, chips, [got_down], [result_out])
    sum_down = Reduce(kept_down, place_of)

    o_both = jnp.concatenate([attn[:own]] + o_mate, axis=1)
    sides, shift = [(xb, du), (o_both, da)], core
    got_up = swap(weight_grad(sides, turns(1 - core, zero, shift), groups, chips, (), [kept_down]), 1)
    two, one = fold_rows(sums_two), fold_rows(sums_one)
    per_shard = lambda v: jnp.moveaxis(bf(v).reshape(groups, chips, -1, 128), 1, 0)
    vec_grads = per_shard(spread([one[2], one[0], one[1], two[2], two[0], two[1], fold_rows(sums_up)], shards, rows))

    grads, waits = None, []
    for n in range(pairs):
        grads, mark = attend_back(qkv, attn, do_mine, do_mate, probs[n], inverse[n], n, grads, waits)
        waits = []
        if n == 0:
            got_up = tie(got_up, mark)
            kept_up = weight_grad(sides, turns(core, zero, shift), groups, chips, [got_up, vec_grads])
            waits = sum_down.chip_sum(mark, kept_up)
            sum_down.along_dp()
            sum_up = Reduce(kept_up, place_of)
        elif n == 1:
            waits = sum_down.dp_sum(mark)
        elif n == 2:
            first = proj_grad(got, mate, span, grads, 0, 3, groups, chips)
            waits = sum_up.chip_sum(mark, first)
            sum_up.along_dp()
            sum_first = Reduce(first, place_of)
    grads = tie(grads, *sum_first.chip_sum(mark), *sum_up.dp_sum(mark))
    bias_sums = jnp.sum(grads.astype(F32), axis=0).reshape(pairs, 3, 128)
    blank = jnp.zeros((half,), F32)

    def whole_vector(c):
        part = bias_sums[:, c].reshape(-1)
        return jnp.where(core == 0, jnp.concatenate([part, blank]), jnp.concatenate([blank, part]))

    bias_grads = per_shard(spread([whole_vector(0), whole_vector(2)], shards, rows))
    token_send = token_grad(grads, w_cat, 1, (), chip, chips, False)[0]
    token_got = swap(token_send, 1)
    last = proj_grad(got, mate, span, grads, 3, 1, groups, chips, [token_send], bias_grads)
    sum_last = Reduce(last, place_of, True)
    grad_mine = token_grad(grads, w_cat, 0, (dh1, token_got), chip, chips, False, [last])[0]
    sum_last.chip_sum(grad_mine)
    grad_mine = tie(grad_mine, sum_last.part)
    grad_tokens = over_chips(grad_mine.reshape(chips, span, d))
    sum_last.part = jnp.concatenate([sum_first.part, sum_last.part], axis=2)
    sum_last.along_dp()
    sum_last.dp_sum(grad_tokens)
    sum_up.total = jnp.concatenate([sum_up.total, sum_last.total], axis=2)

    halves, _ = sum_down.finish()
    grad_down = jnp.concatenate(halves, axis=1)
    halves, both = sum_up.finish()
    cuts = [0, ff // 2, half, 128, 3 * half - 384, 384, 128]
    cuts = [sum(cuts[: n + 1]) for n in range(len(cuts))]
    cut = lambda v, n: v[:, cuts[n] : cuts[n + 1]]
    grad_up = jnp.concatenate([cut(v, 0) for v in halves], axis=1)
    grad_out = jnp.concatenate([cut(v, 1) for v in halves], axis=1)
    small = cut(both, 2).reshape(-1)
    g_bo, g_ga, g_sa, g_bd, g_gm, g_sm = [small[n * width : (n + 1) * width] for n in range(6)]
    g_bu = small[6 * width : 6 * width + ff // shards]
    small = cut(both, 5).reshape(-1)
    g_bq, g_bv = small[:width] * QSCALE, small[width : 2 * width]
    joined = jnp.concatenate([v.reshape(rows, -1, 3, 128) for h in halves for v in (cut(h, 3), cut(h, 4))], axis=1)
    grad_query, grad_key, grad_value = [joined[:, :, c].reshape(rows, d) for c in range(3)]
    return (
        result_out, grad_tokens, grad_query * QSCALE, grad_key, grad_value, grad_out, grad_up, grad_down,
        g_bq, g_bv, g_bo, g_bu, g_bd, g_ga, g_sa, g_gm, g_sm,
    )


def solution(mesh):
    act, flat, mat, vec = P("dp", "ctx", None), P("dp", "ctx"), P(BOTH, None), P(BOTH)
    return jax.shard_map(
        local,
        mesh=mesh,
        in_specs=(act, flat, act) + (mat,) * 6 + (vec,) * 9,
        out_specs=(act, act) + (mat,) * 6 + (vec,) * 9,
        check_vma=False,
    )
```

```python
import functools

import jax
import jax.numpy as jnp
from jax import lax
from jax.experimental import pallas as pl
from jax.experimental.pallas import tpu as pltpu
from jax.sharding import PartitionSpec as P

HD = 64
MASKED = -1e30
EPSILON = 1e-05
QSCALE = 0.125
BF = jnp.bfloat16
F32 = jnp.float32
NT = (((1,), (1,)), ((), ()))
NN = (((1,), (0,)), ((), ()))
TN = (((0,), (0,)), ((), ()))
VMEM_LIMIT = 56 << 20
BOTH = ("dp", "ctx")
ANY = pl.BlockSpec(memory_space=pl.ANY)
SMEM = pl.BlockSpec(memory_space=pltpu.SMEM)
TILE = 16


def mm(a, b, dims=NN):
    return lax.dot_general(a, b, dims, preferred_element_type=F32)


def params():
    return pltpu.CompilerParams(vmem_limit_bytes=VMEM_LIMIT)


def shard_copies(refs, order_ref, cols, target, sems, base=0, turn=None, every=1, skip=0):
    copies = []
    total = target.shape[0]
    for ref in refs:
        rows = ref.shape[1]
        for n in range(ref.shape[0]):
            index = len(copies)
            row = (order_ref[index] * every + skip) * rows
            if turn is not None:
                row = lax.rem(row + turn, total)
            row = pl.multiple_of(row, TILE)
            copies.append(pltpu.make_async_copy(ref.at[n, :, cols], target.at[pl.ds(row, rows), :], sems.at[base + index]))
    return copies


def shards_of(pieces):
    return sum(piece.shape[0] for piece in pieces)


def pack_kernel(wq_ref, wk_ref, wv_ref, wo_ref, wu_ref, wd_ref, vec_ref, proj_ref, up_ref, *down):
    rows, d = wq_ref.shape
    ff = wu_ref.shape[1]
    for n, (ref, scale) in enumerate(((wq_ref, QSCALE), (wk_ref, None), (wv_ref, None))):
        for pair in range(d // 128):
            part = ref[:, pair * 128 : (pair + 1) * 128]
            part = part if scale is None else part * scale
            proj_ref[:, pair * 384 + n * 128 : pair * 384 + (n + 1) * 128] = part.astype(BF)
    proj_ref[:, 3 * d :] = vec_ref[...]
    up_ref[:, 0:d] = wo_ref[...].astype(BF)
    up_ref[:, d : d + ff] = wu_ref[...].astype(BF)
    if down:
        down[0][...] = wd_ref[...].astype(BF)
    else:
        for n in range(wd_ref.shape[0] // rows):
            up_ref[:, d + ff + n * d : d + ff + (n + 1) * d] = wd_ref[n * rows : (n + 1) * rows, :].astype(BF)


def pack(w_query, w_key, w_value, w_out, w_up, w_down, vec):
    rows, d = w_query.shape
    ff = w_up.shape[1]
    joined = rows % TILE == 0
    more = w_down.shape[0] // rows * d if joined else 0
    shapes = [(rows, 3 * d + vec.shape[1]), (rows, d + ff + more)] + ([] if joined else [w_down.shape])
    return pl.pallas_call(
        pack_kernel,
        out_shape=[jax.ShapeDtypeStruct(shape, BF) for shape in shapes],
        compiler_params=params(),
        name="pack",
    )(w_query, w_key, w_value, w_out, w_up, w_down, vec)


def place_kernel(count, width, order_ref, *refs):
    refs, (w_ref, vec_ref, sems) = refs[:count], refs[count:]
    shards = shards_of(refs)
    first = pl.multiple_of(order_ref[shards], 128)
    copies = shard_copies(refs, order_ref, pl.ds(first, width), w_ref, sems)
    copies += shard_copies(refs, order_ref, slice(2 * width, refs[0].shape[2]), vec_ref, sems, shards)
    for copy in copies:
        copy.start()
    for copy in copies:
        copy.wait()


def place(pieces, order, width):
    rows = shards_of(pieces) * pieces[0].shape[1]
    return pl.pallas_call(
        functools.partial(place_kernel, len(pieces), width),
        in_specs=[SMEM] + [ANY] * len(pieces),
        out_shape=[
            jax.ShapeDtypeStruct((rows, width), BF),
            jax.ShapeDtypeStruct((rows, pieces[0].shape[2] - 2 * width), BF),
        ],
        scratch_shapes=[pltpu.SemaphoreType.DMA((2 * shards_of(pieces),))],
        compiler_params=params(),
        name="place",
    )(order, *pieces)


def head_parts(block):
    lane = lax.broadcasted_iota(jnp.int32, block.shape, 1)
    zero = jnp.zeros_like(block)
    return [jnp.where(lane < HD, block, zero), jnp.where(lane < HD, zero, block)]


def attend_kernel(chunk, extra, q_ref, k_ref, v_ref, sq_ref, sk_ref, *rest):
    o_ref, p_ref, l_ref, vt_ref, kn_ref = rest[extra:]
    i = pl.program_id(1)
    total = k_ref.shape[0]
    block = q_ref.shape[0]

    @pl.when(i == 0)
    def _():
        vt_ref[...] = v_ref[...].T
        keys = k_ref[...].astype(F32)
        norms = jnp.sum((keys * keys).T.reshape(2, HD, total), axis=1)
        kn_ref[...] = jnp.sqrt(jnp.max(norms, axis=1, keepdims=True))

    q = q_ref[...]
    parts = head_parts(q)
    q32 = q.astype(F32)
    qn = jnp.sqrt(jnp.sum((q32 * q32).T.reshape(2, HD, block), axis=1))
    bound = qn * kn_ref[...]
    seg_q = sq_ref[...]
    ones = jnp.ones((16, chunk), BF)

    def scores(h, lo):
        s = mm(k_ref[lo : lo + chunk, :], parts[h], NT)
        return jnp.where(sk_ref[lo : lo + chunk, :] == seg_q, s, MASKED)

    def finish(shift):
        acc = [jnp.zeros((HD + 16, block), F32)] * 2
        for lo in range(0, total, chunk):
            for h in range(2):
                p = jnp.exp(scores(h, lo) - shift[h : h + 1]).astype(BF)
                p_ref[h, lo : lo + chunk, :] = p
                left = jnp.concatenate([vt_ref[h * HD : h * HD + HD, lo : lo + chunk], ones], axis=0)
                acc[h] = acc[h] + mm(left, p)
        sums = [acc[h][HD : HD + 1] for h in range(2)]
        out = jnp.concatenate([acc[h][:HD] / sums[h] for h in range(2)], axis=0)
        o_ref[...] = out.T.astype(BF)
        sums = jnp.concatenate(sums, axis=0)
        l_ref[...] = 1.0 / sums
        return sums

    sums = finish(bound)
    good = jnp.min(sums) > 1e-20

    @pl.when(jnp.logical_not(good))
    def _():
        most = [jnp.full((1, block), MASKED, F32)] * 2
        for lo in range(0, total, chunk):
            for h in range(2):
                most[h] = jnp.maximum(most[h], jnp.max(scores(h, lo), axis=0, keepdims=True))
        finish(jnp.concatenate(most, axis=0))


def attend(qkv, seg_row, seg_col, base, pairs, held=None, waits=(), block=512, chunk=1024):
    total = qkv.shape[0]
    specs = lambda c: pl.BlockSpec((total, 128), lambda h, i: (0, 3 * (base + h) + c))
    kept = [] if held is None else [held]
    return pl.pallas_call(
        functools.partial(attend_kernel, chunk, len(waits) + len(kept)),
        grid=(pairs, total // block),
        in_specs=[
            pl.BlockSpec((block, 128), lambda h, i: (i, 3 * (base + h))),
            specs(1),
            specs(2),
            pl.BlockSpec((1, block), lambda h, i: (0, i)),
            pl.BlockSpec((total, 1), lambda h, i: (0, 0)),
        ] + [ANY] * (len(kept) + len(waits)),
        out_specs=[
            pl.BlockSpec((block, 128), lambda h, i: (i, base + h)),
            pl.BlockSpec((None, 2, total, block), lambda h, i: (h, 0, 0, i)),
            pl.BlockSpec((None, 2, block), lambda h, i: (h, 0, i)),
        ],
        out_shape=[
            jax.ShapeDtypeStruct((total, qkv.shape[1] // 3), BF),
            jax.ShapeDtypeStruct((pairs, 2, total, total), BF),
            jax.ShapeDtypeStruct((pairs, 2, total), F32),
        ],
        scratch_shapes=[pltpu.VMEM((128, total), BF), pltpu.VMEM((2, 1), F32)],
        compiler_params=params(),
        cost_estimate=pl.CostEstimate(flops=pairs * 12 * 10**9, bytes_accessed=pairs << 24, transcendentals=0),
        input_output_aliases={5: 0} if kept else {},
        name="attend",
    )(qkv, qkv, qkv, seg_row, seg_col, *kept, *waits)


def attend_back_kernel(chunk, extra, q_ref, k_ref, v_ref, o_ref, do_ref, do2_ref, p_ref, l_ref, *rest):
    out_ref, mark_ref, kt_ref, dk_acc, dv_acc = rest[extra:]
    i = pl.program_id(1)
    total = k_ref.shape[0]
    block = q_ref.shape[0]

    @pl.when(i == 0)
    def _():
        kt_ref[...] = k_ref[...].T
        dk_acc[...] = jnp.zeros_like(dk_acc)
        dv_acc[...] = jnp.zeros_like(dv_acc)

    do = jnp.where(i < pl.num_programs(1) // 2, do_ref[...], do2_ref[...])
    q_parts = head_parts(q_ref[...])
    do_parts = head_parts(do)
    product = do.astype(F32) * o_ref[...].astype(F32)
    delta = jnp.sum(product.T.reshape(2, HD, block), axis=1)
    inverse = l_ref[...]
    grad_q = [jnp.zeros((HD, block), F32)] * 2
    for lo in range(0, total, chunk):
        rows = slice(lo, lo + chunk)
        values = v_ref[rows, :]
        for h in range(2):
            p = p_ref[h, rows, :].astype(F32) * inverse[h : h + 1]
            grad_p = mm(values, do_parts[h], NT)
            grad_s = (p * (grad_p - delta[h : h + 1])).astype(BF)
            dv_acc[rows, :] += mm(p.astype(BF), do_parts[h])
            dk_acc[rows, :] += mm(grad_s, q_parts[h])
            grad_q[h] = grad_q[h] + mm(kt_ref[h * HD : h * HD + HD, rows], grad_s)
    grad_q = jnp.concatenate(grad_q, axis=0).T.astype(BF)
    out_ref[pl.ds(pl.multiple_of(i * block, block), block), 0:128] = grad_q
    add_fold(mark_ref.at[0:8, :], i == 0, grad_q.astype(F32))

    @pl.when(i == pl.num_programs(1) - 1)
    def _():
        out_ref[:, 128:256] = dk_acc[...].astype(BF)
        grad_v = dv_acc[...].astype(BF)
        out_ref[:, 256:384] = grad_v
        mark_ref[8:16, :] = fold(grad_v.astype(F32))


def attend_back(qkv, out, grad_mine, grad_mate, probs, inverse, base, held=None, waits=(), block=256, chunk=1024):
    total = qkv.shape[0]
    kept = [] if held is None else [held]
    pairs, skip = 1, base % probs.shape[0]
    last = total // block // 2 - 1
    whole = lambda c: pl.BlockSpec((total, 128), lambda h, i: (0, 3 * (base + h) + c))
    rows = pl.BlockSpec((block, 128), lambda h, i: (i, base + h))
    return pl.pallas_call(
        functools.partial(attend_back_kernel, chunk, len(waits) + len(kept)),
        grid=(pairs, total // block),
        in_specs=[
            pl.BlockSpec((block, 128), lambda h, i: (i, 3 * (base + h))),
            whole(1),
            whole(2),
            rows,
            pl.BlockSpec((block, 128), lambda h, i: (jnp.minimum(i, last), base + h)),
            pl.BlockSpec((block, 128), lambda h, i: (jnp.maximum(i - last - 1, 0), base + h)),
            pl.BlockSpec((None, 2, total, block), lambda h, i: (skip + h, 0, 0, i)),
            pl.BlockSpec((None, 2, block), lambda h, i: (skip + h, 0, i)),
        ] + [ANY] * (len(kept) + len(waits)),
        out_specs=[pl.BlockSpec((total, 384), lambda h, i: (0, base + h)), pl.BlockSpec((16, 128), lambda h, i: (0, 0))],
        out_shape=[jax.ShapeDtypeStruct(qkv.shape, BF), jax.ShapeDtypeStruct((16, 128), F32)],
        scratch_shapes=[
            pltpu.VMEM((128, total), BF),
            pltpu.VMEM((total, 128), F32),
            pltpu.VMEM((total, 128), F32),
        ],
        compiler_params=params(),
        cost_estimate=pl.CostEstimate(flops=pairs * 21 * 10**9, bytes_accessed=pairs << 24, transcendentals=0),
        input_output_aliases={8: 0} if kept else {},
        name="attend_back",
    )(qkv, qkv, qkv, out, grad_mine, grad_mate, probs, inverse, *kept, *waits)


def gelu_parts(u):
    phi = 0.5 + 0.5 * lax.erf(u * 0.7071067811865476)
    return u * phi, phi + u * (jnp.exp(u * u * -0.5) * 0.3989422804014327)


def mean(value):
    return jnp.mean(value, axis=-1, keepdims=True)


def normed(hidden):
    centred = hidden - mean(hidden)
    inverse = lax.rsqrt(mean(centred * centred) + EPSILON)
    return centred * inverse, inverse


def norm_back(grad_in, scaled, inverse, gain):
    grad_scaled = grad_in * gain
    return inverse * (grad_scaled - mean(grad_scaled) - scaled * mean(grad_scaled * scaled))


def fold(value):
    return jnp.sum(value.reshape(value.shape[0] // 8, 8, value.shape[1]), axis=0)


def add_fold(ref, first, value):
    part = fold(value)

    @pl.when(first)
    def _():
        ref[...] = part

    @pl.when(jnp.logical_not(first))
    def _():
        ref[...] += part


def token_rows(x, span, block, at=lambda i: i):
    return pl.BlockSpec((block // span, span, x.shape[2]), lambda i: (at(i), 0, 0))


def qkv_kernel(xm_ref, xt_ref, w_ref, b_ref, out_ref):
    i = pl.program_id(0)
    x = jnp.where(i < pl.num_programs(0) // 2, xm_ref[...], xt_ref[...])
    out_ref[...] = (mm(x.reshape(out_ref.shape[0], -1), w_ref[...]) + b_ref[...]).astype(BF)


def project(x_mine, x_mate, span, weight, bias, block=256):
    steps = x_mine.shape[0] * span // block
    full = lambda a: pl.BlockSpec(a.shape, lambda i: (0, 0), pipeline_mode=pl.Buffered(1))
    width = weight.shape[1]
    return pl.pallas_call(
        qkv_kernel,
        grid=(2 * steps,),
        in_specs=[
            token_rows(x_mine, span, block, lambda i: jnp.minimum(i, steps - 1)),
            token_rows(x_mate, span, block, lambda i: jnp.maximum(i - steps, 0)),
            full(weight),
            full(bias),
        ],
        out_specs=pl.BlockSpec((block, width), lambda i: (i, 0)),
        out_shape=jax.ShapeDtypeStruct((2 * steps * block, width), BF),
        compiler_params=params(),
        cost_estimate=pl.CostEstimate(flops=7 * 10**9, bytes_accessed=14 << 20, transcendentals=0),
        name="project",
    )(x_mine, x_mate, weight, bias)


def mid_up_kernel(step, count, mates, order_ref, x_ref, om_ref, vec_ref, bu_ref, *refs):
    mate_refs, refs = refs[:mates], refs[mates:]
    pieces, (xh_ref, r_ref, xb_ref, g_ref, gp_ref, wo_ref, wu_ref, sems) = refs[:count], refs[count:]
    first = pl.program_id(0) == 0
    d, ff = wu_ref.shape
    shards = shards_of(pieces)

    def out_copies():
        return shard_copies(pieces, order_ref, slice(0, d), wo_ref, sems, 0, order_ref[shards])

    def up_copies():
        return shard_copies(pieces, order_ref, slice(d, d + ff), wu_ref, sems, shards)

    @pl.when(first)
    def _():
        for copy in out_copies() + up_copies():
            copy.start()
        for copy in out_copies():
            copy.wait()

    half = om_ref.shape[1]
    mixed = mm(om_ref[...], wo_ref[0:half, :])
    for ref in mate_refs:
        mixed = mixed + mm(ref[...], wo_ref[half : half + ref.shape[1], :])
        half += ref.shape[1]
    hidden = x_ref[...].reshape(mixed.shape).astype(F32) + mixed + vec_ref[0:1, :]
    scaled, inverse = normed(hidden)
    xh_ref[...] = scaled
    r_ref[...] = inverse
    xb = (scaled * vec_ref[1:2, :] + vec_ref[2:3, :]).astype(BF)
    xb_ref[...] = xb

    @pl.when(first)
    def _():
        for copy in up_copies():
            copy.wait()

    for lo in range(0, ff, step):
        cols = slice(lo, lo + step)
        g, gp = gelu_parts(mm(xb, wu_ref[:, cols]) + bu_ref[:, cols])
        g_ref[:, cols] = g.astype(BF)
        gp_ref[:, cols] = gp.astype(BF)


def mid_up(x, span, attn, o_mate, pieces, order, vecs, b_up, block=256, step=512):
    rows, d = x.shape[0] * span, x.shape[2]
    ff = b_up.shape[1]
    row = lambda n: pl.BlockSpec((block, n), lambda i: (i, 0))
    full = lambda a: pl.BlockSpec(a.shape, lambda i: (0, 0), pipeline_mode=pl.Buffered(1))
    return pl.pallas_call(
        functools.partial(mid_up_kernel, step, len(pieces), len(o_mate)),
        grid=(rows // block,),
        in_specs=[SMEM, token_rows(x, span, block), row(d // 2), full(vecs), full(b_up)]
        + [row(a.shape[1]) for a in o_mate]
        + [ANY] * len(pieces),
        out_specs=[row(d), row(1), row(d), row(ff), row(ff)],
        out_shape=[
            jax.ShapeDtypeStruct((rows, d), F32),
            jax.ShapeDtypeStruct((rows, 1), F32),
            jax.ShapeDtypeStruct((rows, d), BF),
            jax.ShapeDtypeStruct((rows, ff), BF),
            jax.ShapeDtypeStruct((rows, ff), BF),
        ],
        scratch_shapes=[
            pltpu.VMEM((d, d), BF),
            pltpu.VMEM((d, ff), BF),
            pltpu.SemaphoreType.DMA((2 * shards_of(pieces),)),
        ],
        compiler_params=params(),
        cost_estimate=pl.CostEstimate(flops=20 * 10**9, bytes_accessed=36 << 20, transcendentals=0),
        name="mid_up",
    )(order, x, attn, vecs, b_up, *o_mate, *pieces)


def mid_down_kernel(step, count, blocks, order_ref, g_ref, gp_ref, xh_ref, dy_ref, vec_ref, *refs):
    pieces, (out_ref, dh_ref, dm_ref, du_ref, s_ref, su_ref, wd_ref, sems) = refs[:count], refs[count:]
    first = pl.program_id(0) == 0
    d = wd_ref.shape[1]

    @pl.when(first)
    def _():
        copies = []
        for n in range(blocks[1]):
            cols = slice(blocks[0] + n * d, blocks[0] + (n + 1) * d)
            copies += shard_copies(pieces, order_ref, cols, wd_ref, sems, len(copies), None, blocks[1], n)
        for copy in copies:
            copy.start()
        for copy in copies:
            copy.wait()

    x1 = xh_ref[...] * vec_ref[1:2, :] + vec_ref[2:3, :]
    hidden = x1 + mm(g_ref[...], wd_ref[...]) + vec_ref[3:4, :]
    scaled, inverse = normed(hidden)
    gain = vec_ref[4:5, :]
    out_ref[...] = (scaled * gain + vec_ref[5:6, :]).astype(BF)
    dy = dy_ref[...].astype(F32)
    dh = norm_back(dy, scaled, inverse, gain)
    dm = dh.astype(BF)
    dh_ref[...] = dh
    dm_ref[...] = dm
    add_fold(s_ref.at[0:8, :], first, dy * scaled)
    add_fold(s_ref.at[8:16, :], first, dy)
    add_fold(s_ref.at[16:24, :], first, dm.astype(F32))
    for lo in range(0, wd_ref.shape[0], step):
        cols = slice(lo, lo + step)
        du = (mm(dm, wd_ref[cols, :], NT) * gp_ref[:, cols].astype(F32)).astype(BF)
        du_ref[:, cols] = du
        add_fold(su_ref.at[:, cols], first, du.astype(F32))


def mid_down(g, gp, xh, dy, pieces, order, blocks, vecs, block=256, step=2048):
    rows, d = xh.shape
    ff = g.shape[1]
    row = lambda n: pl.BlockSpec((block, n), lambda i: (i, 0))
    full = lambda a: pl.BlockSpec(a.shape, lambda i: (0, 0), pipeline_mode=pl.Buffered(1))
    keep = lambda r, n: pl.BlockSpec((r, n), lambda i: (0, 0))
    return pl.pallas_call(
        functools.partial(mid_down_kernel, step, len(pieces), blocks),
        grid=(rows // block,),
        in_specs=[SMEM, row(ff), row(ff), row(d), row(d), full(vecs)] + [ANY] * len(pieces),
        out_specs=[row(d), row(d), row(d), row(ff), keep(24, d), keep(8, ff)],
        out_shape=[
            jax.ShapeDtypeStruct((rows, d), BF),
            jax.ShapeDtypeStruct((rows, d), F32),
            jax.ShapeDtypeStruct((rows, d), BF),
            jax.ShapeDtypeStruct((rows, ff), BF),
            jax.ShapeDtypeStruct((24, d), F32),
            jax.ShapeDtypeStruct((8, ff), F32),
        ],
        scratch_shapes=[pltpu.VMEM((ff, d), BF), pltpu.SemaphoreType.DMA((shards_of(pieces) * blocks[1],))],
        compiler_params=params(),
        cost_estimate=pl.CostEstimate(flops=25 * 10**9, bytes_accessed=44 << 20, transcendentals=0),
        name="mid_down",
    )(order, g, gp, xh, dy, vecs, *pieces)


def mid_back_kernel(count, order_ref, dh_ref, du_ref, xh_ref, r_ref, vec_ref, *refs):
    pieces, (dh1_ref, da_ref, dom_ref, dot_ref, s_ref, wu_ref, wo_ref, sems) = refs[:count], refs[count:]
    first = pl.program_id(0) == 0
    d, ff = wu_ref.shape
    half = dom_ref.shape[1]
    shards = shards_of(pieces)

    @pl.when(first)
    def _():
        copies = shard_copies(pieces, order_ref, slice(d, d + ff), wu_ref, sems, shards)
        copies += shard_copies(pieces, order_ref, slice(0, d), wo_ref, sems, 0, order_ref[shards])
        for copy in copies:
            copy.start()
        for copy in copies:
            copy.wait()

    dx = dh_ref[...] + mm(du_ref[...], wu_ref[...], NT)
    scaled = xh_ref[...]
    dh1 = norm_back(dx, scaled, r_ref[...], vec_ref[1:2, :])
    dh1_ref[...] = dh1
    da = dh1.astype(BF)
    da_ref[...] = da
    dom_ref[...] = mm(da, wo_ref[0:half, :], NT).astype(BF)
    dot_ref[...] = mm(da, wo_ref[half:, :], NT).astype(BF)
    add_fold(s_ref.at[0:8, :], first, dx * scaled)
    add_fold(s_ref.at[8:16, :], first, dx)
    add_fold(s_ref.at[16:24, :], first, da.astype(F32))


def mid_back(dh, du, xh, r, pieces, order, vecs, block=256):
    rows, d = dh.shape
    ff = du.shape[1]
    row = lambda n: pl.BlockSpec((block, n), lambda i: (i, 0))
    full = lambda a: pl.BlockSpec(a.shape, lambda i: (0, 0), pipeline_mode=pl.Buffered(1))
    return pl.pallas_call(
        functools.partial(mid_back_kernel, len(pieces)),
        grid=(rows // block,),
        in_specs=[SMEM, row(d), row(ff), row(d), row(1), full(vecs)] + [ANY] * len(pieces),
        out_specs=[row(d), row(d), row(d // 2), row(d // 2), pl.BlockSpec((24, d), lambda i: (0, 0))],
        out_shape=[
            jax.ShapeDtypeStruct((rows, d), F32),
            jax.ShapeDtypeStruct((rows, d), BF),
            jax.ShapeDtypeStruct((rows, d // 2), BF),
            jax.ShapeDtypeStruct((rows, d // 2), BF),
            jax.ShapeDtypeStruct((24, d), F32),
        ],
        scratch_shapes=[
            pltpu.VMEM((d, ff), BF),
            pltpu.VMEM((d, d), BF),
            pltpu.SemaphoreType.DMA((2 * shards_of(pieces),)),
        ],
        compiler_params=params(),
        cost_estimate=pl.CostEstimate(flops=15 * 10**9, bytes_accessed=36 << 20, transcendentals=0),
        name="mid_back",
    )(order, dh, du, xh, r, vecs, *pieces)


def token_kernel(split, waits, chip_ref, grad_ref, w_ref, *refs):
    outs = refs[len(refs) - split :]
    total = mm(grad_ref[...], w_ref[...], NT)
    for ref in refs[: len(refs) - split - waits]:
        total = total + ref[...].astype(F32)
    total = total.astype(BF)
    if split == 1:
        outs[0][...] = total
        return
    for n in range(split):

        @pl.when(pl.program_id(0) == n)
        def _():
            outs[n][...] = total


def token_grad(grads, weight, shift, adds, chip, chips, split, waits=()):
    d = weight.shape[0]
    rows = grads.shape[0] // 2
    block = rows // chips
    base = shift * chips
    at = lambda i, c: c[0] ^ i if split else i
    plain = lambda a: pl.BlockSpec((block, a.shape[1]), lambda i, c: (at(i, c), 0))
    if split:
        out_specs = [pl.BlockSpec((block, d), lambda i, c: (0, 0))] * chips
        out_shape = [jax.ShapeDtypeStruct((block, d), BF)] * chips
    else:
        out_specs = [pl.BlockSpec((block, d), lambda i, c: (i, 0))]
        out_shape = [jax.ShapeDtypeStruct((rows, d), BF)]
    return pl.pallas_call(
        functools.partial(token_kernel, len(out_shape), len(waits)),
        grid_spec=pltpu.PrefetchScalarGridSpec(
            num_scalar_prefetch=1,
            grid=(chips,),
            in_specs=[
                pl.BlockSpec((block, grads.shape[1]), lambda i, c: (base + at(i, c), 0)),
                pl.BlockSpec(weight.shape, lambda i, c: (0, 0), pipeline_mode=pl.Buffered(1)),
            ]
            + [plain(a) for a in adds]
            + [ANY] * len(waits),
            out_specs=out_specs,
        ),
        out_shape=out_shape,
        compiler_params=params(),
        cost_estimate=pl.CostEstimate(flops=10**8, bytes_accessed=1 << 16, transcendentals=0),
        name="token_grad",
    )(jnp.reshape(chip, (1,)).astype(jnp.int32), grads, weight, *adds, *waits)


def order_kernel(chip_ref, *refs):
    pieces, (out_ref, sems) = refs[:-2], refs[-2:]
    copies = [
        pltpu.make_async_copy(piece, out_ref.at[chip_ref[0] ^ n], sems.at[n]) for n, piece in enumerate(pieces)
    ]
    for copy in copies:
        copy.start()
    for copy in copies:
        copy.wait()


def in_order(pieces, chip):
    chips = len(pieces)
    return pl.pallas_call(
        order_kernel,
        in_specs=[SMEM] + [ANY] * chips,
        out_shape=jax.ShapeDtypeStruct((chips,) + pieces[0].shape, BF),
        scratch_shapes=[pltpu.SemaphoreType.DMA((chips,))],
        compiler_params=params(),
        name="in_order",
    )(jnp.reshape(chip, (1,)).astype(jnp.int32), *pieces)


def by_chip(value, out_ref, lo):
    chips, dps, rows, _ = out_ref.shape
    value = value.reshape(dps, chips, rows, value.shape[1])
    for n in range(dps):
        out_ref[:, n, :, lo : lo + value.shape[3]] = value[n].astype(BF)


def proj_kernel(xm_ref, xt_ref, grad_ref, *refs):
    out_ref = refs[-1]
    own = grad_ref.shape[0] // 2
    xm = xm_ref[...].reshape(own, -1)
    xt = xt_ref[...].reshape(own, -1)
    by_chip(mm(xm, grad_ref[0:own, :], TN) + mm(xt, grad_ref[own:, :], TN), out_ref, 0)
    if grad_ref.shape[1] < out_ref.shape[3]:
        out_ref[:, :, :, grad_ref.shape[1] :] = refs[0][...]


def dp_steps(groups, least):
    return max(1, min(groups, least // 128))


def shard_specs(steps, groups, chips, rows, cols):
    spec = pl.BlockSpec((chips, groups // steps, rows, cols), lambda i, *_: (0, i, 0, 0))
    return spec, jax.ShapeDtypeStruct((chips, groups, rows, cols), BF)


def proj_grad(x_mine, x_mate, span, grads, first, pairs, groups, chips, waits=(), extra=None):
    own, d = x_mine.shape[0] * span, x_mine.shape[2]
    width = 384 * pairs
    more = [] if extra is None else [extra]
    steps = dp_steps(groups, d)
    col = pl.BlockSpec((x_mine.shape[0], span, d // steps), lambda i: (0, 0, i))
    rows = d // groups // chips
    spec, shape = shard_specs(steps, groups, chips, rows, width + sum(a.shape[3] for a in more))
    return pl.pallas_call(
        proj_kernel,
        grid=(steps,),
        in_specs=[col, col]
        + [pl.BlockSpec((2 * own, width), lambda i: (0, first // pairs), pipeline_mode=pl.Buffered(1))]
        + [shard_specs(steps, groups, chips, rows, a.shape[3])[0] for a in more]
        + [ANY] * len(waits),
        out_specs=spec,
        out_shape=shape,
        compiler_params=params(),
        cost_estimate=pl.CostEstimate(flops=10**8, bytes_accessed=1 << 16, transcendentals=0),
        name="proj_grad",
    )(x_mine, x_mate, grads, *more, *waits)


def weight_kernel(adds, waits, turn_ref, *refs):
    out_ref, refs = refs[-1], refs[: len(refs) - 1 - waits]
    count = (len(refs) - adds) // 2
    more = refs[2 * count :]
    lo = 0
    for n in range(count):
        value = mm(refs[2 * n][...], refs[2 * n + 1][...], TN)
        width = value.shape[1]
        chips, dps, rows, _ = out_ref.shape
        value = value.reshape(dps, chips, rows, width)
        for k in range(dps):
            part = value[k]
            if more:
                part = part + more[0][:, k, :, lo : lo + width].astype(F32)
            out_ref[:, k, :, lo : lo + width] = part.astype(BF)
        lo += width
    if lo < out_ref.shape[3]:
        out_ref[:, :, :, lo:] = more[-1][...]


def weight_grad(sides, turns, groups, chips, adds=(), waits=()):
    in_specs, args = [], []
    steps = dp_steps(groups, min(left.shape[1] for left, _ in sides))
    rows_of = lambda a: a.shape[1] // steps
    for n, (left, right) in enumerate(sides):
        tokens = left.shape[0]
        in_specs.append(
            pl.BlockSpec((tokens, rows_of(left)), lambda i, t, n=n: (0, lax.rem(i + t[1 + n] * (steps // 2), steps)))
        )
        in_specs.append(
            pl.BlockSpec((tokens, right.shape[1] // 2), lambda i, t: (0, t[0]), pipeline_mode=pl.Buffered(1))
        )
        args += [left, right]
    rows = sides[0][0].shape[1] // groups // chips
    cols = sum(right.shape[1] // 2 for _, right in sides)
    if len(adds) > 1:
        cols += adds[1].shape[3]
    in_specs += [shard_specs(steps, groups, chips, rows, a.shape[3])[0] for a in adds] + [ANY] * len(waits)
    spec, shape = shard_specs(steps, groups, chips, rows, cols)
    flops = sum(a.shape[0] * a.shape[1] * b.shape[1] for a, b in sides)
    return pl.pallas_call(
        functools.partial(weight_kernel, len(adds), len(waits)),
        grid_spec=pltpu.PrefetchScalarGridSpec(
            num_scalar_prefetch=1, grid=(steps,), in_specs=in_specs, out_specs=spec
        ),
        out_shape=shape,
        compiler_params=params(),
        cost_estimate=pl.CostEstimate(flops=flops, bytes_accessed=20 << 20, transcendentals=0),
        name="weight_grad",
    )(turns, *args, *adds, *waits)


def swap(value, mask):
    count = lax.axis_size("ctx")
    return lax.ppermute(value, "ctx", [(d, d ^ mask) for d in range(count)])


def along(value, step):
    count = lax.axis_size("dp")
    return lax.ppermute(value, "dp", [(s, (s + step) % count) for s in range(count)])


def pick(value, index, axis=0):
    return lax.dynamic_index_in_dim(value, index, axis, keepdims=False)


def over_chips(value):
    count = lax.axis_size("ctx")
    groups = [list(range(core, count, 2)) for core in range(2)]
    return lax.all_to_all(value, "ctx", 0, 0, axis_index_groups=groups)


def repeat(value):
    return jnp.broadcast_to(value[None], (lax.axis_size("ctx") // 2,) + value.shape)


def tick(value):
    return (value[(0,) * value.ndim].astype(F32) > 1e30).astype(jnp.int32)


def tie_kernel(*refs):
    pass


def tie(value, *waits):
    return pl.pallas_call(
        tie_kernel,
        in_specs=[ANY] * (1 + len(waits)),
        out_specs=ANY,
        out_shape=jax.ShapeDtypeStruct(value.shape, value.dtype),
        input_output_aliases={0: 0},
        name="tie",
    )(value, *waits)


class Gather:
    def __init__(self, own, place):
        self.place = place
        self.groups = lax.axis_size("dp")
        self.chips = lax.axis_size("ctx") // 2
        self.own = own
        self.whole = own.shape[0] % TILE != 0

    def along_dp(self, value):
        if self.whole:
            return []
        self.turns = [value] + [along(value, s) for s in range(1, self.groups)]
        return self.turns[1:]

    def over_chips(self, later):
        if self.whole:
            return []
        self.held = over_chips(repeat(jnp.stack(self.turns) + later.astype(BF)))
        return [self.held]

    def plane(self):
        if self.whole:
            return []
        got = [swap(self.own, 2 * r) for r in range(1, self.chips)]
        self.held = jnp.stack([self.own] + got)
        return got

    def dp_arrays(self):
        self.held = self.turns
        return self.turns

    def between_cores(self, *waits):
        me, chip, core = self.place
        if self.whole:
            return [lax.all_gather(self.own, BOTH, axis=0, tiled=True)[None]], jnp.zeros((1,), jnp.int32)
        count = 2 * self.chips
        turn = (me - jnp.arange(self.groups)) % self.groups * count
        chip_of = jnp.arange(self.chips)
        if isinstance(self.held, list):
            pieces, order = [], []
            for n, value in enumerate(self.held):
                value = tie(value, *waits) if waits else value
                pieces += [value, swap(value, 1)]
                order += [turn[n] + 2 * (chip_of ^ chip) + core, turn[n] + 2 * (chip_of ^ chip) + 1 - core]
        else:
            flat = self.held.reshape((-1,) + self.own.shape)
            flat = tie(flat, *waits) if waits else flat
            pieces = [flat, swap(flat, 1)]
            numbers = (turn[None] + 2 * chip_of[:, None]).reshape(-1)
            order = [numbers + core, numbers + 1 - core]
        return pieces, jnp.concatenate(order).astype(jnp.int32)


class Reduce:
    def __init__(self, grad, place, direct=False):
        self.place = place
        self.groups = grad.shape[1]
        if direct:
            chip = place[1]
            sent = [pick(grad, chip ^ r) for r in range(1, grad.shape[0])]
            self.got = [pick(grad, chip)] + [swap(v, 2 * (r + 1)) for r, v in enumerate(sent)]
        else:
            self.got = over_chips(grad)

    def chip_sum(self, *waits):
        if isinstance(self.got, list):
            last = tie(self.got[-1], *self.got[1:-1], *waits)
            self.part = sum(v.astype(F32) for v in self.got[:-1] + [last]).astype(BF)
        else:
            self.part = jnp.sum(tie(self.got, *waits).astype(F32), axis=0).astype(BF)
        return [self.part]

    def along_dp(self):
        me = self.place[0]
        sent = [pick(self.part, (me + step) % self.groups) for step in range(1, self.groups)]
        self.turns = [pick(self.part, me)] + [along(v, n + 1) for n, v in enumerate(sent)]

    def dp_sum(self, *waits):
        last = tie(self.turns[-1], *self.turns[1:-1], *waits)
        total = sum(v.astype(F32) for v in self.turns[:-1] + [last]).astype(BF)
        self.total = total.reshape(2, -1, total.shape[1])
        return [self.total]

    def finish(self):
        core = self.place[2]
        mine = pick(self.total, core).astype(F32)
        other = swap(pick(self.total, 1 - core), 1).astype(F32)
        return [jnp.where(core == 0, mine, other), jnp.where(core == 0, other, mine)], mine + other


def half_cols(value, which):
    width = value.shape[-1] // 2
    return lax.dynamic_slice_in_dim(value, which * width, width, value.ndim - 1)


def spread(vectors, shards, rows):
    flat = jnp.concatenate([v.reshape(shards, -1) for v in vectors], axis=1)
    return jnp.pad(flat, ((0, 0), (0, rows * 128 - flat.shape[1]))).reshape(shards, rows, 128)


def fold_rows(sums):
    return jnp.sum(sums.reshape(-1, 8, sums.shape[1]), axis=1)


def local(
    tokens, segments, cotangent, w_query, w_key, w_value, w_out, w_up, w_down,
    b_query, b_value, b_out, b_up, b_down, gain_attn, shift_attn, gain_mlp, shift_mlp,
):
    seqs, span, d = tokens.shape
    count = lax.axis_size("ctx")
    groups = lax.axis_size("dp")
    chips = count // 2
    ctx = lax.axis_index("ctx")
    chip, core = ctx // 2, ctx % 2
    place_of = (lax.axis_index("dp"), chip, core)
    ff = w_up.shape[1]
    half = d // 2
    shards = groups * count
    rows = d // shards
    width = d // shards
    pairs = half // 128
    bf = lambda v: v.astype(BF)

    vec_names = (b_query, b_value, b_out, gain_attn, shift_attn, b_down, gain_mlp, shift_mlp)
    vec_size = 8 * width + ff // shards
    extra = -(-(vec_size + seqs * span) // (rows * 128)) * 128
    vec_pack = jnp.concatenate([bf(v) for v in vec_names] + [bf(b_up), bf(segments.reshape(-1))])
    vec_pack = jnp.pad(vec_pack, (0, rows * extra - vec_pack.shape[0])).reshape(rows, extra)
    packed = pack(w_query, w_key, w_value, w_out, w_up, w_down, vec_pack)

    got = over_chips(tokens)
    own = chips * span
    proj = Gather(packed[0], place_of)
    turns_of = proj.along_dp(proj.own)
    got = tie(got, *turns_of)
    mate = swap(got, 1)
    later = tick(got)
    held = proj.over_chips(later)
    pieces, order = proj.between_cores()
    def everywhere(value):
        return lax.all_gather(tie(value, got), BOTH, axis=0, tiled=True).reshape(2, -1, value.shape[1])

    up_pieces = [everywhere(packed[1])]
    if rows % TILE == 0:
        down_pieces, blocks = [up_pieces[0].reshape(shards, rows, -1)], (d + ff, w_down.shape[0] // rows)
    else:
        down_pieces, blocks = [everywhere(packed[2])], (0, 1)
    down_order = jnp.arange(down_pieces[0].shape[0], dtype=jnp.int32)
    if proj.whole:
        w_cat = half_cols(pieces[0][0, :, : 3 * d], core)
        vec_block = pieces[0][0, :, 3 * d :]
    else:
        w_cat, vec_block = place(pieces, jnp.append(order, core * 3 * half), 3 * half)
    packed = vec_block.reshape(shards, rows * extra)
    vec_all = packed[:, :vec_size].astype(F32)
    seg_all = packed[:, vec_size : vec_size + seqs * span].reshape(groups, chips, 2, seqs, span)
    seg_own = pick(pick(seg_all, place_of[0]), chip, 2)
    seg = jnp.concatenate([pick(seg_own, core, 1), pick(seg_own, 1 - core, 1)]).reshape(-1).astype(jnp.int32)
    vec = [vec_all[:, n * width : (n + 1) * width].reshape(1, d) for n in range(8)]
    bias_up = vec_all[:, 8 * width : 8 * width + ff // shards].reshape(1, ff)
    vecs = jnp.concatenate(vec[2:] + [jnp.zeros((2, d), F32)], axis=0)
    bias_by_pair = [v.reshape(1, 2 * pairs, 1, 128) for v in (vec[0] * QSCALE, jnp.zeros((1, d), F32), vec[1])]
    bias_cat = half_cols(jnp.concatenate(bias_by_pair, axis=2).reshape(1, 3 * d), core)

    qkv = project(got, mate, span, w_cat, bias_cat)
    seg_row, seg_col = seg.reshape(1, -1), seg.reshape(-1, 1)

    attn, probs, inverse, o_mate = None, [], [], []
    for n in range(0, pairs, 2):
        attn, p, l = attend(qkv, seg_row, seg_col, n, 2, attn)
        probs.append(p)
        inverse.append(l)
        o_mate.append(swap(attn[own:, n * 128 : (n + 2) * 128], 1))
    dy = over_chips(cotangent + tick(inverse[0]).astype(BF)).reshape(own, d)
    up_order = jnp.stack([jnp.zeros((), jnp.int32), jnp.ones((), jnp.int32), d - core * half]).astype(jnp.int32)
    xh, r, xb, g, gp = mid_up(got, span, attn, o_mate, up_pieces, up_order, vecs, bias_up)
    out, dh2, dm, du, sums_two, sums_up = mid_down(g, gp, xh, dy, down_pieces, down_order, blocks, vecs)
    result_out = over_chips(out.reshape(chips, span, d))

    zero = jnp.zeros((), jnp.int32)
    turns = lambda half_of, *more: jnp.stack([half_of, *more]).astype(jnp.int32)
    got_down = swap(weight_grad([(g, dm)], turns(1 - core, zero), groups, chips), 1)
    dh1, da, do_mine, do_send, sums_one = mid_back(dh2, du, xh, r, up_pieces, up_order, vecs)
    do_mate = swap(do_send, 1)
    kept_down = weight_grad([(g, dm)], turns(core, zero), groups, chips, [got_down], [result_out])
    sum_down = Reduce(kept_down, place_of)

    o_both = jnp.concatenate([attn[:own]] + o_mate, axis=1)
    sides, shift = [(xb, du), (o_both, da)], core
    got_up = swap(weight_grad(sides, turns(1 - core, zero, shift), groups, chips, (), [kept_down]), 1)
    two, one = fold_rows(sums_two), fold_rows(sums_one)
    per_shard = lambda v: jnp.moveaxis(bf(v).reshape(groups, chips, -1, 128), 1, 0)
    vec_grads = per_shard(spread([one[2], one[0], one[1], two[2], two[0], two[1], fold_rows(sums_up)], shards, rows))

    grads, waits, marks = None, [], []
    for n in range(pairs):
        grads, mark = attend_back(qkv, attn, do_mine, do_mate, probs[n // 2], inverse[n // 2], n, grads, waits)
        waits = []
        marks.append(mark)
        if n == 0:
            got_up = tie(got_up, mark)
            kept_up = weight_grad(sides, turns(core, zero, shift), groups, chips, [got_up, vec_grads])
            waits = sum_down.chip_sum(mark, kept_up)
            sum_down.along_dp()
            sum_up = Reduce(kept_up, place_of)
        elif n == 1:
            waits = sum_down.dp_sum(mark)
        elif n == 2:
            first = proj_grad(got, mate, span, grads, 0, 3, groups, chips)
            waits = sum_up.chip_sum(mark, first)
            sum_up.along_dp()
            sum_first = Reduce(tie(first, sum_up.part), place_of)
    grads = tie(grads, tie(sum_first.got, mark), *[tie(v, mark) for v in sum_up.turns[1:]])
    bias_sums = jnp.stack([fold_rows(v) for v in marks])
    blank = jnp.zeros((half,), F32)

    def whole_vector(c):
        part = bias_sums[:, c].reshape(-1)
        return jnp.where(core == 0, jnp.concatenate([part, blank]), jnp.concatenate([blank, part]))

    bias_grads = per_shard(spread([whole_vector(0), whole_vector(1)], shards, rows))
    token_send = token_grad(grads, w_cat, 1, (), chip, chips, False)[0]
    token_got = swap(token_send, 1)
    last = proj_grad(got, mate, span, grads, 3, 1, groups, chips, [token_send], bias_grads)
    sum_last = Reduce(last, place_of, True)
    grad_mine = token_grad(grads, w_cat, 0, (dh1, token_got), chip, chips, False, [last])[0]
    arrived = sum_last.got[1:]
    grad_mine = tie(grad_mine, *arrived)
    sum_last.chip_sum()
    sum_first.chip_sum(*arrived)
    sum_up.dp_sum(*arrived)
    grad_tokens = over_chips(grad_mine.reshape(chips, span, d))
    sum_last.part = jnp.concatenate([sum_first.part, sum_last.part], axis=2)
    sum_last.along_dp()
    sum_last.dp_sum(grad_tokens)
    sum_up.total = jnp.concatenate([sum_up.total, sum_last.total], axis=2)

    halves, _ = sum_down.finish()
    grad_down = jnp.concatenate(halves, axis=1)
    halves, both = sum_up.finish()
    cuts = [0, ff // 2, half, 128, 3 * half - 384, 384, 128]
    cuts = [sum(cuts[: n + 1]) for n in range(len(cuts))]
    cut = lambda v, n: v[:, cuts[n] : cuts[n + 1]]
    grad_up = jnp.concatenate([cut(v, 0) for v in halves], axis=1)
    grad_out = jnp.concatenate([cut(v, 1) for v in halves], axis=1)
    small = cut(both, 2).reshape(-1)
    g_bo, g_ga, g_sa, g_bd, g_gm, g_sm = [small[n * width : (n + 1) * width] for n in range(6)]
    g_bu = small[6 * width : 6 * width + ff // shards]
    small = cut(both, 5).reshape(-1)
    g_bq, g_bv = small[:width] * QSCALE, small[width : 2 * width]
    joined = jnp.concatenate([v.reshape(rows, -1, 3, 128) for h in halves for v in (cut(h, 3), cut(h, 4))], axis=1)
    grad_query, grad_key, grad_value = [joined[:, :, c].reshape(rows, d) for c in range(3)]
    return (
        result_out, grad_tokens, grad_query * QSCALE, grad_key, grad_value, grad_out, grad_up, grad_down,
        g_bq, g_bv, g_bo, g_bu, g_bd, g_ga, g_sa, g_gm, g_sm,
    )


def solution(mesh):
    act, flat, mat, vec = P("dp", "ctx", None), P("dp", "ctx"), P(BOTH, None), P(BOTH)
    return jax.shard_map(
        local,
        mesh=mesh,
        in_specs=(act, flat, act) + (mat,) * 6 + (vec,) * 9,
        out_specs=(act, act) + (mat,) * 6 + (vec,) * 9,
        check_vma=False,
    )
```

```python
import functools

import jax
import jax.numpy as jnp
from jax import lax
from jax.experimental import pallas as pl
from jax.experimental.pallas import tpu as pltpu
from jax.sharding import PartitionSpec as P

HD = 64
MASKED = -1e30
EPSILON = 1e-05
QSCALE = 0.125
BF = jnp.bfloat16
F32 = jnp.float32
NT = (((1,), (1,)), ((), ()))
NN = (((1,), (0,)), ((), ()))
TN = (((0,), (0,)), ((), ()))
VMEM_LIMIT = 56 << 20
BOTH = ("dp", "ctx")
ANY = pl.BlockSpec(memory_space=pl.ANY)
SMEM = pl.BlockSpec(memory_space=pltpu.SMEM)
TILE = 16


def mm(a, b, dims=NN):
    return lax.dot_general(a, b, dims, preferred_element_type=F32)


def params():
    return pltpu.CompilerParams(vmem_limit_bytes=VMEM_LIMIT)


def shard_copies(refs, order_ref, cols, target, sems, base=0, turn=None, every=1, skip=0):
    copies = []
    total = target.shape[0]
    for ref in refs:
        rows = ref.shape[1]
        for n in range(ref.shape[0]):
            index = len(copies)
            row = (order_ref[index] * every + skip) * rows
            if turn is not None:
                row = lax.rem(row + turn, total)
            row = pl.multiple_of(row, TILE)
            copies.append(pltpu.make_async_copy(ref.at[n, :, cols], target.at[pl.ds(row, rows), :], sems.at[base + index]))
    return copies


def shards_of(pieces):
    return sum(piece.shape[0] for piece in pieces)


def pack_kernel(wq_ref, wk_ref, wv_ref, wo_ref, wu_ref, wd_ref, vec_ref, proj_ref, up_ref, *down):
    rows, d = wq_ref.shape
    ff = wu_ref.shape[1]
    for n, (ref, scale) in enumerate(((wq_ref, QSCALE), (wk_ref, None), (wv_ref, None))):
        for pair in range(d // 128):
            part = ref[:, pair * 128 : (pair + 1) * 128]
            part = part if scale is None else part * scale
            proj_ref[:, pair * 384 + n * 128 : pair * 384 + (n + 1) * 128] = part.astype(BF)
    proj_ref[:, 3 * d :] = vec_ref[...]
    up_ref[:, 0:d] = wo_ref[...].astype(BF)
    up_ref[:, d : d + ff] = wu_ref[...].astype(BF)
    if down:
        down[0][...] = wd_ref[...].astype(BF)
    else:
        for n in range(wd_ref.shape[0] // rows):
            up_ref[:, d + ff + n * d : d + ff + (n + 1) * d] = wd_ref[n * rows : (n + 1) * rows, :].astype(BF)


def pack(w_query, w_key, w_value, w_out, w_up, w_down, vec):
    rows, d = w_query.shape
    ff = w_up.shape[1]
    joined = rows % TILE == 0
    more = w_down.shape[0] // rows * d if joined else 0
    shapes = [(rows, 3 * d + vec.shape[1]), (rows, d + ff + more)] + ([] if joined else [w_down.shape])
    return pl.pallas_call(
        pack_kernel,
        out_shape=[jax.ShapeDtypeStruct(shape, BF) for shape in shapes],
        compiler_params=params(),
        name="pack",
    )(w_query, w_key, w_value, w_out, w_up, w_down, vec)


def place_kernel(count, first, order_ref, *refs):
    refs, (vec_ref, sems) = refs[:count], refs[count:]
    copies = shard_copies(refs, order_ref, slice(first, refs[0].shape[2]), vec_ref, sems)
    for copy in copies:
        copy.start()
    for copy in copies:
        copy.wait()


def place(pieces, order, first):
    rows = shards_of(pieces) * pieces[0].shape[1]
    return pl.pallas_call(
        functools.partial(place_kernel, len(pieces), first),
        in_specs=[SMEM] + [ANY] * len(pieces),
        out_shape=jax.ShapeDtypeStruct((rows, pieces[0].shape[2] - first), BF),
        scratch_shapes=[pltpu.SemaphoreType.DMA((shards_of(pieces),))],
        compiler_params=params(),
        name="place",
    )(order, *pieces)


def load_heads(pieces, order_ref, w_ref, sems):
    @pl.when(pl.program_id(0) == 0)
    def _():
        first = pl.multiple_of(order_ref[shards_of(pieces)], 128)
        copies = shard_copies(pieces, order_ref, pl.ds(first, w_ref.shape[1]), w_ref, sems)
        for copy in copies:
            copy.start()
        for copy in copies:
            copy.wait()


def head_parts(block):
    lane = lax.broadcasted_iota(jnp.int32, block.shape, 1)
    zero = jnp.zeros_like(block)
    return [jnp.where(lane < HD, block, zero), jnp.where(lane < HD, zero, block)]


def attend_kernel(chunk, extra, q_ref, k_ref, v_ref, sq_ref, sk_ref, *rest):
    o_ref, p_ref, l_ref, vt_ref, kn_ref = rest[extra:]
    i = pl.program_id(1)
    total = k_ref.shape[0]
    block = q_ref.shape[0]

    @pl.when(i == 0)
    def _():
        vt_ref[...] = v_ref[...].T
        keys = k_ref[...].astype(F32)
        norms = jnp.sum((keys * keys).T.reshape(2, HD, total), axis=1)
        kn_ref[...] = jnp.sqrt(jnp.max(norms, axis=1, keepdims=True))

    q = q_ref[...]
    parts = head_parts(q)
    q32 = q.astype(F32)
    qn = jnp.sqrt(jnp.sum((q32 * q32).T.reshape(2, HD, block), axis=1))
    bound = qn * kn_ref[...]
    seg_q = sq_ref[...]
    ones = jnp.ones((16, chunk), BF)

    def scores(h, lo):
        s = mm(k_ref[lo : lo + chunk, :], parts[h], NT)
        return jnp.where(sk_ref[lo : lo + chunk, :] == seg_q, s, MASKED)

    def finish(shift):
        acc = [jnp.zeros((HD + 16, block), F32)] * 2
        for lo in range(0, total, chunk):
            for h in range(2):
                p = jnp.exp(scores(h, lo) - shift[h : h + 1]).astype(BF)
                p_ref[h, lo : lo + chunk, :] = p
                left = jnp.concatenate([vt_ref[h * HD : h * HD + HD, lo : lo + chunk], ones], axis=0)
                acc[h] = acc[h] + mm(left, p)
        sums = [acc[h][HD : HD + 1] for h in range(2)]
        out = jnp.concatenate([acc[h][:HD] / sums[h] for h in range(2)], axis=0)
        o_ref[...] = out.T.astype(BF)
        sums = jnp.concatenate(sums, axis=0)
        l_ref[...] = 1.0 / sums
        return sums

    sums = finish(bound)
    good = jnp.min(sums) > 1e-20

    @pl.when(jnp.logical_not(good))
    def _():
        most = [jnp.full((1, block), MASKED, F32)] * 2
        for lo in range(0, total, chunk):
            for h in range(2):
                most[h] = jnp.maximum(most[h], jnp.max(scores(h, lo), axis=0, keepdims=True))
        finish(jnp.concatenate(most, axis=0))


def attend(qkv, seg_row, seg_col, base, pairs, held=None, waits=(), block=512, chunk=1024):
    total = qkv.shape[0]
    specs = lambda c: pl.BlockSpec((total, 128), lambda h, i: (0, 3 * (base + h) + c))
    kept = [] if held is None else [held]
    return pl.pallas_call(
        functools.partial(attend_kernel, chunk, len(waits) + len(kept)),
        grid=(pairs, total // block),
        in_specs=[
            pl.BlockSpec((block, 128), lambda h, i: (i, 3 * (base + h))),
            specs(1),
            specs(2),
            pl.BlockSpec((1, block), lambda h, i: (0, i)),
            pl.BlockSpec((total, 1), lambda h, i: (0, 0)),
        ] + [ANY] * (len(kept) + len(waits)),
        out_specs=[
            pl.BlockSpec((block, 128), lambda h, i: (i, base + h)),
            pl.BlockSpec((None, 2, total, block), lambda h, i: (h, 0, 0, i)),
            pl.BlockSpec((None, 2, block), lambda h, i: (h, 0, i)),
        ],
        out_shape=[
            jax.ShapeDtypeStruct((total, qkv.shape[1] // 3), BF),
            jax.ShapeDtypeStruct((pairs, 2, total, total), BF),
            jax.ShapeDtypeStruct((pairs, 2, total), F32),
        ],
        scratch_shapes=[pltpu.VMEM((128, total), BF), pltpu.VMEM((2, 1), F32)],
        compiler_params=params(),
        cost_estimate=pl.CostEstimate(flops=pairs * 12 * 10**9, bytes_accessed=pairs << 24, transcendentals=0),
        input_output_aliases={5: 0} if kept else {},
        name="attend",
    )(qkv, qkv, qkv, seg_row, seg_col, *kept, *waits)


def attend_back_kernel(chunk, extra, q_ref, k_ref, v_ref, o_ref, do_ref, do2_ref, p_ref, l_ref, *rest):
    out_ref, mark_ref, kt_ref, dk_acc, dv_acc = rest[extra:]
    i = pl.program_id(1)
    total = k_ref.shape[0]
    block = q_ref.shape[0]

    @pl.when(i == 0)
    def _():
        kt_ref[...] = k_ref[...].T
        dk_acc[...] = jnp.zeros_like(dk_acc)
        dv_acc[...] = jnp.zeros_like(dv_acc)

    do = jnp.where(i < pl.num_programs(1) // 2, do_ref[...], do2_ref[...])
    q_parts = head_parts(q_ref[...])
    do_parts = head_parts(do)
    product = do.astype(F32) * o_ref[...].astype(F32)
    delta = jnp.sum(product.T.reshape(2, HD, block), axis=1)
    inverse = l_ref[...]
    grad_q = [jnp.zeros((HD, block), F32)] * 2
    for lo in range(0, total, chunk):
        rows = slice(lo, lo + chunk)
        values = v_ref[rows, :]
        for h in range(2):
            p = p_ref[h, rows, :].astype(F32) * inverse[h : h + 1]
            grad_p = mm(values, do_parts[h], NT)
            grad_s = (p * (grad_p - delta[h : h + 1])).astype(BF)
            dv_acc[rows, :] += mm(p.astype(BF), do_parts[h])
            dk_acc[rows, :] += mm(grad_s, q_parts[h])
            grad_q[h] = grad_q[h] + mm(kt_ref[h * HD : h * HD + HD, rows], grad_s)
    grad_q = jnp.concatenate(grad_q, axis=0).T.astype(BF)
    out_ref[pl.ds(pl.multiple_of(i * block, block), block), 0:128] = grad_q
    add_fold(mark_ref.at[0:8, :], i == 0, grad_q.astype(F32))

    @pl.when(i == pl.num_programs(1) - 1)
    def _():
        out_ref[:, 128:256] = dk_acc[...].astype(BF)
        grad_v = dv_acc[...].astype(BF)
        out_ref[:, 256:384] = grad_v
        mark_ref[8:16, :] = fold(grad_v.astype(F32))


def attend_back(qkv, out, grad_mine, grad_mate, probs, inverse, base, held=None, waits=(), block=256, chunk=1024):
    total = qkv.shape[0]
    kept = [] if held is None else [held]
    pairs, skip = 1, base % probs.shape[0]
    last = total // block // 2 - 1
    whole = lambda c: pl.BlockSpec((total, 128), lambda h, i: (0, 3 * (base + h) + c))
    rows = pl.BlockSpec((block, 128), lambda h, i: (i, base + h))
    return pl.pallas_call(
        functools.partial(attend_back_kernel, chunk, len(waits) + len(kept)),
        grid=(pairs, total // block),
        in_specs=[
            pl.BlockSpec((block, 128), lambda h, i: (i, 3 * (base + h))),
            whole(1),
            whole(2),
            rows,
            pl.BlockSpec((block, 128), lambda h, i: (jnp.minimum(i, last), base + h)),
            pl.BlockSpec((block, 128), lambda h, i: (jnp.maximum(i - last - 1, 0), base + h)),
            pl.BlockSpec((None, 2, total, block), lambda h, i: (skip + h, 0, 0, i)),
            pl.BlockSpec((None, 2, block), lambda h, i: (skip + h, 0, i)),
        ] + [ANY] * (len(kept) + len(waits)),
        out_specs=[pl.BlockSpec((total, 384), lambda h, i: (0, base + h)), pl.BlockSpec((16, 128), lambda h, i: (0, 0))],
        out_shape=[jax.ShapeDtypeStruct(qkv.shape, BF), jax.ShapeDtypeStruct((16, 128), F32)],
        scratch_shapes=[
            pltpu.VMEM((128, total), BF),
            pltpu.VMEM((total, 128), F32),
            pltpu.VMEM((total, 128), F32),
        ],
        compiler_params=params(),
        cost_estimate=pl.CostEstimate(flops=10**8, bytes_accessed=1 << 16, transcendentals=0),
        input_output_aliases={8: 0} if kept else {},
        name="attend_back",
    )(qkv, qkv, qkv, out, grad_mine, grad_mate, probs, inverse, *kept, *waits)


def gelu_parts(u):
    phi = 0.5 + 0.5 * lax.erf(u * 0.7071067811865476)
    return u * phi, phi + u * (jnp.exp(u * u * -0.5) * 0.3989422804014327)


def mean(value):
    return jnp.mean(value, axis=-1, keepdims=True)


def normed(hidden):
    centred = hidden - mean(hidden)
    inverse = lax.rsqrt(mean(centred * centred) + EPSILON)
    return centred * inverse, inverse


def norm_back(grad_in, scaled, inverse, gain):
    grad_scaled = grad_in * gain
    return inverse * (grad_scaled - mean(grad_scaled) - scaled * mean(grad_scaled * scaled))


def fold(value):
    return jnp.sum(value.reshape(value.shape[0] // 8, 8, value.shape[1]), axis=0)


def add_fold(ref, first, value):
    part = fold(value)

    @pl.when(first)
    def _():
        ref[...] = part

    @pl.when(jnp.logical_not(first))
    def _():
        ref[...] += part


def token_rows(x, span, block, at=lambda i: i):
    return pl.BlockSpec((block // span, span, x.shape[2]), lambda i: (at(i), 0, 0))


def qkv_kernel(order_ref, xm_ref, xt_ref, b_ref, *refs):
    pieces, (out_ref, w_ref, sems) = refs[:-3], refs[-3:]
    load_heads(pieces, order_ref, w_ref, sems)
    i = pl.program_id(0)
    x = jnp.where(i < pl.num_programs(0) // 2, xm_ref[...], xt_ref[...])
    out_ref[...] = (mm(x.reshape(out_ref.shape[0], -1), w_ref[...]) + b_ref[...]).astype(BF)


def project(x_mine, x_mate, span, pieces, order, bias, block=256):
    steps = x_mine.shape[0] * span // block
    width = bias.shape[1]
    return pl.pallas_call(
        qkv_kernel,
        grid=(2 * steps,),
        in_specs=[
            SMEM,
            token_rows(x_mine, span, block, lambda i: jnp.minimum(i, steps - 1)),
            token_rows(x_mate, span, block, lambda i: jnp.maximum(i - steps, 0)),
            pl.BlockSpec((1, width), lambda i: (0, 0)),
        ]
        + [ANY] * len(pieces),
        out_specs=pl.BlockSpec((block, width), lambda i: (i, 0)),
        out_shape=jax.ShapeDtypeStruct((2 * steps * block, width), BF),
        scratch_shapes=[pltpu.VMEM((x_mine.shape[2], width), BF), pltpu.SemaphoreType.DMA((shards_of(pieces),))],
        compiler_params=params(),
        cost_estimate=pl.CostEstimate(flops=7 * 10**9, bytes_accessed=14 << 20, transcendentals=0),
        name="project",
    )(order, x_mine, x_mate, bias, *pieces)


def mid_up_kernel(step, count, mates, order_ref, x_ref, om_ref, vec_ref, bu_ref, *refs):
    mate_refs, refs = refs[:mates], refs[mates:]
    pieces, (xh_ref, r_ref, xb_ref, g_ref, gp_ref, wo_ref, wu_ref, sems) = refs[:count], refs[count:]
    first = pl.program_id(0) == 0
    d, ff = wu_ref.shape
    shards = shards_of(pieces)

    def out_copies():
        return shard_copies(pieces, order_ref, slice(0, d), wo_ref, sems, 0, order_ref[shards])

    def up_copies():
        return shard_copies(pieces, order_ref, slice(d, d + ff), wu_ref, sems, shards)

    @pl.when(first)
    def _():
        for copy in out_copies() + up_copies():
            copy.start()
        for copy in out_copies():
            copy.wait()

    half = om_ref.shape[1]
    mixed = mm(om_ref[...], wo_ref[0:half, :])
    for ref in mate_refs:
        mixed = mixed + mm(ref[...], wo_ref[half : half + ref.shape[1], :])
        half += ref.shape[1]
    hidden = x_ref[...].reshape(mixed.shape).astype(F32) + mixed + vec_ref[0:1, :]
    scaled, inverse = normed(hidden)
    xh_ref[...] = scaled
    r_ref[...] = inverse
    xb = (scaled * vec_ref[1:2, :] + vec_ref[2:3, :]).astype(BF)
    xb_ref[...] = xb

    @pl.when(first)
    def _():
        for copy in up_copies():
            copy.wait()

    for lo in range(0, ff, step):
        cols = slice(lo, lo + step)
        g, gp = gelu_parts(mm(xb, wu_ref[:, cols]) + bu_ref[:, cols])
        g_ref[:, cols] = g.astype(BF)
        gp_ref[:, cols] = gp.astype(BF)


def mid_up(x, span, attn, o_mate, pieces, order, vecs, b_up, block=256, step=512):
    rows, d = x.shape[0] * span, x.shape[2]
    ff = b_up.shape[1]
    row = lambda n: pl.BlockSpec((block, n), lambda i: (i, 0))
    full = lambda a: pl.BlockSpec(a.shape, lambda i: (0, 0), pipeline_mode=pl.Buffered(1))
    return pl.pallas_call(
        functools.partial(mid_up_kernel, step, len(pieces), len(o_mate)),
        grid=(rows // block,),
        in_specs=[SMEM, token_rows(x, span, block), row(d // 2), full(vecs), full(b_up)]
        + [row(a.shape[1]) for a in o_mate]
        + [ANY] * len(pieces),
        out_specs=[row(d), row(1), row(d), row(ff), row(ff)],
        out_shape=[
            jax.ShapeDtypeStruct((rows, d), F32),
            jax.ShapeDtypeStruct((rows, 1), F32),
            jax.ShapeDtypeStruct((rows, d), BF),
            jax.ShapeDtypeStruct((rows, ff), BF),
            jax.ShapeDtypeStruct((rows, ff), BF),
        ],
        scratch_shapes=[
            pltpu.VMEM((d, d), BF),
            pltpu.VMEM((d, ff), BF),
            pltpu.SemaphoreType.DMA((2 * shards_of(pieces),)),
        ],
        compiler_params=params(),
        cost_estimate=pl.CostEstimate(flops=20 * 10**9, bytes_accessed=36 << 20, transcendentals=0),
        name="mid_up",
    )(order, x, attn, vecs, b_up, *o_mate, *pieces)


def mid_down_kernel(step, count, blocks, order_ref, g_ref, gp_ref, xh_ref, dy_ref, vec_ref, *refs):
    pieces, (out_ref, dh_ref, dm_ref, du_ref, s_ref, su_ref, wd_ref, sems) = refs[:count], refs[count:]
    first = pl.program_id(0) == 0
    d = wd_ref.shape[1]

    @pl.when(first)
    def _():
        copies = []
        for n in range(blocks[1]):
            cols = slice(blocks[0] + n * d, blocks[0] + (n + 1) * d)
            copies += shard_copies(pieces, order_ref, cols, wd_ref, sems, len(copies), None, blocks[1], n)
        for copy in copies:
            copy.start()
        for copy in copies:
            copy.wait()

    x1 = xh_ref[...] * vec_ref[1:2, :] + vec_ref[2:3, :]
    hidden = x1 + mm(g_ref[...], wd_ref[...]) + vec_ref[3:4, :]
    scaled, inverse = normed(hidden)
    gain = vec_ref[4:5, :]
    out_ref[...] = (scaled * gain + vec_ref[5:6, :]).astype(BF)
    dy = dy_ref[...].astype(F32)
    dh = norm_back(dy, scaled, inverse, gain)
    dm = dh.astype(BF)
    dh_ref[...] = dh
    dm_ref[...] = dm
    add_fold(s_ref.at[0:8, :], first, dy * scaled)
    add_fold(s_ref.at[8:16, :], first, dy)
    add_fold(s_ref.at[16:24, :], first, dm.astype(F32))
    for lo in range(0, wd_ref.shape[0], step):
        cols = slice(lo, lo + step)
        du = (mm(dm, wd_ref[cols, :], NT) * gp_ref[:, cols].astype(F32)).astype(BF)
        du_ref[:, cols] = du
        add_fold(su_ref.at[:, cols], first, du.astype(F32))


def mid_down(g, gp, xh, dy, pieces, order, blocks, vecs, block=256, step=2048):
    rows, d = xh.shape
    ff = g.shape[1]
    row = lambda n: pl.BlockSpec((block, n), lambda i: (i, 0))
    full = lambda a: pl.BlockSpec(a.shape, lambda i: (0, 0), pipeline_mode=pl.Buffered(1))
    keep = lambda r, n: pl.BlockSpec((r, n), lambda i: (0, 0))
    return pl.pallas_call(
        functools.partial(mid_down_kernel, step, len(pieces), blocks),
        grid=(rows // block,),
        in_specs=[SMEM, row(ff), row(ff), row(d), row(d), full(vecs)] + [ANY] * len(pieces),
        out_specs=[row(d), row(d), row(d), row(ff), keep(24, d), keep(8, ff)],
        out_shape=[
            jax.ShapeDtypeStruct((rows, d), BF),
            jax.ShapeDtypeStruct((rows, d), F32),
            jax.ShapeDtypeStruct((rows, d), BF),
            jax.ShapeDtypeStruct((rows, ff), BF),
            jax.ShapeDtypeStruct((24, d), F32),
            jax.ShapeDtypeStruct((8, ff), F32),
        ],
        scratch_shapes=[pltpu.VMEM((ff, d), BF), pltpu.SemaphoreType.DMA((shards_of(pieces) * blocks[1],))],
        compiler_params=params(),
        cost_estimate=pl.CostEstimate(flops=25 * 10**9, bytes_accessed=44 << 20, transcendentals=0),
        name="mid_down",
    )(order, g, gp, xh, dy, vecs, *pieces)


def mid_back_kernel(count, order_ref, dh_ref, du_ref, xh_ref, r_ref, vec_ref, *refs):
    pieces, (dh1_ref, da_ref, dom_ref, dot_ref, s_ref, wu_ref, wo_ref, sems) = refs[:count], refs[count:]
    first = pl.program_id(0) == 0
    d, ff = wu_ref.shape
    half = dom_ref.shape[1]
    shards = shards_of(pieces)

    @pl.when(first)
    def _():
        copies = shard_copies(pieces, order_ref, slice(d, d + ff), wu_ref, sems, shards)
        copies += shard_copies(pieces, order_ref, slice(0, d), wo_ref, sems, 0, order_ref[shards])
        for copy in copies:
            copy.start()
        for copy in copies:
            copy.wait()

    dx = dh_ref[...] + mm(du_ref[...], wu_ref[...], NT)
    scaled = xh_ref[...]
    dh1 = norm_back(dx, scaled, r_ref[...], vec_ref[1:2, :])
    dh1_ref[...] = dh1
    da = dh1.astype(BF)
    da_ref[...] = da
    dom_ref[...] = mm(da, wo_ref[0:half, :], NT).astype(BF)
    dot_ref[...] = mm(da, wo_ref[half:, :], NT).astype(BF)
    add_fold(s_ref.at[0:8, :], first, dx * scaled)
    add_fold(s_ref.at[8:16, :], first, dx)
    add_fold(s_ref.at[16:24, :], first, da.astype(F32))


def mid_back(dh, du, xh, r, pieces, order, vecs, block=256):
    rows, d = dh.shape
    ff = du.shape[1]
    row = lambda n: pl.BlockSpec((block, n), lambda i: (i, 0))
    full = lambda a: pl.BlockSpec(a.shape, lambda i: (0, 0), pipeline_mode=pl.Buffered(1))
    return pl.pallas_call(
        functools.partial(mid_back_kernel, len(pieces)),
        grid=(rows // block,),
        in_specs=[SMEM, row(d), row(ff), row(d), row(1), full(vecs)] + [ANY] * len(pieces),
        out_specs=[row(d), row(d), row(d // 2), row(d // 2), pl.BlockSpec((24, d), lambda i: (0, 0))],
        out_shape=[
            jax.ShapeDtypeStruct((rows, d), F32),
            jax.ShapeDtypeStruct((rows, d), BF),
            jax.ShapeDtypeStruct((rows, d // 2), BF),
            jax.ShapeDtypeStruct((rows, d // 2), BF),
            jax.ShapeDtypeStruct((24, d), F32),
        ],
        scratch_shapes=[
            pltpu.VMEM((d, ff), BF),
            pltpu.VMEM((d, d), BF),
            pltpu.SemaphoreType.DMA((2 * shards_of(pieces),)),
        ],
        compiler_params=params(),
        cost_estimate=pl.CostEstimate(flops=15 * 10**9, bytes_accessed=36 << 20, transcendentals=0),
        name="mid_back",
    )(order, dh, du, xh, r, vecs, *pieces)


def token_kernel(adds, count, order_ref, grad_ref, *refs):
    add_refs, pieces, (out_ref, w_ref, sems) = refs[:adds], refs[adds : adds + count], refs[-3:]
    load_heads(pieces, order_ref, w_ref, sems)
    total = mm(grad_ref[...], w_ref[...], NT)
    for ref in add_refs:
        total = total + ref[...].astype(F32)
    out_ref[...] = total.astype(BF)


def token_grad(grads, pieces, order, d, shift, adds, waits=(), block=256):
    rows, width = grads.shape[0] // 2, grads.shape[1]
    base = shift * (rows // block)
    row = pl.BlockSpec((block, d), lambda i: (i, 0))
    return pl.pallas_call(
        functools.partial(token_kernel, len(adds), len(pieces)),
        grid=(rows // block,),
        in_specs=[SMEM, pl.BlockSpec((block, width), lambda i: (base + i, 0))]
        + [row] * len(adds)
        + [ANY] * (len(pieces) + len(waits)),
        out_specs=row,
        out_shape=jax.ShapeDtypeStruct((rows, d), BF),
        scratch_shapes=[pltpu.VMEM((d, width), BF), pltpu.SemaphoreType.DMA((shards_of(pieces),))],
        compiler_params=params(),
        cost_estimate=pl.CostEstimate(flops=10**8, bytes_accessed=1 << 16, transcendentals=0),
        name="token_grad",
    )(order, grads, *adds, *pieces, *waits)


def finish_kernel(core_ref, up_ref, up_mate_ref, last_ref, last_mate_ref, *outs):
    gu_ref, go_ref, gq_ref, gk_ref, gv_ref, small_ref = outs
    core = core_ref[0]
    first = core == 0
    ff, half = gu_ref.shape[1], go_ref.shape[1] // 2

    def halves(ref, mate_ref, lo, width):
        mine, mate = ref[core, :, lo : lo + width].astype(F32), mate_ref[:, lo : lo + width].astype(F32)
        return jnp.where(first, mine, mate), jnp.where(first, mate, mine), mine + mate

    left, right, _ = halves(up_ref, up_mate_ref, 0, ff // 2)
    gu_ref[:, : ff // 2], gu_ref[:, ff // 2 :] = left, right
    left, right, _ = halves(up_ref, up_mate_ref, ff // 2, half)
    go_ref[:, :half], go_ref[:, half:] = left, right
    small_ref[0] = halves(up_ref, up_mate_ref, ff // 2 + half, 128)[2]
    for pair in range(half // 128):
        at = pair * 128
        for n, out in enumerate((gq_ref, gk_ref, gv_ref)):
            left, right, _ = halves(last_ref, last_mate_ref, 3 * at + n * 128, 128)
            scale = QSCALE if n == 0 else 1.0
            out[:, at : at + 128], out[:, half + at : half + at + 128] = left * scale, right * scale
    small_ref[1] = halves(last_ref, last_mate_ref, 3 * half, 128)[2]


def finish(core, rows, ff, d, *arrays):
    shapes = [(rows, ff)] + [(rows, d)] * 4 + [(2, rows, 128)]
    return pl.pallas_call(
        finish_kernel,
        in_specs=[SMEM] + [pl.BlockSpec(memory_space=pltpu.VMEM)] * 4,
        out_shape=[jax.ShapeDtypeStruct(shape, F32) for shape in shapes],
        compiler_params=params(),
        name="finish",
    )(jnp.reshape(core, (1,)).astype(jnp.int32), *arrays)


def by_chip(value, out_ref, lo):
    chips, dps, rows, _ = out_ref.shape
    value = value.reshape(dps, chips, rows, value.shape[1])
    for n in range(dps):
        out_ref[:, n, :, lo : lo + value.shape[3]] = value[n].astype(BF)


def proj_kernel(xm_ref, xt_ref, grad_ref, *refs):
    out_ref = refs[-1]
    own = grad_ref.shape[0] // 2
    xm = xm_ref[...].reshape(own, -1)
    xt = xt_ref[...].reshape(own, -1)
    by_chip(mm(xm, grad_ref[0:own, :], TN) + mm(xt, grad_ref[own:, :], TN), out_ref, 0)
    if grad_ref.shape[1] < out_ref.shape[3]:
        out_ref[:, :, :, grad_ref.shape[1] :] = refs[0][...]


def dp_steps(groups, least):
    return max(1, min(groups, least // 128))


def shard_specs(steps, groups, chips, rows, cols):
    spec = pl.BlockSpec((chips, groups // steps, rows, cols), lambda i, *_: (0, i, 0, 0))
    return spec, jax.ShapeDtypeStruct((chips, groups, rows, cols), BF)


def proj_grad(x_mine, x_mate, span, grads, first, pairs, groups, chips, waits=(), extra=None):
    own, d = x_mine.shape[0] * span, x_mine.shape[2]
    width = 384 * pairs
    more = [] if extra is None else [extra]
    steps = dp_steps(groups, d)
    col = pl.BlockSpec((x_mine.shape[0], span, d // steps), lambda i: (0, 0, i))
    rows = d // groups // chips
    spec, shape = shard_specs(steps, groups, chips, rows, width + sum(a.shape[3] for a in more))
    return pl.pallas_call(
        proj_kernel,
        grid=(steps,),
        in_specs=[col, col]
        + [pl.BlockSpec((2 * own, width), lambda i: (0, first // pairs), pipeline_mode=pl.Buffered(1))]
        + [shard_specs(steps, groups, chips, rows, a.shape[3])[0] for a in more]
        + [ANY] * len(waits),
        out_specs=spec,
        out_shape=shape,
        compiler_params=params(),
        cost_estimate=pl.CostEstimate(flops=10**8, bytes_accessed=1 << 16, transcendentals=0),
        name="proj_grad",
    )(x_mine, x_mate, grads, *more, *waits)


def weight_kernel(adds, waits, turn_ref, *refs):
    out_ref, refs = refs[-1], refs[: len(refs) - 1 - waits]
    count = (len(refs) - adds) // 2
    more = refs[2 * count :]
    lo = 0
    for n in range(count):
        value = mm(refs[2 * n][...], refs[2 * n + 1][...], TN)
        width = value.shape[1]
        chips, dps, rows, _ = out_ref.shape
        value = value.reshape(dps, chips, rows, width)
        for k in range(dps):
            part = value[k]
            if more:
                part = part + more[0][:, k, :, lo : lo + width].astype(F32)
            out_ref[:, k, :, lo : lo + width] = part.astype(BF)
        lo += width
    if lo < out_ref.shape[3]:
        out_ref[:, :, :, lo:] = more[-1][...]


def weight_grad(sides, turns, groups, chips, adds=(), waits=()):
    in_specs, args = [], []
    steps = dp_steps(groups, min(left.shape[1] for left, _ in sides))
    rows_of = lambda a: a.shape[1] // steps
    for n, (left, right) in enumerate(sides):
        tokens = left.shape[0]
        in_specs.append(
            pl.BlockSpec((tokens, rows_of(left)), lambda i, t, n=n: (0, lax.rem(i + t[1 + n] * (steps // 2), steps)))
        )
        in_specs.append(
            pl.BlockSpec((tokens, right.shape[1] // 2), lambda i, t: (0, t[0]), pipeline_mode=pl.Buffered(1))
        )
        args += [left, right]
    rows = sides[0][0].shape[1] // groups // chips
    cols = sum(right.shape[1] // 2 for _, right in sides)
    if len(adds) > 1:
        cols += adds[1].shape[3]
    in_specs += [shard_specs(steps, groups, chips, rows, a.shape[3])[0] for a in adds] + [ANY] * len(waits)
    spec, shape = shard_specs(steps, groups, chips, rows, cols)
    flops = sum(a.shape[0] * a.shape[1] * b.shape[1] for a, b in sides)
    return pl.pallas_call(
        functools.partial(weight_kernel, len(adds), len(waits)),
        grid_spec=pltpu.PrefetchScalarGridSpec(
            num_scalar_prefetch=1, grid=(steps,), in_specs=in_specs, out_specs=spec
        ),
        out_shape=shape,
        compiler_params=params(),
        cost_estimate=pl.CostEstimate(flops=10**8, bytes_accessed=1 << 16, transcendentals=0),
        name="weight_grad",
    )(turns, *args, *adds, *waits)


def swap(value, mask):
    count = lax.axis_size("ctx")
    return lax.ppermute(value, "ctx", [(d, d ^ mask) for d in range(count)])


def along(value, step):
    count = lax.axis_size("dp")
    return lax.ppermute(value, "dp", [(s, (s + step) % count) for s in range(count)])


def pick(value, index, axis=0):
    return lax.dynamic_index_in_dim(value, index, axis, keepdims=False)


def over_chips(value):
    count = lax.axis_size("ctx")
    groups = [list(range(core, count, 2)) for core in range(2)]
    return lax.all_to_all(value, "ctx", 0, 0, axis_index_groups=groups)


def tick(value):
    return (value[(0,) * value.ndim].astype(F32) > 1e30).astype(jnp.int32)


def tie_kernel(*refs):
    pass


def tie(value, *waits):
    return pl.pallas_call(
        tie_kernel,
        in_specs=[ANY] * (1 + len(waits)),
        out_specs=ANY,
        out_shape=jax.ShapeDtypeStruct(value.shape, value.dtype),
        input_output_aliases={0: 0},
        name="tie",
    )(value, *waits)


class Gather:
    def __init__(self, own, place):
        self.place = place
        self.groups = lax.axis_size("dp")
        self.chips = lax.axis_size("ctx") // 2
        self.own = own
        self.whole = own.shape[0] % TILE != 0

    def along_dp(self, value):
        if self.whole:
            return []
        self.turns = [value] + [along(value, s) for s in range(1, self.groups)]
        return self.turns[1:]

    def over_chips(self, later):
        if self.whole:
            return
        half = self.groups // 2
        bits = list(range(self.chips.bit_length() - 1))
        stacked = jnp.stack(self.turns) + later.astype(BF)
        self.held = []
        for first, order in ((0, bits), (half, bits[::-1])):
            value = stacked[first : first + half]
            labels = [(first + n, 0) for n in range(half)]
            for n, bit in enumerate(order):
                other = swap(value, 2 << bit)
                more = [(t, r ^ (1 << bit)) for t, r in labels]
                if n + 1 < len(order):
                    value, labels = jnp.concatenate([value, other]), labels + more
                else:
                    self.held += [(value, labels), (other, more)]

    def between_cores(self):
        me, chip, core = self.place
        if self.whole:
            return [lax.all_gather(self.own, BOTH, axis=0, tiled=True)[None]], jnp.zeros((1,), jnp.int32)
        pieces, order = [], []
        for value, labels in self.held:
            pieces += [value, swap(value, 1)]
            for mate in (core, 1 - core):
                order += [(me - t) % self.groups * 2 * self.chips + 2 * (chip ^ r) + mate for t, r in labels]
        return pieces, jnp.stack(order).astype(jnp.int32)


class Reduce:
    def __init__(self, grad, place, direct=False):
        self.place = place
        self.groups = grad.shape[1]
        if direct:
            chip = place[1]
            sent = [pick(grad, chip ^ r) for r in range(1, grad.shape[0])]
            self.got = [pick(grad, chip)] + [swap(v, 2 * (r + 1)) for r, v in enumerate(sent)]
        else:
            self.got = over_chips(grad)

    def chip_sum(self, *waits):
        if isinstance(self.got, list):
            last = tie(self.got[-1], *self.got[1:-1], *waits)
            self.part = sum(v.astype(F32) for v in self.got[:-1] + [last]).astype(BF)
        else:
            self.part = jnp.sum(tie(self.got, *waits).astype(F32), axis=0).astype(BF)
        return [self.part]

    def along_dp(self):
        me = self.place[0]
        sent = [pick(self.part, (me + step) % self.groups) for step in range(1, self.groups)]
        self.turns = [pick(self.part, me)] + [along(v, n + 1) for n, v in enumerate(sent)]

    def dp_sum(self, *waits):
        last = tie(self.turns[-1], *self.turns[1:-1], *waits)
        total = sum(v.astype(F32) for v in self.turns[:-1] + [last]).astype(BF)
        self.total = total.reshape(2, -1, total.shape[1])
        return [self.total]

    def both(self):
        return self.total, swap(pick(self.total, 1 - self.place[2]), 1)


def half_cols(value, which):
    width = value.shape[-1] // 2
    return lax.dynamic_slice_in_dim(value, which * width, width, value.ndim - 1)


def spread(vectors, shards, rows):
    flat = jnp.concatenate([v.reshape(shards, -1) for v in vectors], axis=1)
    return jnp.pad(flat, ((0, 0), (0, rows * 128 - flat.shape[1]))).reshape(shards, rows, 128)


def fold_rows(sums):
    return jnp.sum(sums.reshape(-1, 8, sums.shape[1]), axis=1)


def local(
    tokens, segments, cotangent, w_query, w_key, w_value, w_out, w_up, w_down,
    b_query, b_value, b_out, b_up, b_down, gain_attn, shift_attn, gain_mlp, shift_mlp,
):
    seqs, span, d = tokens.shape
    count = lax.axis_size("ctx")
    groups = lax.axis_size("dp")
    chips = count // 2
    ctx = lax.axis_index("ctx")
    chip, core = ctx // 2, ctx % 2
    place_of = (lax.axis_index("dp"), chip, core)
    ff = w_up.shape[1]
    half = d // 2
    shards = groups * count
    rows = d // shards
    width = d // shards
    pairs = half // 128
    bf = lambda v: v.astype(BF)

    vec_names = (b_query, b_value, b_out, gain_attn, shift_attn, b_down, gain_mlp, shift_mlp)
    vec_size = 8 * width + ff // shards
    extra = -(-(vec_size + seqs * span) // (rows * 128)) * 128
    vec_pack = jnp.concatenate([bf(v) for v in vec_names] + [bf(b_up), bf(segments.reshape(-1))])
    vec_pack = jnp.pad(vec_pack, (0, rows * extra - vec_pack.shape[0])).reshape(rows, extra)
    packed = pack(w_query, w_key, w_value, w_out, w_up, w_down, vec_pack)

    got = over_chips(tokens)
    own = chips * span
    proj = Gather(packed[0], place_of)
    turns_of = proj.along_dp(proj.own)
    got = tie(got, *turns_of)
    mate = swap(got, 1)
    later = tick(got)
    proj.over_chips(later)
    pieces, order = proj.between_cores()
    def everywhere(value):
        return lax.all_gather(tie(value, got), BOTH, axis=0, tiled=True).reshape(2, -1, value.shape[1])

    up_pieces = [everywhere(packed[1])]
    if rows % TILE == 0:
        down_pieces, blocks = [up_pieces[0].reshape(shards, rows, -1)], (d + ff, w_down.shape[0] // rows)
    else:
        down_pieces, blocks = [everywhere(packed[2])], (0, 1)
    down_order = jnp.arange(down_pieces[0].shape[0], dtype=jnp.int32)
    vec_block = pieces[0][0, :, 3 * d :] if proj.whole else place(pieces, order, 3 * d)
    order = jnp.append(order, core * 3 * half).astype(jnp.int32)
    packed = vec_block.reshape(shards, rows * extra)
    vec_all = packed[:, :vec_size].astype(F32)
    seg_all = packed[:, vec_size : vec_size + seqs * span].reshape(groups, chips, 2, seqs, span)
    seg_own = pick(pick(seg_all, place_of[0]), chip, 2)
    seg = jnp.concatenate([pick(seg_own, core, 1), pick(seg_own, 1 - core, 1)]).reshape(-1).astype(jnp.int32)
    vec = [vec_all[:, n * width : (n + 1) * width].reshape(1, d) for n in range(8)]
    bias_up = vec_all[:, 8 * width : 8 * width + ff // shards].reshape(1, ff)
    vecs = jnp.concatenate(vec[2:] + [jnp.zeros((2, d), F32)], axis=0)
    bias_by_pair = [v.reshape(1, 2 * pairs, 1, 128) for v in (vec[0] * QSCALE, jnp.zeros((1, d), F32), vec[1])]
    bias_cat = half_cols(jnp.concatenate(bias_by_pair, axis=2).reshape(1, 3 * d), core)

    qkv = project(got, mate, span, pieces, order, bias_cat)
    seg_row, seg_col = seg.reshape(1, -1), seg.reshape(-1, 1)

    attn, probs, inverse, o_mate = None, [], [], []
    for n in range(0, pairs, 2):
        attn, p, l = attend(qkv, seg_row, seg_col, n, 2, attn)
        probs.append(p)
        inverse.append(l)
        o_mate.append(swap(attn[own:, n * 128 : (n + 2) * 128], 1))
    dy = over_chips(cotangent + tick(inverse[0]).astype(BF)).reshape(own, d)
    up_order = jnp.stack([jnp.zeros((), jnp.int32), jnp.ones((), jnp.int32), d - core * half]).astype(jnp.int32)
    xh, r, xb, g, gp = mid_up(got, span, attn, o_mate, up_pieces, up_order, vecs, bias_up)
    out, dh2, dm, du, sums_two, sums_up = mid_down(g, gp, xh, dy, down_pieces, down_order, blocks, vecs)
    result_out = over_chips(out.reshape(chips, span, d))

    zero = jnp.zeros((), jnp.int32)
    turns = lambda half_of, *more: jnp.stack([half_of, *more]).astype(jnp.int32)
    got_down = swap(weight_grad([(g, dm)], turns(1 - core, zero), groups, chips), 1)
    dh1, da, do_mine, do_send, sums_one = mid_back(dh2, du, xh, r, up_pieces, up_order, vecs)
    do_mate = swap(do_send, 1)
    kept_down = weight_grad([(g, dm)], turns(core, zero), groups, chips, [got_down], [result_out])
    sum_down = Reduce(kept_down, place_of)

    o_both = jnp.concatenate([attn[:own]] + o_mate, axis=1)
    sides, shift = [(xb, du), (o_both, da)], core
    got_up = swap(weight_grad(sides, turns(1 - core, zero, shift), groups, chips, (), [kept_down]), 1)
    two, one = fold_rows(sums_two), fold_rows(sums_one)
    per_shard = lambda v: jnp.moveaxis(bf(v).reshape(groups, chips, -1, 128), 1, 0)
    vec_grads = per_shard(spread([one[2], one[0], one[1], two[2], two[0], two[1], fold_rows(sums_up)], shards, rows))

    grads, waits, marks = None, [], []
    for n in range(pairs):
        grads, mark = attend_back(qkv, attn, do_mine, do_mate, probs[n // 2], inverse[n // 2], n, grads, waits)
        waits = []
        marks.append(mark)
        if n == 0:
            got_up = tie(got_up, mark)
            kept_up = weight_grad(sides, turns(core, zero, shift), groups, chips, [got_up, vec_grads])
            waits = sum_down.chip_sum(mark, kept_up)
            sum_down.along_dp()
            sum_up = Reduce(kept_up, place_of)
        elif n == 1:
            waits = sum_down.dp_sum(mark)
        elif n == 2:
            first = proj_grad(got, mate, span, grads, 0, 3, groups, chips)
            waits = sum_up.chip_sum(mark, first)
            sum_up.along_dp()
            sum_first = Reduce(tie(first, sum_up.part), place_of)
    bias_sums = jnp.stack([fold_rows(v) for v in marks])
    blank = jnp.zeros((half,), F32)

    def whole_vector(c):
        part = bias_sums[:, c].reshape(-1)
        return jnp.where(core == 0, jnp.concatenate([part, blank]), jnp.concatenate([blank, part]))

    bias_grads = per_shard(spread([whole_vector(0), whole_vector(1)], shards, rows))
    token_send = token_grad(grads, pieces, order, d, 1, (), [sum_first.got] + sum_up.turns[1:])
    token_got = swap(token_send, 1)
    last = proj_grad(got, mate, span, grads, 3, 1, groups, chips, [token_send], bias_grads)
    sum_last = Reduce(last, place_of, True)
    grad_mine = token_grad(grads, pieces, order, d, 0, (dh1, token_got), [last])
    arrived = sum_last.got[1:]
    grad_mine = tie(grad_mine, *arrived)
    sum_last.chip_sum()
    sum_first.chip_sum(*arrived)
    sum_up.dp_sum(*arrived)
    arrived_tokens = over_chips(grad_mine.reshape(chips, span, d))
    grad_tokens = arrived_tokens + tick(arrived_tokens).astype(BF)
    sum_last.part = jnp.concatenate([sum_first.part, sum_last.part], axis=2)
    sum_last.along_dp()
    sum_last.dp_sum(arrived_tokens)

    mine, other = sum_down.both()
    mine = pick(mine, core)
    order_of = jnp.where(core == 0, jnp.stack([mine, other]), jnp.stack([other, mine]))
    grad_down = jnp.concatenate([order_of[0], order_of[1]], axis=1).astype(F32)
    grad_up, grad_out, grad_query, grad_key, grad_value, small = finish(
        core, rows, ff, d, *sum_up.both(), *sum_last.both()
    )
    sums = small[0].reshape(-1)
    g_bo, g_ga, g_sa, g_bd, g_gm, g_sm = [sums[n * width : (n + 1) * width] for n in range(6)]
    g_bu = sums[6 * width : 6 * width + ff // shards]
    sums = small[1].reshape(-1)
    g_bq, g_bv = sums[:width] * QSCALE, sums[width : 2 * width]
    return (
        result_out, grad_tokens, grad_query, grad_key, grad_value, grad_out, grad_up, grad_down,
        g_bq, g_bv, g_bo, g_bu, g_bd, g_ga, g_sa, g_gm, g_sm,
    )


def solution(mesh):
    act, flat, mat, vec = P("dp", "ctx", None), P("dp", "ctx"), P(BOTH, None), P(BOTH)
    return jax.shard_map(
        local,
        mesh=mesh,
        in_specs=(act, flat, act) + (mat,) * 6 + (vec,) * 9,
        out_specs=(act, act) + (mat,) * 6 + (vec,) * 9,
        check_vma=False,
    )
```

```python
import functools

import jax
import jax.numpy as jnp
from jax import lax
from jax.experimental import pallas as pl
from jax.experimental.pallas import tpu as pltpu
from jax.sharding import PartitionSpec as P

HD = 64
MASKED = -1e30
EPSILON = 1e-05
QSCALE = 0.125
BF = jnp.bfloat16
F32 = jnp.float32
NT = (((1,), (1,)), ((), ()))
NN = (((1,), (0,)), ((), ()))
TN = (((0,), (0,)), ((), ()))
VMEM_LIMIT = 56 << 20
BOTH = ("dp", "ctx")
ANY = pl.BlockSpec(memory_space=pl.ANY)
SMEM = pl.BlockSpec(memory_space=pltpu.SMEM)
TILE = 16


def mm(a, b, dims=NN):
    return lax.dot_general(a, b, dims, preferred_element_type=F32)


def params():
    return pltpu.CompilerParams(vmem_limit_bytes=VMEM_LIMIT)


def shard_copies(refs, order_ref, cols, target, sems, base=0, turn=None, every=1, skip=0):
    copies = []
    total = target.shape[0]
    for ref in refs:
        rows = ref.shape[1]
        for n in range(ref.shape[0]):
            index = len(copies)
            row = (order_ref[index] * every + skip) * rows
            if turn is not None:
                row = lax.rem(row + turn, total)
            row = pl.multiple_of(row, TILE)
            copies.append(pltpu.make_async_copy(ref.at[n, :, cols], target.at[pl.ds(row, rows), :], sems.at[base + index]))
    return copies


def shards_of(pieces):
    return sum(piece.shape[0] for piece in pieces)


def pack_kernel(wq_ref, wk_ref, wv_ref, wo_ref, wu_ref, wd_ref, vec_ref, proj_ref, up_ref, *down):
    rows, d = wq_ref.shape
    ff = wu_ref.shape[1]
    for n, (ref, scale) in enumerate(((wq_ref, QSCALE), (wk_ref, None), (wv_ref, None))):
        for pair in range(d // 128):
            part = ref[:, pair * 128 : (pair + 1) * 128]
            part = part if scale is None else part * scale
            proj_ref[:, pair * 384 + n * 128 : pair * 384 + (n + 1) * 128] = part.astype(BF)
    proj_ref[:, 3 * d :] = vec_ref[...]
    up_ref[:, 0:d] = wo_ref[...].astype(BF)
    up_ref[:, d : d + ff] = wu_ref[...].astype(BF)
    if down:
        down[0][...] = wd_ref[...].astype(BF)
    else:
        for n in range(wd_ref.shape[0] // rows):
            up_ref[:, d + ff + n * d : d + ff + (n + 1) * d] = wd_ref[n * rows : (n + 1) * rows, :].astype(BF)


def pack(w_query, w_key, w_value, w_out, w_up, w_down, vec):
    rows, d = w_query.shape
    ff = w_up.shape[1]
    joined = rows % TILE == 0
    more = w_down.shape[0] // rows * d if joined else 0
    shapes = [(rows, 3 * d + vec.shape[1]), (rows, d + ff + more)] + ([] if joined else [w_down.shape])
    return pl.pallas_call(
        pack_kernel,
        out_shape=[jax.ShapeDtypeStruct(shape, BF) for shape in shapes],
        compiler_params=params(),
        name="pack",
    )(w_query, w_key, w_value, w_out, w_up, w_down, vec)


def place_kernel(count, first, order_ref, *refs):
    refs, (vec_ref, sems) = refs[:count], refs[count:]
    copies = shard_copies(refs, order_ref, slice(first, refs[0].shape[2]), vec_ref, sems)
    for copy in copies:
        copy.start()
    for copy in copies:
        copy.wait()


def place(pieces, order, first):
    rows = shards_of(pieces) * pieces[0].shape[1]
    return pl.pallas_call(
        functools.partial(place_kernel, len(pieces), first),
        in_specs=[SMEM] + [ANY] * len(pieces),
        out_shape=jax.ShapeDtypeStruct((rows, pieces[0].shape[2] - first), BF),
        scratch_shapes=[pltpu.SemaphoreType.DMA((shards_of(pieces),))],
        compiler_params=params(),
        name="place",
    )(order, *pieces)


def load_heads(pieces, order_ref, w_ref, sems):
    @pl.when(pl.program_id(0) == 0)
    def _():
        first = pl.multiple_of(order_ref[shards_of(pieces)], 128)
        copies = shard_copies(pieces, order_ref, pl.ds(first, w_ref.shape[1]), w_ref, sems)
        for copy in copies:
            copy.start()
        for copy in copies:
            copy.wait()


def head_parts(block):
    lane = lax.broadcasted_iota(jnp.int32, block.shape, 1)
    zero = jnp.zeros_like(block)
    return [jnp.where(lane < HD, block, zero), jnp.where(lane < HD, zero, block)]


def attend_kernel(chunk, extra, q_ref, k_ref, v_ref, sq_ref, sk_ref, *rest):
    o_ref, p_ref, l_ref, vt_ref, kn_ref = rest[extra:]
    i = pl.program_id(1)
    total = k_ref.shape[0]
    block = q_ref.shape[0]

    @pl.when(i == 0)
    def _():
        vt_ref[...] = v_ref[...].T
        keys = k_ref[...].astype(F32)
        norms = jnp.sum((keys * keys).T.reshape(2, HD, total), axis=1)
        kn_ref[...] = jnp.sqrt(jnp.max(norms, axis=1, keepdims=True))

    q = q_ref[...]
    parts = head_parts(q)
    q32 = q.astype(F32)
    qn = jnp.sqrt(jnp.sum((q32 * q32).T.reshape(2, HD, block), axis=1))
    bound = qn * kn_ref[...]
    seg_q = sq_ref[...]
    ones = jnp.ones((16, chunk), BF)

    def scores(h, lo):
        s = mm(k_ref[lo : lo + chunk, :], parts[h], NT)
        return jnp.where(sk_ref[lo : lo + chunk, :] == seg_q, s, MASKED)

    def finish(shift):
        acc = [jnp.zeros((HD + 16, block), F32)] * 2
        for lo in range(0, total, chunk):
            for h in range(2):
                p = jnp.exp(scores(h, lo) - shift[h : h + 1]).astype(BF)
                p_ref[h, lo : lo + chunk, :] = p
                left = jnp.concatenate([vt_ref[h * HD : h * HD + HD, lo : lo + chunk], ones], axis=0)
                acc[h] = acc[h] + mm(left, p)
        sums = [acc[h][HD : HD + 1] for h in range(2)]
        out = jnp.concatenate([acc[h][:HD] / sums[h] for h in range(2)], axis=0)
        o_ref[...] = out.T.astype(BF)
        sums = jnp.concatenate(sums, axis=0)
        l_ref[...] = 1.0 / sums
        return sums

    sums = finish(bound)
    good = jnp.min(sums) > 1e-20

    @pl.when(jnp.logical_not(good))
    def _():
        most = [jnp.full((1, block), MASKED, F32)] * 2
        for lo in range(0, total, chunk):
            for h in range(2):
                most[h] = jnp.maximum(most[h], jnp.max(scores(h, lo), axis=0, keepdims=True))
        finish(jnp.concatenate(most, axis=0))


def attend(qkv, seg_row, seg_col, base, pairs, held=None, waits=(), block=512, chunk=1024):
    total = qkv.shape[0]
    specs = lambda c: pl.BlockSpec((total, 128), lambda h, i: (0, 3 * (base + h) + c))
    kept = [] if held is None else [held]
    return pl.pallas_call(
        functools.partial(attend_kernel, chunk, len(waits) + len(kept)),
        grid=(pairs, total // block),
        in_specs=[
            pl.BlockSpec((block, 128), lambda h, i: (i, 3 * (base + h))),
            specs(1),
            specs(2),
            pl.BlockSpec((1, block), lambda h, i: (0, i)),
            pl.BlockSpec((total, 1), lambda h, i: (0, 0)),
        ] + [ANY] * (len(kept) + len(waits)),
        out_specs=[
            pl.BlockSpec((block, 128), lambda h, i: (i, base + h)),
            pl.BlockSpec((None, 2, total, block), lambda h, i: (h, 0, 0, i)),
            pl.BlockSpec((None, 2, block), lambda h, i: (h, 0, i)),
        ],
        out_shape=[
            jax.ShapeDtypeStruct((total, qkv.shape[1] // 3), BF),
            jax.ShapeDtypeStruct((pairs, 2, total, total), BF),
            jax.ShapeDtypeStruct((pairs, 2, total), F32),
        ],
        scratch_shapes=[pltpu.VMEM((128, total), BF), pltpu.VMEM((2, 1), F32)],
        compiler_params=params(),
        cost_estimate=pl.CostEstimate(flops=pairs * 12 * 10**9, bytes_accessed=pairs << 24, transcendentals=0),
        input_output_aliases={5: 0} if kept else {},
        name="attend",
    )(qkv, qkv, qkv, seg_row, seg_col, *kept, *waits)


def attend_back_kernel(chunk, extra, q_ref, k_ref, v_ref, o_ref, do_ref, do2_ref, p_ref, l_ref, *rest):
    out_ref, mark_ref, kt_ref, dk_acc, dv_acc = rest[extra:]
    i = pl.program_id(1)
    total = k_ref.shape[0]
    block = q_ref.shape[0]

    @pl.when(i == 0)
    def _():
        kt_ref[...] = k_ref[...].T
        dk_acc[...] = jnp.zeros_like(dk_acc)
        dv_acc[...] = jnp.zeros_like(dv_acc)

    do = jnp.where(i < pl.num_programs(1) // 2, do_ref[...], do2_ref[...])
    q_parts = head_parts(q_ref[...])
    do_parts = head_parts(do)
    product = do.astype(F32) * o_ref[...].astype(F32)
    delta = jnp.sum(product.T.reshape(2, HD, block), axis=1)
    inverse = l_ref[...]
    grad_q = [jnp.zeros((HD, block), F32)] * 2
    for lo in range(0, total, chunk):
        rows = slice(lo, lo + chunk)
        values = v_ref[rows, :]
        for h in range(2):
            p = p_ref[h, rows, :].astype(F32) * inverse[h : h + 1]
            grad_p = mm(values, do_parts[h], NT)
            grad_s = (p * (grad_p - delta[h : h + 1])).astype(BF)
            dv_acc[rows, :] += mm(p.astype(BF), do_parts[h])
            dk_acc[rows, :] += mm(grad_s, q_parts[h])
            grad_q[h] = grad_q[h] + mm(kt_ref[h * HD : h * HD + HD, rows], grad_s)
    grad_q = jnp.concatenate(grad_q, axis=0).T.astype(BF)
    out_ref[pl.ds(pl.multiple_of(i * block, block), block), 0:128] = grad_q
    add_fold(mark_ref.at[0:8, :], i == 0, grad_q.astype(F32))

    @pl.when(i == pl.num_programs(1) - 1)
    def _():
        out_ref[:, 128:256] = dk_acc[...].astype(BF)
        grad_v = dv_acc[...].astype(BF)
        out_ref[:, 256:384] = grad_v
        mark_ref[8:16, :] = fold(grad_v.astype(F32))


def attend_back(qkv, out, grad_mine, grad_mate, probs, inverse, base, held=None, waits=(), block=256, chunk=1024):
    total = qkv.shape[0]
    kept = [] if held is None else [held]
    pairs, skip = 1, base % probs.shape[0]
    last = total // block // 2 - 1
    whole = lambda c: pl.BlockSpec((total, 128), lambda h, i: (0, 3 * (base + h) + c))
    rows = pl.BlockSpec((block, 128), lambda h, i: (i, base + h))
    return pl.pallas_call(
        functools.partial(attend_back_kernel, chunk, len(waits) + len(kept)),
        grid=(pairs, total // block),
        in_specs=[
            pl.BlockSpec((block, 128), lambda h, i: (i, 3 * (base + h))),
            whole(1),
            whole(2),
            rows,
            pl.BlockSpec((block, 128), lambda h, i: (jnp.minimum(i, last), base + h)),
            pl.BlockSpec((block, 128), lambda h, i: (jnp.maximum(i - last - 1, 0), base + h)),
            pl.BlockSpec((None, 2, total, block), lambda h, i: (skip + h, 0, 0, i)),
            pl.BlockSpec((None, 2, block), lambda h, i: (skip + h, 0, i)),
        ] + [ANY] * (len(kept) + len(waits)),
        out_specs=[pl.BlockSpec((total, 384), lambda h, i: (0, base + h)), pl.BlockSpec((16, 128), lambda h, i: (0, 0))],
        out_shape=[jax.ShapeDtypeStruct(qkv.shape, BF), jax.ShapeDtypeStruct((16, 128), F32)],
        scratch_shapes=[
            pltpu.VMEM((128, total), BF),
            pltpu.VMEM((total, 128), F32),
            pltpu.VMEM((total, 128), F32),
        ],
        compiler_params=params(),
        cost_estimate=pl.CostEstimate(flops=10**8, bytes_accessed=1 << 16, transcendentals=0),
        input_output_aliases={8: 0} if kept else {},
        name="attend_back",
    )(qkv, qkv, qkv, out, grad_mine, grad_mate, probs, inverse, *kept, *waits)


def gelu_parts(u):
    phi = 0.5 + 0.5 * lax.erf(u * 0.7071067811865476)
    return u * phi, phi + u * (jnp.exp(u * u * -0.5) * 0.3989422804014327)


def mean(value):
    return jnp.mean(value, axis=-1, keepdims=True)


def normed(hidden):
    centred = hidden - mean(hidden)
    inverse = lax.rsqrt(mean(centred * centred) + EPSILON)
    return centred * inverse, inverse


def norm_back(grad_in, scaled, inverse, gain):
    grad_scaled = grad_in * gain
    return inverse * (grad_scaled - mean(grad_scaled) - scaled * mean(grad_scaled * scaled))


def fold(value):
    return jnp.sum(value.reshape(value.shape[0] // 8, 8, value.shape[1]), axis=0)


def add_fold(ref, first, value):
    part = fold(value)

    @pl.when(first)
    def _():
        ref[...] = part

    @pl.when(jnp.logical_not(first))
    def _():
        ref[...] += part


def token_rows(x, span, block, at=lambda i: i):
    return pl.BlockSpec((block // span, span, x.shape[2]), lambda i: (at(i), 0, 0))


def qkv_kernel(order_ref, xm_ref, xt_ref, b_ref, *refs):
    pieces, (out_ref, w_ref, sems) = refs[:-3], refs[-3:]
    load_heads(pieces, order_ref, w_ref, sems)
    i = pl.program_id(0)
    x = jnp.where(i < pl.num_programs(0) // 2, xm_ref[...], xt_ref[...])
    out_ref[...] = (mm(x.reshape(out_ref.shape[0], -1), w_ref[...]) + b_ref[...]).astype(BF)


def project(x_mine, x_mate, span, pieces, order, bias, block=256):
    steps = x_mine.shape[0] * span // block
    width = bias.shape[1]
    return pl.pallas_call(
        qkv_kernel,
        grid=(2 * steps,),
        in_specs=[
            SMEM,
            token_rows(x_mine, span, block, lambda i: jnp.minimum(i, steps - 1)),
            token_rows(x_mate, span, block, lambda i: jnp.maximum(i - steps, 0)),
            pl.BlockSpec((1, width), lambda i: (0, 0)),
        ]
        + [ANY] * len(pieces),
        out_specs=pl.BlockSpec((block, width), lambda i: (i, 0)),
        out_shape=jax.ShapeDtypeStruct((2 * steps * block, width), BF),
        scratch_shapes=[pltpu.VMEM((x_mine.shape[2], width), BF), pltpu.SemaphoreType.DMA((shards_of(pieces),))],
        compiler_params=params(),
        cost_estimate=pl.CostEstimate(flops=7 * 10**9, bytes_accessed=14 << 20, transcendentals=0),
        name="project",
    )(order, x_mine, x_mate, bias, *pieces)


def mid_up_kernel(step, count, mates, order_ref, x_ref, om_ref, vec_ref, bu_ref, *refs):
    mate_refs, refs = refs[:mates], refs[mates:]
    pieces, (xh_ref, r_ref, xb_ref, g_ref, gp_ref, wo_ref, wu_ref, sems) = refs[:count], refs[count:]
    first = pl.program_id(0) == 0
    d, ff = wu_ref.shape
    shards = shards_of(pieces)

    def out_copies():
        return shard_copies(pieces, order_ref, slice(0, d), wo_ref, sems, 0, order_ref[shards])

    def up_copies():
        return shard_copies(pieces, order_ref, slice(d, d + ff), wu_ref, sems, shards)

    @pl.when(first)
    def _():
        for copy in out_copies() + up_copies():
            copy.start()
        for copy in out_copies():
            copy.wait()

    half = om_ref.shape[1]
    mixed = mm(om_ref[...], wo_ref[0:half, :])
    for ref in mate_refs:
        mixed = mixed + mm(ref[...], wo_ref[half : half + ref.shape[1], :])
        half += ref.shape[1]
    hidden = x_ref[...].reshape(mixed.shape).astype(F32) + mixed + vec_ref[0:1, :]
    scaled, inverse = normed(hidden)
    xh_ref[...] = scaled
    r_ref[...] = inverse
    xb = (scaled * vec_ref[1:2, :] + vec_ref[2:3, :]).astype(BF)
    xb_ref[...] = xb

    @pl.when(first)
    def _():
        for copy in up_copies():
            copy.wait()

    for lo in range(0, ff, step):
        cols = slice(lo, lo + step)
        g, gp = gelu_parts(mm(xb, wu_ref[:, cols]) + bu_ref[:, cols])
        g_ref[:, cols] = g.astype(BF)
        gp_ref[:, cols] = gp.astype(BF)


def mid_up(x, span, attn, o_mate, pieces, order, vecs, b_up, block=256, step=512):
    rows, d = x.shape[0] * span, x.shape[2]
    ff = b_up.shape[1]
    row = lambda n: pl.BlockSpec((block, n), lambda i: (i, 0))
    full = lambda a: pl.BlockSpec(a.shape, lambda i: (0, 0), pipeline_mode=pl.Buffered(1))
    return pl.pallas_call(
        functools.partial(mid_up_kernel, step, len(pieces), len(o_mate)),
        grid=(rows // block,),
        in_specs=[SMEM, token_rows(x, span, block), row(d // 2), full(vecs), full(b_up)]
        + [row(a.shape[1]) for a in o_mate]
        + [ANY] * len(pieces),
        out_specs=[row(d), row(1), row(d), row(ff), row(ff)],
        out_shape=[
            jax.ShapeDtypeStruct((rows, d), F32),
            jax.ShapeDtypeStruct((rows, 1), F32),
            jax.ShapeDtypeStruct((rows, d), BF),
            jax.ShapeDtypeStruct((rows, ff), BF),
            jax.ShapeDtypeStruct((rows, ff), BF),
        ],
        scratch_shapes=[
            pltpu.VMEM((d, d), BF),
            pltpu.VMEM((d, ff), BF),
            pltpu.SemaphoreType.DMA((2 * shards_of(pieces),)),
        ],
        compiler_params=params(),
        cost_estimate=pl.CostEstimate(flops=20 * 10**9, bytes_accessed=36 << 20, transcendentals=0),
        name="mid_up",
    )(order, x, attn, vecs, b_up, *o_mate, *pieces)


def mid_down_kernel(step, count, blocks, order_ref, g_ref, gp_ref, xh_ref, dy_ref, vec_ref, *refs):
    pieces, (out_ref, dh_ref, dm_ref, du_ref, s_ref, su_ref, wd_ref, sems) = refs[:count], refs[count:]
    first = pl.program_id(0) == 0
    d = wd_ref.shape[1]

    @pl.when(first)
    def _():
        copies = []
        for n in range(blocks[1]):
            cols = slice(blocks[0] + n * d, blocks[0] + (n + 1) * d)
            copies += shard_copies(pieces, order_ref, cols, wd_ref, sems, len(copies), None, blocks[1], n)
        for copy in copies:
            copy.start()
        for copy in copies:
            copy.wait()

    x1 = xh_ref[...] * vec_ref[1:2, :] + vec_ref[2:3, :]
    hidden = x1 + mm(g_ref[...], wd_ref[...]) + vec_ref[3:4, :]
    scaled, inverse = normed(hidden)
    gain = vec_ref[4:5, :]
    out_ref[...] = (scaled * gain + vec_ref[5:6, :]).astype(BF)
    dy = dy_ref[...].astype(F32)
    dh = norm_back(dy, scaled, inverse, gain)
    dm = dh.astype(BF)
    dh_ref[...] = dh
    dm_ref[...] = dm
    add_fold(s_ref.at[0:8, :], first, dy * scaled)
    add_fold(s_ref.at[8:16, :], first, dy)
    add_fold(s_ref.at[16:24, :], first, dm.astype(F32))
    for lo in range(0, wd_ref.shape[0], step):
        cols = slice(lo, lo + step)
        du = (mm(dm, wd_ref[cols, :], NT) * gp_ref[:, cols].astype(F32)).astype(BF)
        du_ref[:, cols] = du
        add_fold(su_ref.at[:, cols], first, du.astype(F32))


def mid_down(g, gp, xh, dy, pieces, order, blocks, vecs, block=256, step=2048):
    rows, d = xh.shape
    ff = g.shape[1]
    row = lambda n: pl.BlockSpec((block, n), lambda i: (i, 0))
    full = lambda a: pl.BlockSpec(a.shape, lambda i: (0, 0), pipeline_mode=pl.Buffered(1))
    keep = lambda r, n: pl.BlockSpec((r, n), lambda i: (0, 0))
    return pl.pallas_call(
        functools.partial(mid_down_kernel, step, len(pieces), blocks),
        grid=(rows // block,),
        in_specs=[SMEM, row(ff), row(ff), row(d), row(d), full(vecs)] + [ANY] * len(pieces),
        out_specs=[row(d), row(d), row(d), row(ff), keep(24, d), keep(8, ff)],
        out_shape=[
            jax.ShapeDtypeStruct((rows, d), BF),
            jax.ShapeDtypeStruct((rows, d), F32),
            jax.ShapeDtypeStruct((rows, d), BF),
            jax.ShapeDtypeStruct((rows, ff), BF),
            jax.ShapeDtypeStruct((24, d), F32),
            jax.ShapeDtypeStruct((8, ff), F32),
        ],
        scratch_shapes=[pltpu.VMEM((ff, d), BF), pltpu.SemaphoreType.DMA((shards_of(pieces) * blocks[1],))],
        compiler_params=params(),
        cost_estimate=pl.CostEstimate(flops=25 * 10**9, bytes_accessed=44 << 20, transcendentals=0),
        name="mid_down",
    )(order, g, gp, xh, dy, vecs, *pieces)


def mid_back_kernel(count, order_ref, dh_ref, du_ref, xh_ref, r_ref, vec_ref, *refs):
    pieces, (dh1_ref, da_ref, dom_ref, dot_ref, s_ref, wu_ref, wo_ref, sems) = refs[:count], refs[count:]
    first = pl.program_id(0) == 0
    d, ff = wu_ref.shape
    half = dom_ref.shape[1]
    shards = shards_of(pieces)

    @pl.when(first)
    def _():
        copies = shard_copies(pieces, order_ref, slice(d, d + ff), wu_ref, sems, shards)
        copies += shard_copies(pieces, order_ref, slice(0, d), wo_ref, sems, 0, order_ref[shards])
        for copy in copies:
            copy.start()
        for copy in copies:
            copy.wait()

    dx = dh_ref[...] + mm(du_ref[...], wu_ref[...], NT)
    scaled = xh_ref[...]
    dh1 = norm_back(dx, scaled, r_ref[...], vec_ref[1:2, :])
    dh1_ref[...] = dh1
    da = dh1.astype(BF)
    da_ref[...] = da
    dom_ref[...] = mm(da, wo_ref[0:half, :], NT).astype(BF)
    dot_ref[...] = mm(da, wo_ref[half:, :], NT).astype(BF)
    add_fold(s_ref.at[0:8, :], first, dx * scaled)
    add_fold(s_ref.at[8:16, :], first, dx)
    add_fold(s_ref.at[16:24, :], first, da.astype(F32))


def mid_back(dh, du, xh, r, pieces, order, vecs, block=256):
    rows, d = dh.shape
    ff = du.shape[1]
    row = lambda n: pl.BlockSpec((block, n), lambda i: (i, 0))
    full = lambda a: pl.BlockSpec(a.shape, lambda i: (0, 0), pipeline_mode=pl.Buffered(1))
    return pl.pallas_call(
        functools.partial(mid_back_kernel, len(pieces)),
        grid=(rows // block,),
        in_specs=[SMEM, row(d), row(ff), row(d), row(1), full(vecs)] + [ANY] * len(pieces),
        out_specs=[row(d), row(d), row(d // 2), row(d // 2), pl.BlockSpec((24, d), lambda i: (0, 0))],
        out_shape=[
            jax.ShapeDtypeStruct((rows, d), F32),
            jax.ShapeDtypeStruct((rows, d), BF),
            jax.ShapeDtypeStruct((rows, d // 2), BF),
            jax.ShapeDtypeStruct((rows, d // 2), BF),
            jax.ShapeDtypeStruct((24, d), F32),
        ],
        scratch_shapes=[
            pltpu.VMEM((d, ff), BF),
            pltpu.VMEM((d, d), BF),
            pltpu.SemaphoreType.DMA((2 * shards_of(pieces),)),
        ],
        compiler_params=params(),
        cost_estimate=pl.CostEstimate(flops=15 * 10**9, bytes_accessed=36 << 20, transcendentals=0),
        name="mid_back",
    )(order, dh, du, xh, r, vecs, *pieces)


def token_kernel(adds, count, order_ref, grad_ref, *refs):
    add_refs, pieces, (out_ref, w_ref, sems) = refs[:adds], refs[adds : adds + count], refs[-3:]
    load_heads(pieces, order_ref, w_ref, sems)
    total = mm(grad_ref[...], w_ref[...], NT)
    for ref in add_refs:
        total = total + ref[...].astype(F32)
    out_ref[...] = total.astype(BF)


def token_grad(grads, pieces, order, d, shift, adds, waits=(), block=512):
    rows, width = grads.shape[0] // 2, grads.shape[1]
    base = shift * (rows // block)
    row = pl.BlockSpec((block, d), lambda i: (i, 0))
    return pl.pallas_call(
        functools.partial(token_kernel, len(adds), len(pieces)),
        grid=(rows // block,),
        in_specs=[SMEM, pl.BlockSpec((block, width), lambda i: (base + i, 0))]
        + [row] * len(adds)
        + [ANY] * (len(pieces) + len(waits)),
        out_specs=row,
        out_shape=jax.ShapeDtypeStruct((rows, d), BF),
        scratch_shapes=[pltpu.VMEM((d, width), BF), pltpu.SemaphoreType.DMA((shards_of(pieces),))],
        compiler_params=params(),
        cost_estimate=pl.CostEstimate(flops=10**8, bytes_accessed=1 << 16, transcendentals=0),
        name="token_grad",
    )(order, grads, *adds, *pieces, *waits)


def finish_kernel(core_ref, up_ref, up_mate_ref, last_ref, last_mate_ref, *outs):
    gu_ref, go_ref, gq_ref, gk_ref, gv_ref, small_ref = outs
    core = core_ref[0]
    first = core == 0
    ff, half = gu_ref.shape[1], go_ref.shape[1] // 2

    def halves(ref, mate_ref, lo, width):
        mine, mate = ref[core, :, lo : lo + width].astype(F32), mate_ref[:, lo : lo + width].astype(F32)
        return jnp.where(first, mine, mate), jnp.where(first, mate, mine), mine + mate

    left, right, _ = halves(up_ref, up_mate_ref, 0, ff // 2)
    gu_ref[:, : ff // 2], gu_ref[:, ff // 2 :] = left, right
    left, right, _ = halves(up_ref, up_mate_ref, ff // 2, half)
    go_ref[:, :half], go_ref[:, half:] = left, right
    small_ref[0] = halves(up_ref, up_mate_ref, ff // 2 + half, 128)[2]
    for pair in range(half // 128):
        at = pair * 128
        for n, out in enumerate((gq_ref, gk_ref, gv_ref)):
            left, right, _ = halves(last_ref, last_mate_ref, 3 * at + n * 128, 128)
            scale = QSCALE if n == 0 else 1.0
            out[:, at : at + 128], out[:, half + at : half + at + 128] = left * scale, right * scale
    small_ref[1] = halves(last_ref, last_mate_ref, 3 * half, 128)[2]


def finish(core, rows, ff, d, *arrays):
    shapes = [(rows, ff)] + [(rows, d)] * 4 + [(2, rows, 128)]
    return pl.pallas_call(
        finish_kernel,
        in_specs=[SMEM] + [pl.BlockSpec(memory_space=pltpu.VMEM)] * 4,
        out_shape=[jax.ShapeDtypeStruct(shape, F32) for shape in shapes],
        compiler_params=params(),
        name="finish",
    )(jnp.reshape(core, (1,)).astype(jnp.int32), *arrays)


def by_chip(value, out_ref, lo):
    chips, dps, rows, _ = out_ref.shape
    value = value.reshape(dps, chips, rows, value.shape[1])
    for n in range(dps):
        out_ref[:, n, :, lo : lo + value.shape[3]] = value[n].astype(BF)


def proj_kernel(xm_ref, xt_ref, grad_ref, *refs):
    out_ref = refs[-1]
    own = grad_ref.shape[0] // 2
    xm = xm_ref[...].reshape(own, -1)
    xt = xt_ref[...].reshape(own, -1)
    by_chip(mm(xm, grad_ref[0:own, :], TN) + mm(xt, grad_ref[own:, :], TN), out_ref, 0)
    if grad_ref.shape[1] < out_ref.shape[3]:
        out_ref[:, :, :, grad_ref.shape[1] :] = refs[0][...]


def dp_steps(groups, least):
    return max(1, min(groups, least // 128))


def shard_specs(steps, groups, chips, rows, cols):
    spec = pl.BlockSpec((chips, groups // steps, rows, cols), lambda i, *_: (0, i, 0, 0))
    return spec, jax.ShapeDtypeStruct((chips, groups, rows, cols), BF)


def proj_grad(x_mine, x_mate, span, grads, first, pairs, groups, chips, waits=(), extra=None):
    own, d = x_mine.shape[0] * span, x_mine.shape[2]
    width = 384 * pairs
    more = [] if extra is None else [extra]
    steps = dp_steps(groups, d)
    col = pl.BlockSpec((x_mine.shape[0], span, d // steps), lambda i: (0, 0, i))
    rows = d // groups // chips
    spec, shape = shard_specs(steps, groups, chips, rows, width + sum(a.shape[3] for a in more))
    return pl.pallas_call(
        proj_kernel,
        grid=(steps,),
        in_specs=[col, col]
        + [pl.BlockSpec((2 * own, width), lambda i: (0, first // pairs), pipeline_mode=pl.Buffered(1))]
        + [shard_specs(steps, groups, chips, rows, a.shape[3])[0] for a in more]
        + [ANY] * len(waits),
        out_specs=spec,
        out_shape=shape,
        compiler_params=params(),
        cost_estimate=pl.CostEstimate(flops=10**8, bytes_accessed=1 << 16, transcendentals=0),
        name="proj_grad",
    )(x_mine, x_mate, grads, *more, *waits)


def weight_kernel(adds, waits, turn_ref, *refs):
    out_ref, refs = refs[-1], refs[: len(refs) - 1 - waits]
    count = (len(refs) - adds) // 2
    more = refs[2 * count :]
    lo = 0
    for n in range(count):
        value = mm(refs[2 * n][...], refs[2 * n + 1][...], TN)
        width = value.shape[1]
        chips, dps, rows, _ = out_ref.shape
        value = value.reshape(dps, chips, rows, width)
        for k in range(dps):
            part = value[k]
            if more:
                part = part + more[0][:, k, :, lo : lo + width].astype(F32)
            out_ref[:, k, :, lo : lo + width] = part.astype(BF)
        lo += width
    if lo < out_ref.shape[3]:
        out_ref[:, :, :, lo:] = more[-1][...]


def weight_grad(sides, turns, groups, chips, adds=(), waits=()):
    in_specs, args = [], []
    steps = dp_steps(groups, min(left.shape[1] for left, _ in sides))
    rows_of = lambda a: a.shape[1] // steps
    for n, (left, right) in enumerate(sides):
        tokens = left.shape[0]
        in_specs.append(
            pl.BlockSpec((tokens, rows_of(left)), lambda i, t, n=n: (0, lax.rem(i + t[1 + n] * (steps // 2), steps)))
        )
        in_specs.append(
            pl.BlockSpec((tokens, right.shape[1] // 2), lambda i, t: (0, t[0]), pipeline_mode=pl.Buffered(1))
        )
        args += [left, right]
    rows = sides[0][0].shape[1] // groups // chips
    cols = sum(right.shape[1] // 2 for _, right in sides)
    if len(adds) > 1:
        cols += adds[1].shape[3]
    in_specs += [shard_specs(steps, groups, chips, rows, a.shape[3])[0] for a in adds] + [ANY] * len(waits)
    spec, shape = shard_specs(steps, groups, chips, rows, cols)
    flops = sum(a.shape[0] * a.shape[1] * b.shape[1] for a, b in sides)
    return pl.pallas_call(
        functools.partial(weight_kernel, len(adds), len(waits)),
        grid_spec=pltpu.PrefetchScalarGridSpec(
            num_scalar_prefetch=1, grid=(steps,), in_specs=in_specs, out_specs=spec
        ),
        out_shape=shape,
        compiler_params=params(),
        cost_estimate=pl.CostEstimate(flops=10**8, bytes_accessed=1 << 16, transcendentals=0),
        name="weight_grad",
    )(turns, *args, *adds, *waits)


def swap(value, mask):
    count = lax.axis_size("ctx")
    return lax.ppermute(value, "ctx", [(d, d ^ mask) for d in range(count)])


def along(value, step):
    count = lax.axis_size("dp")
    return lax.ppermute(value, "dp", [(s, (s + step) % count) for s in range(count)])


def pick(value, index, axis=0):
    return lax.dynamic_index_in_dim(value, index, axis, keepdims=False)


def over_chips(value):
    count = lax.axis_size("ctx")
    groups = [list(range(core, count, 2)) for core in range(2)]
    return lax.all_to_all(value, "ctx", 0, 0, axis_index_groups=groups)


def tick(value):
    return (value[(0,) * value.ndim].astype(F32) > 1e30).astype(jnp.int32)


def tie_kernel(*refs):
    pass


def tie(value, *waits):
    return pl.pallas_call(
        tie_kernel,
        in_specs=[ANY] * (1 + len(waits)),
        out_specs=ANY,
        out_shape=jax.ShapeDtypeStruct(value.shape, value.dtype),
        input_output_aliases={0: 0},
        name="tie",
    )(value, *waits)


class Gather:
    def __init__(self, own, place):
        self.place = place
        self.groups = lax.axis_size("dp")
        self.chips = lax.axis_size("ctx") // 2
        self.own = own
        self.whole = own.shape[0] % TILE != 0

    def along_dp(self, value):
        if self.whole:
            return []
        self.turns = [value] + [along(value, s) for s in range(1, self.groups)]
        return self.turns[1:]

    def over_chips(self, later):
        if self.whole:
            return
        half = self.groups // 2
        bits = list(range(self.chips.bit_length() - 1))
        stacked = jnp.stack(self.turns) + later.astype(BF)
        self.held = []
        for first, order in ((0, bits), (half, bits[::-1])):
            value = stacked[first : first + half]
            labels = [(first + n, 0) for n in range(half)]
            for n, bit in enumerate(order):
                other = swap(value, 2 << bit)
                more = [(t, r ^ (1 << bit)) for t, r in labels]
                if n + 1 < len(order):
                    value, labels = jnp.concatenate([value, other]), labels + more
                else:
                    self.held += [(value, labels), (other, more)]

    def between_cores(self):
        me, chip, core = self.place
        if self.whole:
            return [lax.all_gather(self.own, BOTH, axis=0, tiled=True)[None]], jnp.zeros((1,), jnp.int32)
        pieces, order = [], []
        for value, labels in self.held:
            pieces += [value, swap(value, 1)]
            for mate in (core, 1 - core):
                order += [(me - t) % self.groups * 2 * self.chips + 2 * (chip ^ r) + mate for t, r in labels]
        return pieces, jnp.stack(order).astype(jnp.int32)


class Reduce:
    def __init__(self, grad, place, direct=False):
        self.place = place
        self.groups = grad.shape[1]
        if direct:
            chip = place[1]
            sent = [pick(grad, chip ^ r) for r in range(1, grad.shape[0])]
            self.got = [pick(grad, chip)] + [swap(v, 2 * (r + 1)) for r, v in enumerate(sent)]
        else:
            self.got = over_chips(grad)

    def chip_sum(self, *waits):
        if isinstance(self.got, list):
            last = tie(self.got[-1], *self.got[1:-1], *waits)
            self.part = sum(v.astype(F32) for v in self.got[:-1] + [last]).astype(BF)
        else:
            self.part = jnp.sum(tie(self.got, *waits).astype(F32), axis=0).astype(BF)
        return [self.part]

    def along_dp(self):
        me = self.place[0]
        sent = [pick(self.part, (me + step) % self.groups) for step in range(1, self.groups)]
        self.turns = [pick(self.part, me)] + [along(v, n + 1) for n, v in enumerate(sent)]

    def dp_sum(self, *waits):
        last = tie(self.turns[-1], *self.turns[1:-1], *waits)
        total = sum(v.astype(F32) for v in self.turns[:-1] + [last]).astype(BF)
        self.total = total.reshape(2, -1, total.shape[1])
        return [self.total]

    def both(self):
        return self.total, swap(pick(self.total, 1 - self.place[2]), 1)


def half_cols(value, which):
    width = value.shape[-1] // 2
    return lax.dynamic_slice_in_dim(value, which * width, width, value.ndim - 1)


def spread(vectors, shards, rows):
    flat = jnp.concatenate([v.reshape(shards, -1) for v in vectors], axis=1)
    return jnp.pad(flat, ((0, 0), (0, rows * 128 - flat.shape[1]))).reshape(shards, rows, 128)


def fold_rows(sums):
    return jnp.sum(sums.reshape(-1, 8, sums.shape[1]), axis=1)


def local(
    tokens, segments, cotangent, w_query, w_key, w_value, w_out, w_up, w_down,
    b_query, b_value, b_out, b_up, b_down, gain_attn, shift_attn, gain_mlp, shift_mlp,
):
    seqs, span, d = tokens.shape
    count = lax.axis_size("ctx")
    groups = lax.axis_size("dp")
    chips = count // 2
    ctx = lax.axis_index("ctx")
    chip, core = ctx // 2, ctx % 2
    place_of = (lax.axis_index("dp"), chip, core)
    ff = w_up.shape[1]
    half = d // 2
    shards = groups * count
    rows = d // shards
    width = d // shards
    pairs = half // 128
    bf = lambda v: v.astype(BF)

    vec_names = (b_query, b_value, b_out, gain_attn, shift_attn, b_down, gain_mlp, shift_mlp)
    vec_size = 8 * width + ff // shards
    extra = -(-(vec_size + seqs * span) // (rows * 128)) * 128
    vec_pack = jnp.concatenate([bf(v) for v in vec_names] + [bf(b_up), bf(segments.reshape(-1))])
    vec_pack = jnp.pad(vec_pack, (0, rows * extra - vec_pack.shape[0])).reshape(rows, extra)
    packed = pack(w_query, w_key, w_value, w_out, w_up, w_down, vec_pack)

    got = over_chips(tokens)
    own = chips * span
    proj = Gather(packed[0], place_of)
    turns_of = proj.along_dp(proj.own)
    got = tie(got, *turns_of)
    mate = swap(got, 1)
    later = tick(got)
    proj.over_chips(later)
    pieces, order = proj.between_cores()
    def everywhere(value):
        return lax.all_gather(tie(value, got), BOTH, axis=0, tiled=True).reshape(2, -1, value.shape[1])

    up_pieces = [everywhere(packed[1])]
    if rows % TILE == 0:
        down_pieces, blocks = [up_pieces[0].reshape(shards, rows, -1)], (d + ff, w_down.shape[0] // rows)
    else:
        down_pieces, blocks = [everywhere(packed[2])], (0, 1)
    down_order = jnp.arange(down_pieces[0].shape[0], dtype=jnp.int32)
    vec_block = pieces[0][0, :, 3 * d :] if proj.whole else place(pieces, order, 3 * d)
    order = jnp.append(order, core * 3 * half).astype(jnp.int32)
    by_row = vec_block.reshape(shards, rows, extra)
    vec_all = by_row[:, : -(-vec_size // extra)].reshape(shards, -1)[:, :vec_size].astype(F32)
    if vec_size % extra == 0 and span % extra == 0:
        seg_all = by_row[:, vec_size // extra : (vec_size + seqs * span) // extra]
    else:
        seg_all = vec_block.reshape(shards, rows * extra)[:, vec_size : vec_size + seqs * span]
    seg_all = seg_all.reshape(groups, chips, 2, seqs, -1, min(span, extra))
    seg_own = pick(pick(seg_all, place_of[0]), chip, 2)
    seg = jnp.concatenate([pick(seg_own, core, 1), pick(seg_own, 1 - core, 1)]).reshape(-1).astype(jnp.int32)
    vec = [vec_all[:, n * width : (n + 1) * width].reshape(1, d) for n in range(8)]
    bias_up = vec_all[:, 8 * width : 8 * width + ff // shards].reshape(1, ff)
    vecs = jnp.concatenate(vec[2:] + [jnp.zeros((2, d), F32)], axis=0)
    bias_by_pair = [v.reshape(1, 2 * pairs, 1, 128) for v in (vec[0] * QSCALE, jnp.zeros((1, d), F32), vec[1])]
    bias_cat = half_cols(jnp.concatenate(bias_by_pair, axis=2).reshape(1, 3 * d), core)

    qkv = project(got, mate, span, pieces, order, bias_cat)
    seg_row, seg_col = seg.reshape(1, -1), seg.reshape(-1, 1)

    attn, probs, inverse, o_mate = None, [], [], []
    for n in range(0, pairs, 2):
        attn, p, l = attend(qkv, seg_row, seg_col, n, 2, attn)
        probs.append(p)
        inverse.append(l)
        o_mate.append(swap(attn[own:, n * 128 : (n + 2) * 128], 1))
    dy = over_chips(cotangent + tick(inverse[0]).astype(BF)).reshape(own, d)
    up_order = jnp.stack([jnp.zeros((), jnp.int32), jnp.ones((), jnp.int32), d - core * half]).astype(jnp.int32)
    xh, r, xb, g, gp = mid_up(got, span, attn, o_mate, up_pieces, up_order, vecs, bias_up)
    out, dh2, dm, du, sums_two, sums_up = mid_down(g, gp, xh, dy, down_pieces, down_order, blocks, vecs)
    result_out = over_chips(out.reshape(chips, span, d))

    zero = jnp.zeros((), jnp.int32)
    turns_sent = jnp.stack([1 - core, zero, core]).astype(jnp.int32)
    turns_kept = jnp.stack([core, zero, core]).astype(jnp.int32)
    got_down = swap(weight_grad([(g, dm)], turns_sent, groups, chips), 1)
    dh1, da, do_mine, do_send, sums_one = mid_back(dh2, du, xh, r, up_pieces, up_order, vecs)
    do_mate = swap(do_send, 1)
    kept_down = weight_grad([(g, dm)], turns_kept, groups, chips, [got_down], [result_out])
    sum_down = Reduce(kept_down, place_of)

    o_both = jnp.concatenate([attn[:own]] + o_mate, axis=1)
    sides = [(xb, du), (o_both, da)]
    got_up = swap(weight_grad(sides, turns_sent, groups, chips, (), [kept_down]), 1)
    two, one = fold_rows(sums_two), fold_rows(sums_one)
    per_shard = lambda v: jnp.moveaxis(bf(v).reshape(groups, chips, -1, 128), 1, 0)
    vec_grads = per_shard(spread([one[2], one[0], one[1], two[2], two[0], two[1], fold_rows(sums_up)], shards, rows))

    grads, waits, marks = None, [], []
    for n in range(pairs):
        grads, mark = attend_back(qkv, attn, do_mine, do_mate, probs[n // 2], inverse[n // 2], n, grads, waits)
        waits = []
        marks.append(mark)
        if n == 0:
            got_up = tie(got_up, mark)
            kept_up = weight_grad(sides, turns_kept, groups, chips, [got_up, vec_grads])
            waits = sum_down.chip_sum(mark, kept_up)
            sum_down.along_dp()
            sum_up = Reduce(kept_up, place_of)
        elif n == 1:
            waits = sum_down.dp_sum(mark)
        elif n == 2:
            first = proj_grad(got, mate, span, grads, 0, 3, groups, chips)
            waits = sum_up.chip_sum(mark, first)
            sum_up.along_dp()
            sum_first = Reduce(tie(first, sum_up.part), place_of)
    bias_sums = jnp.stack([fold_rows(v) for v in marks])
    blank = jnp.zeros((half,), F32)

    def whole_vector(c):
        part = bias_sums[:, c].reshape(-1)
        return jnp.where(core == 0, jnp.concatenate([part, blank]), jnp.concatenate([blank, part]))

    bias_grads = per_shard(spread([whole_vector(0), whole_vector(1)], shards, rows))
    token_send = token_grad(grads, pieces, order, d, 1, (), [sum_first.got] + sum_up.turns[1:])
    token_got = swap(token_send, 1)
    last = proj_grad(got, mate, span, grads, 3, 1, groups, chips, [token_send], bias_grads)
    sum_last = Reduce(last, place_of, True)
    grad_mine = token_grad(grads, pieces, order, d, 0, (dh1, token_got), [last])
    arrived = sum_last.got[1:]
    grad_mine = tie(grad_mine, *arrived)
    sum_last.chip_sum()
    sum_first.chip_sum(*arrived)
    sum_up.dp_sum(*arrived)
    arrived_tokens = over_chips(grad_mine.reshape(chips, span, d))
    grad_tokens = arrived_tokens + tick(arrived_tokens).astype(BF)
    sum_last.part = jnp.concatenate([sum_first.part, sum_last.part], axis=2)
    sum_last.along_dp()
    sum_last.dp_sum(arrived_tokens)

    mine, other = sum_down.both()
    mine = pick(mine, core)
    order_of = jnp.where(core == 0, jnp.stack([mine, other]), jnp.stack([other, mine]))
    grad_down = jnp.concatenate([order_of[0], order_of[1]], axis=1).astype(F32)
    grad_up, grad_out, grad_query, grad_key, grad_value, small = finish(
        core, rows, ff, d, *sum_up.both(), *sum_last.both()
    )
    sums = small[0].reshape(-1)
    g_bo, g_ga, g_sa, g_bd, g_gm, g_sm = [sums[n * width : (n + 1) * width] for n in range(6)]
    g_bu = sums[6 * width : 6 * width + ff // shards]
    sums = small[1].reshape(-1)
    g_bq, g_bv = sums[:width] * QSCALE, sums[width : 2 * width]
    return (
        result_out, grad_tokens, grad_query, grad_key, grad_value, grad_out, grad_up, grad_down,
        g_bq, g_bv, g_bo, g_bu, g_bd, g_ga, g_sa, g_gm, g_sm,
    )


def solution(mesh):
    act, flat, mat, vec = P("dp", "ctx", None), P("dp", "ctx"), P(BOTH, None), P(BOTH)
    return jax.shard_map(
        local,
        mesh=mesh,
        in_specs=(act, flat, act) + (mat,) * 6 + (vec,) * 9,
        out_specs=(act, act) + (mat,) * 6 + (vec,) * 9,
        check_vma=False,
    )
```
